32 devices in a mesh: leaf: 8 (over z, y), draw: 4 (over x, core).
Axes of the slice: x: 2, y: 2, z: 4, core: 2. Of those that a mesh axis runs over, the one named last changes fastest.
Arguments:
- noise_draws: bfloat16 [3, 16, 256, 2048], P(None, 'leaf', None, 'draw'), may hold values from -6 to 6
- inverse_diagonal: bfloat16 [3, 16, 256, 256], P(None, 'leaf', 'draw'), as said below
- coupling_blocks: bfloat16 [2, 16, 8, 256, 256], P(None, 'leaf', 'draw'), may hold values from -0.09375 to 0.09375
- ancestor_pick: int32 [2, 8, 8], replicated, may hold values from 0 to 1
- coupling_lists: int32 [2, 16, 8], P(None, 'leaf'), may hold values from 0 to 15, as said below
- live_counts: int32 [2, 16], P(None, 'leaf'), may hold values from 1 to 8, as said below
Outputs:
- samples: bfloat16 [3, 16, 256, 2048], P(None, 'leaf', None, 'draw')
The draws below stay inside these ranges and needn't reach their ends.
Inputs may be any that keep to these rules, and one draw needn't show every extreme that they name: `coupling_lists`: the 8 entries of one supernode are distinct. Level 1 entries are below 8, and the live entries of the 2 level-1 supernodes of one owner together name every owner. In level 2 the first 4 entries are 8 or more and the rest below 8; the first halves of one owner's level-2 supernodes together name every value from 8 to 15. `live_counts`: the level-1 counts of one owner's 2 supernodes sum to more than 8; level-2 counts are 4 or more; in each level some supernode has 8. `inverse_diagonal`: each block is lower triangular, with diagonal entries between 0.6 and 1.4.
All inputs are finite; a program needn't handle non-finite values.
Results may differ from the reference program's by a relative error of at most 0.0052.
Values may be sent and summed in bfloat16 or wider, within the bound.
No kernel may reach another device: no remote copies, remote signals or barrier semaphores. Data moves between devices by JAX's collectives and lax.ppermute only.
A program may use at most 64 MiB of HBM per device.

```python
import jax
import jax.numpy as jnp
from jax import lax

W = 256
NODES_DEV = 2
LEVELS = 3
OWNERS = 8
COUPLE = 8
NODES = 16
S = 2048


def owner_orders(seed_key, rows, owners):
    scores = jax.random.randint(seed_key, (rows, owners), 0, 1 << 20, dtype=jnp.int32)
    scores = scores * owners + lax.broadcasted_iota(jnp.int32, (rows, owners), 1)
    return jnp.argsort(scores, axis=1, stable=True).astype(jnp.int32)


def coupling_structure(base_key):
    owners = NODES // NODES_DEV
    half = COUPLE // 2
    keys = jax.random.split(jax.random.fold_in(base_key, 4099), 8)
    first_order = owner_orders(keys[0], owners, owners)
    level_one = jnp.stack([first_order, first_order[:, ::-1]], axis=1).reshape(NODES, COUPLE)
    upper_order = owner_orders(keys[1], owners, owners) + owners
    lower_order = owner_orders(keys[2], owners, owners)
    node_zero = jnp.concatenate([upper_order[:, :half], lower_order[:, :half]], axis=1)
    node_one = jnp.concatenate([upper_order[:, half:], lower_order[:, half:]], axis=1)
    level_two = jnp.stack([node_zero, node_one], axis=1).reshape(NODES, COUPLE)
    lists = jnp.stack([level_one, level_two], axis=0).astype(jnp.int32)
    first_count = jax.random.randint(keys[3], (owners,), 1, COUPLE + 1, dtype=jnp.int32)
    extra = jax.random.randint(keys[4], (owners,), 0, COUPLE, dtype=jnp.int32)
    second_count = COUPLE + 1 - first_count + extra % first_count
    count_one = jnp.stack([first_count, second_count], axis=1).reshape(NODES)
    count_two = jax.random.randint(keys[5], (NODES,), half, COUPLE + 1, dtype=jnp.int32)
    positions = lax.broadcasted_iota(jnp.int32, (NODES,), 0)
    chosen_one = jax.random.randint(keys[6], (), 0, NODES, dtype=jnp.int32)
    chosen_two = jax.random.randint(keys[7], (), 0, NODES, dtype=jnp.int32)
    count_one = jnp.where(positions == chosen_one, COUPLE, count_one)
    count_two = jnp.where(positions == chosen_two, COUPLE, count_two)
    counts = jnp.stack([count_one, count_two], axis=0).astype(jnp.int32)
    return (lists, counts)


def draw_coupling_lists(key, part):
    return coupling_structure(key)[0]


def draw_live_counts(key, part):
    return coupling_structure(key)[1]


def draw_inverse_diagonal(key, part):
    key_rough, key_diag = jax.random.split(jax.random.fold_in(key, 811))
    shape = (LEVELS, NODES, W, W)
    rough = jax.random.normal(key_rough, shape, jnp.float32)
    rows = lax.broadcasted_iota(jnp.int32, (W, W), 0)
    cols = lax.broadcasted_iota(jnp.int32, (W, W), 1)
    lower = (rows > cols).astype(jnp.float32)
    unit = (rows == cols).astype(jnp.float32)
    diagonal = jax.random.uniform(key_diag, (LEVELS, NODES, 1, W), jnp.float32, 0.6, 1.4)
    return (rough * lower * (0.8 / W ** 0.5) + unit * diagonal).astype(jnp.bfloat16)


def place_ends(array, rng, smallest, top_value):
    longest = array.shape.index(max(array.shape))
    spots = []
    for shift in (0, 1):
        where = [jax.random.randint(jax.random.fold_in(rng, axis), (), 0, length) for axis, length in enumerate(array.shape)]
        where[longest] = (where[longest] + shift) % array.shape[longest]
        spots.append(tuple(where))
    return array.at[spots[0]].set(smallest).at[spots[1]].set(top_value)


def levels(key, dims, shards, smallest, top_value):
    factor_of, own = 1.0, jax.random.fold_in(key, 6)
    for axis_at, parts in shards:
        draws = jnp.exp(jax.random.uniform(jax.random.fold_in(own, axis_at), (parts,), jnp.float32, smallest / len(shards), top_value / len(shards)))
        factor_of = factor_of * jnp.repeat(draws, dims[axis_at] // parts).reshape([-1 if axis == axis_at else 1 for axis in range(len(dims))])
    return factor_of


def noise(stream_key, dims, spread, bound, cuts=(), kind=jnp.bfloat16):
    entries = jax.random.normal(stream_key, dims, jnp.float32) * spread
    if len(cuts) > 0:
        entries = levels(stream_key, dims, cuts, -0.22, 0.18) * entries
    return jnp.clip(entries, min=-bound, max=bound).astype(kind)


def setup_inputs(seed: int = 0) -> dict:
    streams_of = jax.random.split(jax.random.key(seed), 7)
    noise_draws = noise(streams_of[0], (LEVELS, NODES, W, S), 1.0, 6.0, ((1, 8), (3, 4)))
    inverse_diagonal = draw_inverse_diagonal(jax.random.fold_in(streams_of[6], 71), 0)
    coupling_blocks = noise(streams_of[2], (LEVELS - 1, NODES, COUPLE, W, W), (2 * W * COUPLE) ** -0.5, 0.09375, ((1, 8), (2, 4)))
    ancestor_pick = place_ends(jax.random.randint(streams_of[3], (LEVELS - 1, OWNERS, OWNERS), 0, NODES_DEV), jax.random.fold_in(streams_of[3], 1), 0, NODES_DEV - 1).astype(jnp.int32)
    coupling_lists = draw_coupling_lists(jax.random.fold_in(streams_of[6], 71), 0)
    live_counts = draw_live_counts(jax.random.fold_in(streams_of[6], 71), 0)
    return {"noise_draws": noise_draws, "inverse_diagonal": inverse_diagonal, "coupling_blocks": coupling_blocks, "ancestor_pick": ancestor_pick, "coupling_lists": coupling_lists, "live_counts": live_counts}


def apply_inverse(inverse, right_side):
    product = jnp.einsum("nrc,nrs->ncs", inverse.astype(jnp.float32), right_side.astype(jnp.float32))
    return product.astype(jnp.bfloat16)


def reference(noise_draws, inverse_diagonal, coupling_blocks, ancestor_pick, coupling_lists, live_counts):
    owners = NODES // NODES_DEV
    node_owner = (jnp.arange(NODES) // NODES_DEV).astype(jnp.int32)
    levels_done = [apply_inverse(inverse_diagonal[0], noise_draws[0])]
    for level in range(1, LEVELS):
        known = jnp.concatenate(levels_done, axis=0)
        values = coupling_lists[level - 1]
        source_level = values // owners
        source_owner = values % owners
        local = ancestor_pick[source_level, node_owner[:, None], source_owner]
        rows_used = (source_level * NODES + source_owner * NODES_DEV + local).astype(jnp.int32)
        counts_here = live_counts[level - 1]
        blocks = coupling_blocks[level - 1]

        def turn(slot, total):
            picked = jnp.take(known, rows_used[:, slot], axis=0).astype(jnp.float32)
            alive = (slot < counts_here).astype(jnp.float32)
            block = lax.dynamic_index_in_dim(blocks, slot, 1, keepdims=False).astype(jnp.float32)
            return total + alive[:, None, None] * jnp.einsum("nrc,nrs->ncs", block, picked)

        updates = lax.fori_loop(0, COUPLE, turn, jnp.zeros(noise_draws.shape[1:], jnp.float32))
        right_side = (noise_draws[level].astype(jnp.float32) - updates).astype(jnp.bfloat16)
        levels_done.append(apply_inverse(inverse_diagonal[level], right_side))
    return jnp.stack(levels_done, axis=0)
```

```python
import functools

import jax
import jax.numpy as jnp
from jax import lax
from jax.experimental import pallas as pl
from jax.experimental.pallas import tpu as pltpu
from jax.sharding import PartitionSpec as P

CHUNKS = 2
VMEM = pl.BlockSpec(memory_space=pltpu.VMEM)
SMEM = pl.BlockSpec(memory_space=pltpu.SMEM)


def hop(value, axis, size, step):
    return lax.ppermute(value, axis, [(at, at ^ step) for at in range(size)])


def gather_parts(value, axis, size):
    parts = {0: value}
    step = size // 2
    while step:
        for have in sorted(parts):
            parts[have ^ step] = hop(parts[have], axis, size, step)
        step //= 2
    return [parts[at] for at in range(size)]


def transposed_dot(left, right):
    return lax.dot_general(
        left, right, (((0,), (0,)), ((), ())), preferred_element_type=jnp.float32
    )


def pick_block(blocks, index):
    return lax.dynamic_index_in_dim(blocks, index, 0, keepdims=False)


def exchange(blocks, picks, myself, owners):
    half = owners // 2
    far = hop(blocks, "leaf", owners, half)
    table = {}
    for step in range(1, half):
        table[step] = hop(pick_block(blocks, picks[myself ^ step, myself]), "leaf", owners, step)
    for step in range(1, half):
        wanted = pick_block(far, picks[myself ^ step, myself ^ half])
        table[step ^ half] = hop(wanted, "leaf", owners, step)
    table[0] = pick_block(blocks, picks[myself, myself])
    table[half] = pick_block(far, picks[myself, myself ^ half])
    return [table[at] for at in range(owners)]


def fill_rows(target, parts, draw):
    rows = parts[0].shape[1]
    for step, part in enumerate(parts):
        start = pl.multiple_of((draw ^ step) * rows, rows)
        target[:, pl.ds(start, rows), :] = part[...]


def add_slots(total, table, parts, scalars, lists, counts, source):
    owners = table.shape[0]
    myself, draw = scalars[0], scalars[1]
    nodes, width = parts[0].shape[:2]
    for step, part in enumerate(parts):
        for offset in range(width):
            slot = (draw ^ step) * width + offset
            for node in range(nodes):
                entry = lists[node, slot] - source * owners
                live = (slot < counts[node]) & (entry >= 0) & (entry < owners)

                @pl.when(live)
                def _():
                    total[node] += transposed_dot(part[node, offset], table[entry ^ myself])


def solve(result, inverse, total, noise):
    for node in range(noise.shape[0]):
        right_side = (noise[node].astype(jnp.float32) - total[node]).astype(jnp.bfloat16)
        result[node] = transposed_dot(inverse[node], right_side).astype(jnp.bfloat16)


def first_kernel(owners, draws, scalars, lists, counts, *refs):
    refs = list(refs)
    take = lambda count: [refs.pop(0) for _ in range(count)]
    table_in, picked, inv_first, inv_here, blocks = (
        take(owners), take(draws), take(draws), take(draws), take(draws)
    )
    noise_first, noise, below, here, table, inv_table, inv_full, total = take(8)
    draw = scalars[1]
    fill_rows(inv_table, picked, draw)
    for step in range(owners):
        table[step] = transposed_dot(inv_table[step], table_in[step][...]).astype(jnp.bfloat16)
    fill_rows(inv_full, inv_first, draw)
    for node in range(noise.shape[0]):
        below[node] = transposed_dot(inv_full[node], noise_first[node]).astype(jnp.bfloat16)
    total[...] = jnp.zeros_like(total)
    add_slots(total, table, blocks, scalars, lists, counts, 0)
    fill_rows(inv_full, inv_here, draw)
    solve(here, inv_full, total, noise)


def partial_kernel(source, draws, scalars, lists, counts, *refs):
    blocks, (table, total) = refs[:draws], refs[draws:]
    total[...] = jnp.zeros_like(total)
    add_slots(total, table, blocks, scalars, lists, counts, source)


def last_kernel(source, owners, draws, scalars, lists, counts, *refs):
    refs = list(refs)
    take = lambda count: [refs.pop(0) for _ in range(count)]
    table_in, inv_here, blocks = take(owners), take(draws), take(draws)
    before, noise, here, table, inv_full, total = take(6)
    for step in range(owners):
        table[step] = table_in[step][...]
    total[...] = before[...]
    add_slots(total, table, blocks, scalars, lists, counts, source)
    fill_rows(inv_full, inv_here, scalars[1])
    solve(here, inv_full, total, noise)


def call(kernel, outs, scratch, small, arrays):
    return pl.pallas_call(
        kernel,
        out_shape=outs,
        in_specs=[SMEM] * len(small) + [VMEM] * len(arrays),
        out_specs=jax.tree.map(lambda _: VMEM, outs),
        scratch_shapes=scratch,
        compiler_params=pltpu.CompilerParams(vmem_limit_bytes=48 * 1024 * 1024),
    )(*small, *arrays)


def on_device(owners, draws, noise, inverse, coupling, picks, lists, counts):
    myself, draw = lax.axis_index("leaf"), lax.axis_index("draw")
    scalars = jnp.stack([myself, draw]).astype(jnp.int32)
    levels, nodes, rows, columns = noise.shape
    wide = columns // CHUNKS
    bf16, f32 = jnp.bfloat16, jnp.float32
    pieces = [
        [noise[level, :, :, at * wide:(at + 1) * wide] for at in range(CHUNKS)]
        for level in range(levels)
    ]
    tables = [exchange(piece, picks[0], myself, owners) for piece in pieces[0]]
    mine = jnp.take(inverse[0], picks[0][:, myself], axis=0)
    got = lax.all_to_all(mine, "leaf", split_axis=0, concat_axis=0, tiled=True)
    got = jnp.take(got, myself ^ jnp.arange(owners), axis=0)
    picked = gather_parts(got, "draw", draws)
    blocks = [gather_parts(coupling[0], "draw", draws)]
    inv = gather_parts(inverse, "draw", draws)
    blocks += [gather_parts(coupling[at], "draw", draws) for at in range(1, levels - 1)]
    inv_at = lambda level: [part[level] for part in inv]
    table_shape = pltpu.VMEM((owners, rows, wide), bf16)
    total_shape = pltpu.VMEM((nodes, rows, wide), f32)
    inv_shape = pltpu.VMEM((nodes, rows, rows), bf16)
    solved = [[], []]
    known = []
    for at in range(CHUNKS):
        part = jax.ShapeDtypeStruct((nodes, rows, wide), bf16)
        below, here, table = call(
            functools.partial(first_kernel, owners, draws),
            (part, part, jax.ShapeDtypeStruct((owners, rows, wide), bf16)),
            [pltpu.VMEM((owners, rows, rows), bf16), inv_shape, total_shape],
            (scalars, lists[0], counts[0]),
            (*tables[at], *picked, *inv_at(0), *inv_at(1), *blocks[0],
             pieces[0][at], pieces[1][at]),
        )
        solved[0].append(below)
        solved[1].append(here)
        known.append([table])
    for level in range(2, levels):
        fresh = [exchange(piece, picks[level - 1], myself, owners) for piece in solved[level - 1]]
        solved.append([])
        for at in range(CHUNKS):
            before = sum(
                call(
                    functools.partial(partial_kernel, source, draws),
                    jax.ShapeDtypeStruct((nodes, rows, wide), f32),
                    [],
                    (scalars, lists[level - 1], counts[level - 1]),
                    (*blocks[level - 1], known[at][source]),
                )
                for source in range(level - 1)
            )
            here = call(
                functools.partial(last_kernel, level - 1, owners, draws),
                jax.ShapeDtypeStruct((nodes, rows, wide), bf16),
                [table_shape, inv_shape, total_shape],
                (scalars, lists[level - 1], counts[level - 1]),
                (*fresh[at], *inv_at(level), *blocks[level - 1], before, pieces[level][at]),
            )
            solved[level].append(here)
            known[at].append(jnp.stack(fresh[at]))
    return jnp.stack([jnp.concatenate(parts, axis=2) for parts in solved])


def solution(mesh):
    placed = (
        P(None, "leaf", None, "draw"),
        P(None, "leaf", "draw", None),
        P(None, "leaf", "draw", None, None),
        P(),
        P(None, "leaf", None),
        P(None, "leaf"),
    )
    return jax.shard_map(
        functools.partial(on_device, mesh.shape["leaf"], mesh.shape["draw"]),
        mesh=mesh,
        in_specs=placed,
        out_specs=P(None, "leaf", None, "draw"),
        check_vma=False,
    )
```

```python
import functools

import jax
import jax.numpy as jnp
from jax import lax
from jax.experimental import pallas as pl
from jax.experimental.pallas import tpu as pltpu
from jax.sharding import PartitionSpec as P

CHUNKS = 2
ANY = pl.BlockSpec(memory_space=pl.ANY)
SMEM = pl.BlockSpec(memory_space=pltpu.SMEM)
BF16, F32 = jnp.bfloat16, jnp.float32


def hop(value, axis, size, step):
    return lax.ppermute(value, axis, [(at, at ^ step) for at in range(size)])


def transposed_dot(left, right):
    return lax.dot_general(left, right, (((0,), (0,)), ((), ())), preferred_element_type=F32)


class Copies:
    def __init__(self, sems):
        self.sems, self.used = sems, 0

    def start(self, source, target):
        copy = pltpu.make_async_copy(source, target, self.sems.at[self.used])
        self.used += 1
        copy.start()
        return copy


def wait_all(copies):
    for copy in copies:
        copy.wait()


def load_rows(copies, target, parts):
    draws, _, rows, _ = parts.shape
    return [
        copies.start(parts.at[at], target.at[:, pl.ds(at * rows, rows), :])
        for at in range(draws)
    ]


def add_slots(total, table, blocks, lists, counts, source, myself):
    owners = table.shape[0]
    draws, nodes, width = blocks.shape[:3]
    for part in range(draws):
        for offset in range(width):
            slot = part * width + offset
            for node in range(nodes):
                entry = lists(node, slot) - source * owners
                live = (slot < counts(node)) & (entry >= 0) & (entry < owners)

                @pl.when(live)
                def _():
                    total[node] += transposed_dot(
                        blocks[part, node, offset], table[entry ^ myself]
                    )


def call(kernel, outs, scratch, small, arrays, aliases={}, sems=64, flops=0):
    return pl.pallas_call(
        kernel,
        out_shape=outs,
        in_specs=[SMEM] * len(small) + [ANY] * len(arrays),
        out_specs=jax.tree.map(lambda _: ANY, outs),
        scratch_shapes=[*scratch, pltpu.SemaphoreType.DMA((sems,))],
        input_output_aliases=aliases,
        compiler_params=pltpu.CompilerParams(vmem_limit_bytes=24 * 1024 * 1024),
    )(*small, *arrays)


def here_pick(picks, source, myself, step, origin):
    return picks[source, myself ^ step, myself ^ origin]


def own_first(owners, wide, picks, noise, inverse, *refs):
    out, own, *rest = refs
    sends, (right, inv, solved, sems) = rest[:-4], rest[-4:]
    myself = lax.axis_index("leaf")
    copies = Copies(sems)
    loads = [copies.start(noise.at[0], right)] + load_rows(copies, inv, inverse.at[:, 0])
    wait_all(loads)
    for node in range(inv.shape[0]):
        solved[node] = transposed_dot(inv[node], right[node]).astype(BF16)
    stores = [copies.start(solved, out.at[0]), copies.start(solved, own)]
    for step, send in enumerate(sends, 1):
        node = here_pick(picks, 0, myself, step, 0)
        stores.append(copies.start(solved.at[node, :, pl.ds(0, wide)], send))
    wait_all(stores)


def far_first(owners, wide, chunk, last, picks, far, inverse, own, *refs):
    half = owners // 2
    mine, *rest = refs
    sends, (right, inv, solved, sems) = rest[:-4], rest[-4:]
    myself = lax.axis_index("leaf")
    copies = Copies(sems)
    loads = [copies.start(far, right)] + load_rows(copies, inv, inverse)
    stores = []
    if not last:
        columns = pl.ds((chunk + 1) * wide, wide)
        for step, send in enumerate(sends, 1):
            node = here_pick(picks, 0, myself, step, 0)
            stores.append(copies.start(own.at[node, :, columns], send.at[1]))
    wait_all(loads)
    for node in range(inv.shape[0]):
        solved[node] = transposed_dot(inv[node], right[node]).astype(BF16)
    stores.append(copies.start(solved.at[here_pick(picks, 0, myself, 0, half)], mine))
    for step, send in enumerate(sends, 1):
        node = here_pick(picks, 0, myself, step, half)
        stores.append(copies.start(solved.at[node], send.at[0]))
    wait_all(stores)


def far_next(owners, source, last, picks, far, *refs):
    half = owners // 2
    own, refs = (None, refs) if last else (refs[0], refs[1:])
    sends, sems = refs[:-1], refs[-1]
    myself = lax.axis_index("leaf")
    copies = Copies(sems)
    stores = []
    for step, send in enumerate(sends, 1):
        node = here_pick(picks, source, myself, step, half)
        stores.append(copies.start(far.at[node], send.at[0]))
        if not last:
            node = here_pick(picks, source, myself, step, 0)
            stores.append(copies.start(own.at[node], send.at[1]))
    wait_all(stores)


def table_loads(copies, owners, wide, chunk, source, picks, myself, pieces, table):
    half = owners // 2
    own, far, near, distant = pieces
    columns = pl.ds(chunk * wide, wide)
    node = here_pick(picks, source, myself, 0, 0)
    whole = own.shape[-1] != wide
    loads = [copies.start(own.at[node, :, columns] if whole else own.at[node], table.at[0])]
    if len(far.shape) == 3:
        far = far.at[here_pick(picks, source, myself, 0, half)]
    loads.append(copies.start(far, table.at[half]))
    for step in range(1, half):
        ref = near[step - 1]
        loads.append(copies.start(ref if len(ref.shape) == 2 else ref.at[1], table.at[step]))
        loads.append(copies.start(distant[step - 1].at[0], table.at[half ^ step]))
    return loads


def split_pieces(owners, refs):
    side = owners // 2 - 1
    own, far = refs[:2]
    return (own, far, refs[2:2 + side], refs[2 + side:2 + 2 * side]), refs[2 + 2 * side:]


def partial_kernel(level, source, owners, wide, chunk, picks, lists, counts, blocks, *refs):
    pieces, refs = split_pieces(owners, refs)
    result, table, coupling, total, sems = refs
    myself = lax.axis_index("leaf")
    copies = Copies(sems)
    loads = [copies.start(blocks, coupling)]
    loads += table_loads(copies, owners, wide, chunk, source, picks, myself, pieces, table)
    total[...] = jnp.zeros_like(total)
    wait_all(loads)
    add_slots(
        total, table, coupling, lambda node, slot: lists[level - 1, node, slot],
        lambda node: counts[level - 1, node], source, myself,
    )
    copies.start(total, result).wait()


def level_kernel(
    level, owners, wide, chunk, befores, sending,
    picks, lists, counts, noise, inverse, blocks, out_before, *refs,
):
    befores_in, refs = refs[:befores], refs[befores:]
    pieces, refs = split_pieces(owners, refs)
    out, solved, *refs = refs
    side = owners // 2 - 1 if sending else 0
    sends, (table, coupling, total, inv, right, here, sems) = refs[:side], refs[side:]
    myself = lax.axis_index("leaf")
    copies = Copies(sems)
    source = level - 1
    columns = pl.ds(chunk * wide, wide)
    loads = [copies.start(before, total) for before in befores_in]
    if not befores:
        total[...] = jnp.zeros_like(total)
    loads.append(copies.start(blocks, coupling))
    loads += table_loads(copies, owners, wide, chunk, source, picks, myself, pieces, table)
    later = [copies.start(noise.at[level, :, :, columns], right)]
    later += load_rows(copies, inv, inverse.at[:, level])
    wait_all(loads)
    add_slots(
        total, table, coupling, lambda node, slot: lists[level - 1, node, slot],
        lambda node: counts[level - 1, node], source, myself,
    )
    wait_all(later)
    for node in range(inv.shape[0]):
        side_here = (right[node].astype(F32) - total[node]).astype(BF16)
        here[node] = transposed_dot(inv[node], side_here).astype(BF16)
    stores = [copies.start(here, out.at[level, :, :, columns]), copies.start(here, solved)]
    for step, send in enumerate(sends, 1):
        node = here_pick(picks, level, myself, step, 0)
        stores.append(copies.start(here.at[node], send))
    wait_all(stores)


def on_device(owners, draws, noise, inverse, coupling, picks, lists, counts):
    levels, nodes, rows, columns = noise.shape
    wide, half = columns // CHUNKS, owners // 2
    width = coupling.shape[2]
    shape = lambda *dims, kind=BF16: jax.ShapeDtypeStruct(dims, kind)
    block = shape(rows, wide)
    message = shape(2, rows, wide)
    part = shape(nodes, rows, wide)
    table = pltpu.VMEM((owners, rows, wide), BF16)
    blocks_here = pltpu.VMEM((draws, nodes, width, rows, rows), BF16)
    total = pltpu.VMEM((nodes, rows, wide), F32)
    inv = pltpu.VMEM((nodes, rows, rows), BF16)
    chunk_here = pltpu.VMEM((nodes, rows, wide), BF16)
    leaf = lambda value, step: hop(value, "leaf", owners, step)
    near = lambda values: [leaf(value, step) for step, value in enumerate(values, 1)]
    gather = lambda value: lax.all_gather(value, "draw", axis=0)

    chunks = range(CHUNKS)
    far_inverse = leaf(inverse[0], half)
    far = [leaf(noise[0, :, :, at * wide:(at + 1) * wide], half) for at in chunks]
    blocks = [gather(coupling[at]) for at in range(levels - 1)]
    inverse_all = gather(inverse)
    far_inverse_all = gather(far_inverse)

    out, own, *sends = call(
        functools.partial(own_first, owners, wide),
        [shape(levels, nodes, rows, columns), shape(nodes, rows, columns)] + [block] * (half - 1),
        [pltpu.VMEM((nodes, rows, columns), BF16), inv, pltpu.VMEM((nodes, rows, columns), BF16)],
        (picks,),
        (noise, inverse_all),
    )
    got = [near(sends)]
    mine = []
    for at in chunks:
        last = at == CHUNKS - 1
        kept, *sends = call(
            functools.partial(far_first, owners, wide, at, last),
            [block] + [shape(1, rows, wide) if last else message] * (half - 1),
            [chunk_here, inv, chunk_here],
            (picks,),
            (far[at], far_inverse_all, own),
        )
        mine.append(kept)
        got.append(near(sends))
    pieces = [[(own, mine[at], *got[at], *got[at + 1]) for at in chunks]]

    for level in range(1, levels):
        solved, sends = [], []
        for at in chunks:
            befores = [
                call(
                    functools.partial(partial_kernel, level, source, owners, wide, at),
                    shape(nodes, rows, wide, kind=F32),
                    [table, blocks_here, total],
                    (picks, lists, counts),
                    (blocks[level - 1], *pieces[source][at]),
                )
                for source in range(level - 1)
            ]
            befores = [functools.reduce(jnp.add, befores)] if befores else []
            sending = at == 0 and level < levels - 1
            out, here, *sent = call(
                functools.partial(level_kernel, level, owners, wide, at, len(befores), sending),
                [shape(*out.shape), part] + ([block] * (half - 1) if sending else []),
                [table, blocks_here, total, inv, chunk_here, chunk_here],
                (picks, lists, counts),
                (noise, inverse_all, blocks[level - 1], out, *befores, *pieces[level - 1][at]),
                aliases={6: 0},
            )
            solved.append(here)
            sends += sent
        if level == levels - 1:
            break
        far = [leaf(here, half) for here in solved]
        got = [near(sends)]
        for at in chunks:
            last = at == CHUNKS - 1
            sends = call(
                functools.partial(far_next, owners, level, last),
                [shape(1, rows, wide) if last else message] * (half - 1),
                [],
                (picks,),
                (far[at],) if last else (far[at], solved[at + 1]),
            )
            got.append(near(sends))
        pieces.append([(solved[at], far[at], *got[at], *got[at + 1]) for at in chunks])
    return out


def solution(mesh):
    placed = (
        P(None, "leaf", None, "draw"),
        P(None, "leaf", "draw", None),
        P(None, "leaf", "draw", None, None),
        P(),
        P(None, "leaf", None),
        P(None, "leaf"),
    )
    return jax.shard_map(
        functools.partial(on_device, mesh.shape["leaf"], mesh.shape["draw"]),
        mesh=mesh,
        in_specs=placed,
        out_specs=P(None, "leaf", None, "draw"),
        check_vma=False,
    )
```

```python
import functools

import jax
import jax.numpy as jnp
from jax import lax
from jax.experimental import pallas as pl
from jax.experimental.pallas import tpu as pltpu
from jax.sharding import PartitionSpec as P

CHUNKS = 2
HBM = pl.BlockSpec(memory_space=pltpu.HBM)
SMEM = pl.BlockSpec(memory_space=pltpu.SMEM)
BF16, F32 = jnp.bfloat16, jnp.float32


def hop(value, axis, size, step):
    return lax.ppermute(value, axis, [(at, at ^ step) for at in range(size)])


def gather_parts(value, axis, size):
    parts = {0: value}
    step = size // 2
    while step:
        for have in sorted(parts):
            parts[have ^ step] = hop(parts[have], axis, size, step)
        step //= 2
    return [parts[at] for at in range(size)]


def transposed_dot(left, right):
    return lax.dot_general(left, right, (((0,), (0,)), ((), ())), preferred_element_type=F32)


class Copies:
    def __init__(self, sems):
        self.sems, self.used = sems, 0

    def start(self, source, target):
        copy = pltpu.make_async_copy(source, target, self.sems.at[self.used])
        self.used += 1
        copy.start()
        return copy


def wait_all(copies):
    for copy in copies:
        copy.wait()


def load_rows(copies, target, parts):
    draw = lax.axis_index("draw")
    rows = parts[0].shape[1]
    loads = []
    for step, part in enumerate(parts):
        start = pl.multiple_of((draw ^ step) * rows, rows)
        loads.append(copies.start(part, target.at[:, pl.ds(start, rows), :]))
    return loads


def load_blocks(copies, target, parts):
    draw = lax.axis_index("draw")
    return [copies.start(part, target.at[draw ^ step]) for step, part in enumerate(parts)]


def add_slots(total, table, blocks, lists, counts, source, myself):
    owners = table.shape[0]
    draws, nodes, width = blocks.shape[:3]
    for part in range(draws):
        for offset in range(width):
            slot = part * width + offset
            for node in range(nodes):
                entry = lists(node, slot) - source * owners
                live = (slot < counts(node)) & (entry >= 0) & (entry < owners)

                @pl.when(live)
                def _():
                    total[node] += transposed_dot(
                        blocks[part, node, offset], table[entry ^ myself]
                    )


def call(kernel, outs, scratch, small, arrays, aliases={}, sems=64, flops=0):
    return pl.pallas_call(
        kernel,
        out_shape=outs,
        in_specs=[SMEM] * len(small) + [HBM] * len(arrays),
        out_specs=jax.tree.map(lambda _: HBM, outs),
        scratch_shapes=[*scratch, pltpu.SemaphoreType.DMA((sems,))],
        input_output_aliases=aliases,
        compiler_params=pltpu.CompilerParams(vmem_limit_bytes=24 * 1024 * 1024),
    )(*small, *arrays)


def here_pick(picks, source, myself, step, origin):
    return picks[source, myself ^ step, myself ^ origin]


def own_first(owners, draws, wide, picks, noise, *refs):
    inverse, refs = refs[:draws], refs[draws:]
    out, own, *rest = refs
    chunks = noise.shape[-1] // wide
    nexts, rest = rest[:chunks - 1], rest[chunks - 1:]
    sends, (right, inv, solved, sems) = rest[:-4], rest[-4:]
    myself = lax.axis_index("leaf")
    copies = Copies(sems)
    stores = [
        copies.start(noise.at[0, :, :, pl.ds(at * wide, wide)], target)
        for at, target in enumerate(nexts, 1)
    ]
    loads = [copies.start(noise.at[0], right)]
    loads += load_rows(copies, inv, [part.at[0] for part in inverse])
    wait_all(loads)
    for node in range(inv.shape[0]):
        solved[node] = transposed_dot(inv[node], right[node]).astype(BF16)
    stores += [copies.start(solved, out.at[0]), copies.start(solved, own)]
    for step, send in enumerate(sends, 1):
        node = here_pick(picks, 0, myself, step, 0)
        stores.append(copies.start(solved.at[node, :, pl.ds(0, wide)], send))
    wait_all(stores)


def far_first(owners, draws, wide, chunk, last, picks, far, own, *refs):
    half = owners // 2
    inverse, refs = refs[:draws], refs[draws:]
    mine, *rest = refs
    sends, (right, inv, solved, sems) = rest[:-4], rest[-4:]
    myself = lax.axis_index("leaf")
    copies = Copies(sems)
    loads = [copies.start(far, right)] + load_rows(copies, inv, inverse)
    stores = []
    if not last:
        columns = pl.ds((chunk + 1) * wide, wide)
        for step, send in enumerate(sends, 1):
            node = here_pick(picks, 0, myself, step, 0)
            stores.append(copies.start(own.at[node, :, columns], send.at[1]))
    wait_all(loads)
    for node in range(inv.shape[0]):
        solved[node] = transposed_dot(inv[node], right[node]).astype(BF16)
    stores.append(copies.start(solved.at[here_pick(picks, 0, myself, 0, half)], mine))
    for step, send in enumerate(sends, 1):
        node = here_pick(picks, 0, myself, step, half)
        stores.append(copies.start(solved.at[node], send.at[0]))
    wait_all(stores)


def far_next(owners, source, last, picks, far, *refs):
    half = owners // 2
    own, refs = (None, refs) if last else (refs[0], refs[1:])
    sends, sems = refs[:-1], refs[-1]
    myself = lax.axis_index("leaf")
    copies = Copies(sems)
    stores = []
    for step, send in enumerate(sends, 1):
        node = here_pick(picks, source, myself, step, half)
        stores.append(copies.start(far.at[node], send.at[0]))
        if not last:
            node = here_pick(picks, source, myself, step, 0)
            stores.append(copies.start(own.at[node], send.at[1]))
    wait_all(stores)


def table_loads(copies, owners, wide, chunk, source, picks, myself, pieces, table):
    half = owners // 2
    own, far, near, distant = pieces
    columns = pl.ds(chunk * wide, wide)
    node = here_pick(picks, source, myself, 0, 0)
    whole = own.shape[-1] != wide
    loads = [copies.start(own.at[node, :, columns] if whole else own.at[node], table.at[0])]
    if len(far.shape) == 3:
        far = far.at[here_pick(picks, source, myself, 0, half)]
    loads.append(copies.start(far, table.at[half]))
    for step in range(1, half):
        ref = near[step - 1]
        loads.append(copies.start(ref if len(ref.shape) == 2 else ref.at[1], table.at[step]))
        loads.append(copies.start(distant[step - 1].at[0], table.at[half ^ step]))
    return loads


def split_pieces(owners, refs):
    side = owners // 2 - 1
    own, far = refs[:2]
    return (own, far, refs[2:2 + side], refs[2 + side:2 + 2 * side]), refs[2 + 2 * side:]


def partial_kernel(level, source, owners, draws, wide, chunk, picks, lists, counts, *refs):
    blocks, refs = refs[:draws], refs[draws:]
    pieces, refs = split_pieces(owners, refs)
    result, table, coupling, total, sems = refs
    myself = lax.axis_index("leaf")
    copies = Copies(sems)
    loads = load_blocks(copies, coupling, blocks)
    loads += table_loads(copies, owners, wide, chunk, source, picks, myself, pieces, table)
    total[...] = jnp.zeros_like(total)
    wait_all(loads)
    add_slots(
        total, table, coupling, lambda node, slot: lists[level - 1, node, slot],
        lambda node: counts[level - 1, node], source, myself,
    )
    copies.start(total, result).wait()


def level_kernel(
    level, owners, draws, wide, chunk, befores, sending,
    picks, lists, counts, noise, out_before, *refs,
):
    inverse, refs = refs[:draws], refs[draws:]
    blocks, refs = refs[:draws], refs[draws:]
    befores_in, refs = refs[:befores], refs[befores:]
    pieces, refs = split_pieces(owners, refs)
    out, solved, *refs = refs
    side = owners // 2 - 1 if sending else 0
    sends, (table, coupling, total, inv, right, here, sems) = refs[:side], refs[side:]
    myself = lax.axis_index("leaf")
    copies = Copies(sems)
    source = level - 1
    columns = pl.ds(chunk * wide, wide)
    loads = [copies.start(before, total) for before in befores_in]
    if not befores:
        total[...] = jnp.zeros_like(total)
    loads += load_blocks(copies, coupling, blocks)
    loads += table_loads(copies, owners, wide, chunk, source, picks, myself, pieces, table)
    later = [copies.start(noise.at[level, :, :, columns], right)]
    later += load_rows(copies, inv, [part.at[level] for part in inverse])
    wait_all(loads)
    add_slots(
        total, table, coupling, lambda node, slot: lists[level - 1, node, slot],
        lambda node: counts[level - 1, node], source, myself,
    )
    wait_all(later)
    for node in range(inv.shape[0]):
        side_here = (right[node].astype(F32) - total[node]).astype(BF16)
        here[node] = transposed_dot(inv[node], side_here).astype(BF16)
    stores = [copies.start(here, out.at[level, :, :, columns]), copies.start(here, solved)]
    for step, send in enumerate(sends, 1):
        node = here_pick(picks, level, myself, step, 0)
        stores.append(copies.start(here.at[node], send))
    wait_all(stores)


def on_device(owners, draws, noise, inverse, coupling, picks, lists, counts):
    levels, nodes, rows, columns = noise.shape
    wide, half = columns // CHUNKS, owners // 2
    width = coupling.shape[2]
    shape = lambda *dims, kind=BF16: jax.ShapeDtypeStruct(dims, kind)
    block = shape(rows, wide)
    message = shape(2, rows, wide)
    part = shape(nodes, rows, wide)
    table = pltpu.VMEM((owners, rows, wide), BF16)
    blocks_here = pltpu.VMEM((draws, nodes, width, rows, rows), BF16)
    total = pltpu.VMEM((nodes, rows, wide), F32)
    inv = pltpu.VMEM((nodes, rows, rows), BF16)
    chunk_here = pltpu.VMEM((nodes, rows, wide), BF16)
    leaf = lambda value, step: hop(value, "leaf", owners, step)
    near = lambda values: [leaf(value, step) for step, value in enumerate(values, 1)]
    gather = lambda value: gather_parts(value, "draw", draws)

    chunks = range(CHUNKS)
    far_inverse = leaf(inverse[0], half)
    far = [leaf(noise[0, :, :, :wide], half)]
    inverse_all = gather(inverse)
    far_inverse_all = gather(far_inverse)
    blocks = [gather(coupling[at]) for at in range(levels - 1)]

    out, own, *sends = call(
        functools.partial(own_first, owners, draws, wide),
        [shape(levels, nodes, rows, columns), shape(nodes, rows, columns)]
        + [part] * (CHUNKS - 1) + [block] * (half - 1),
        [pltpu.VMEM((nodes, rows, columns), BF16), inv, pltpu.VMEM((nodes, rows, columns), BF16)],
        (picks,),
        (noise, *inverse_all),
    )
    far += [leaf(piece, half) for piece in sends[:CHUNKS - 1]]
    got = [near(sends[CHUNKS - 1:])]
    mine = []
    for at in chunks:
        last = at == CHUNKS - 1
        kept, *sends = call(
            functools.partial(far_first, owners, draws, wide, at, last),
            [block] + [shape(1, rows, wide) if last else message] * (half - 1),
            [chunk_here, inv, chunk_here],
            (picks,),
            (far[at], own, *far_inverse_all),
        )
        mine.append(kept)
        got.append(near(sends))
    pieces = [[(own, mine[at], *got[at], *got[at + 1]) for at in chunks]]

    for level in range(1, levels):
        solved, sends = [], []
        for at in chunks:
            befores = [
                call(
                    functools.partial(partial_kernel, level, source, owners, draws, wide, at),
                    shape(nodes, rows, wide, kind=F32),
                    [table, blocks_here, total],
                    (picks, lists, counts),
                    (*blocks[level - 1], *pieces[source][at]),
                )
                for source in range(level - 1)
            ]
            befores = [functools.reduce(jnp.add, befores)] if befores else []
            sending = at == 0 and level < levels - 1
            out, here, *sent = call(
                functools.partial(level_kernel, level, owners, draws, wide, at, len(befores), sending),
                [shape(*out.shape), part] + ([block] * (half - 1) if sending else []),
                [table, blocks_here, total, inv, chunk_here, chunk_here],
                (picks, lists, counts),
                (noise, out, *inverse_all, *blocks[level - 1], *befores, *pieces[level - 1][at]),
                aliases={4: 0},
            )
            solved.append(here)
            sends += sent
        if level == levels - 1:
            break
        far = [leaf(here, half) for here in solved]
        got = [near(sends)]
        for at in chunks:
            last = at == CHUNKS - 1
            sends = call(
                functools.partial(far_next, owners, level, last),
                [shape(1, rows, wide) if last else message] * (half - 1),
                [],
                (picks,),
                (far[at],) if last else (far[at], solved[at + 1]),
            )
            got.append(near(sends))
        pieces.append([(solved[at], far[at], *got[at], *got[at + 1]) for at in chunks])
    return out


def solution(mesh):
    placed = (
        P(None, "leaf", None, "draw"),
        P(None, "leaf", "draw", None),
        P(None, "leaf", "draw", None, None),
        P(),
        P(None, "leaf", None),
        P(None, "leaf"),
    )
    return jax.shard_map(
        functools.partial(on_device, mesh.shape["leaf"], mesh.shape["draw"]),
        mesh=mesh,
        in_specs=placed,
        out_specs=P(None, "leaf", None, "draw"),
        check_vma=False,
    )
```

```python
import functools

import jax
import jax.numpy as jnp
from jax import lax
from jax.experimental import pallas as pl
from jax.experimental.pallas import tpu as pltpu
from jax.sharding import PartitionSpec as P

CHUNKS = 2
HBM = pl.BlockSpec(memory_space=pltpu.HBM)
SMEM = pl.BlockSpec(memory_space=pltpu.SMEM)
BF16, F32 = jnp.bfloat16, jnp.float32


def hop(value, axis, size, step):
    return lax.ppermute(value, axis, [(at, at ^ step) for at in range(size)])


def gather_parts(value, axis, size):
    parts = {0: value}
    step = size // 2
    while step:
        for have in sorted(parts):
            parts[have ^ step] = hop(parts[have], axis, size, step)
        step //= 2
    return [parts[at] for at in range(size)]


def transposed_dot(left, right):
    return lax.dot_general(left, right, (((0,), (0,)), ((), ())), preferred_element_type=F32)


class Copies:
    def __init__(self, sems):
        self.sems, self.used = sems, 0

    def start(self, source, target):
        copy = pltpu.make_async_copy(source, target, self.sems.at[self.used])
        self.used += 1
        copy.start()
        return copy


def wait_all(copies):
    for copy in copies:
        copy.wait()


def load_rows(copies, target, parts):
    draw = lax.axis_index("draw")
    rows = parts[0].shape[1]
    loads = []
    for step, part in enumerate(parts):
        start = pl.multiple_of((draw ^ step) * rows, rows)
        loads.append(copies.start(part, target.at[:, pl.ds(start, rows), :]))
    return loads


def load_blocks(copies, target, parts):
    draw = lax.axis_index("draw")
    return [copies.start(part, target.at[draw ^ step]) for step, part in enumerate(parts)]


def coupled(node, table, blocks, entries, count, owners, myself):
    draws, _, width = blocks.shape[:3]
    empty = table.shape[0] - 1
    total = None
    for slot in range(draws * width):
        entry = jnp.where(slot < count, entries(slot) ^ myself, empty)
        term = transposed_dot(blocks[slot // width, node, slot % width], table[entry])
        total = term if total is None else total + term
    return total


def call(kernel, outs, scratch, small, arrays, aliases={}):
    sems = len(arrays) + 2 * len(outs)
    return pl.pallas_call(
        kernel,
        out_shape=outs,
        in_specs=[SMEM] * len(small) + [HBM] * len(arrays),
        out_specs=jax.tree.map(lambda _: HBM, outs),
        scratch_shapes=[*scratch, pltpu.SemaphoreType.DMA((sems,))],
        input_output_aliases=aliases,
        compiler_params=pltpu.CompilerParams(vmem_limit_bytes=24 * 1024 * 1024),
    )(*small, *arrays)


def here_pick(picks, source, myself, step, origin):
    return picks[source, myself ^ step, myself ^ origin]


def own_first(owners, draws, wide, picks, noise, coupling, *refs):
    inverse, refs = refs[:draws], refs[draws:]
    out, own, blocks, *rest = refs
    chunks = noise.shape[-1] // wide
    nexts, rest = rest[:chunks - 1], rest[chunks - 1:]
    sends, (right, inv, solved, sems) = rest[:-4], rest[-4:]
    myself = lax.axis_index("leaf")
    copies = Copies(sems)
    loads = [copies.start(noise.at[0], right)]
    loads += load_rows(copies, inv, [part.at[0] for part in inverse])
    stores = [
        copies.start(noise.at[0, :, :, pl.ds(at * wide, wide)], target)
        for at, target in enumerate(nexts, 1)
    ]
    stores.append(copies.start(coupling.at[0], blocks))
    wait_all(loads)
    for node in range(inv.shape[0]):
        solved[node] = transposed_dot(inv[node], right[node]).astype(BF16)
    stores += [copies.start(solved, out.at[0]), copies.start(solved, own)]
    for step, send in enumerate(sends, 1):
        node = here_pick(picks, 0, myself, step, 0)
        stores.append(copies.start(solved.at[node, :, pl.ds(0, wide)], send))
    wait_all(stores)


def far_first(owners, draws, wide, chunk, last, picks, far, own, coupling, *refs):
    half = owners // 2
    inverse, refs = refs[:draws], refs[draws:]
    mine, *rest = refs
    later, rest = (rest[:coupling.shape[0] - 1], rest[coupling.shape[0] - 1:]) if chunk == 0 else ([], rest)
    sends, (right, inv, solved, sems) = rest[:-4], rest[-4:]
    myself = lax.axis_index("leaf")
    copies = Copies(sems)
    loads = [copies.start(far, right)] + load_rows(copies, inv, inverse)
    stores = [copies.start(coupling.at[at], target) for at, target in enumerate(later, 1)]
    if not last:
        columns = pl.ds((chunk + 1) * wide, wide)
        for step, send in enumerate(sends, 1):
            node = here_pick(picks, 0, myself, step, 0)
            stores.append(copies.start(own.at[node, :, columns], send.at[1]))
    wait_all(loads)
    for node in range(inv.shape[0]):
        solved[node] = transposed_dot(inv[node], right[node]).astype(BF16)
    stores.append(copies.start(solved.at[here_pick(picks, 0, myself, 0, half)], mine))
    for step, send in enumerate(sends, 1):
        node = here_pick(picks, 0, myself, step, half)
        stores.append(copies.start(solved.at[node], send.at[0]))
    wait_all(stores)


def far_next(owners, source, last, picks, far, *refs):
    half = owners // 2
    own, refs = (None, refs) if last else (refs[0], refs[1:])
    sends, sems = refs[:-1], refs[-1]
    myself = lax.axis_index("leaf")
    copies = Copies(sems)
    stores = []
    for step, send in enumerate(sends, 1):
        node = here_pick(picks, source, myself, step, half)
        stores.append(copies.start(far.at[node], send.at[0]))
        if not last:
            node = here_pick(picks, source, myself, step, 0)
            stores.append(copies.start(own.at[node], send.at[1]))
    wait_all(stores)


def table_loads(copies, owners, wide, chunk, source, picks, myself, pieces, table):
    half = owners // 2
    own, far, near, distant = pieces
    columns = pl.ds(chunk * wide, wide)
    node = here_pick(picks, source, myself, 0, 0)
    whole = own.shape[-1] != wide
    first = source * owners
    loads = [copies.start(own.at[node, :, columns] if whole else own.at[node], table.at[first])]
    if len(far.shape) == 3:
        far = far.at[here_pick(picks, source, myself, 0, half)]
    loads.append(copies.start(far, table.at[first + half]))
    for step in range(1, half):
        ref = near[step - 1]
        loads.append(copies.start(ref if len(ref.shape) == 2 else ref.at[1], table.at[first + step]))
        loads.append(copies.start(distant[step - 1].at[0], table.at[first + (half ^ step)]))
    return loads


def split_pieces(owners, refs):
    side = owners // 2 - 1
    own, far = refs[:2]
    return (own, far, refs[2:2 + side], refs[2 + side:2 + 2 * side]), refs[2 + 2 * side:]


def level_kernel(
    level, owners, draws, wide, chunk, sending, picks, lists, counts, noise, out_before, *refs
):
    inverse, refs = refs[:draws], refs[draws:]
    blocks, refs = refs[:draws], refs[draws:]
    pieces = []
    for _ in range(level):
        piece, refs = split_pieces(owners, refs)
        pieces.append(piece)
    out, solved, *refs = refs
    side = owners // 2 - 1 if sending else 0
    sends, (table, coupling, inv, right, here, sems) = refs[:side], refs[side:]
    myself = lax.axis_index("leaf")
    copies = Copies(sems)
    columns = pl.ds(chunk * wide, wide)
    loads = load_blocks(copies, coupling, blocks)
    for source, piece in enumerate(pieces):
        loads += table_loads(copies, owners, wide, chunk, source, picks, myself, piece, table)
    later = [copies.start(noise.at[level, :, :, columns], right)]
    later += load_rows(copies, inv, [part.at[level] for part in inverse])
    table[level * owners] = jnp.zeros_like(table[level * owners])
    wait_all(loads)
    nodes = inv.shape[0]
    totals = [
        coupled(
            node, table, coupling, lambda slot: lists[level - 1, node, slot],
            counts[level - 1, node], owners, myself,
        )
        for node in range(nodes)
    ]
    wait_all(later)
    stores = []
    for node in range(nodes):
        side_here = (right[node].astype(F32) - totals[node]).astype(BF16)
        here[node] = transposed_dot(inv[node], side_here).astype(BF16)
    stores += [copies.start(here, solved), copies.start(here, out.at[level, :, :, columns])]
    for step, send in enumerate(sends, 1):
        node = here_pick(picks, level, myself, step, 0)
        stores.append(copies.start(here.at[node], send))
    wait_all(stores)


def on_device(owners, draws, noise, inverse, coupling, picks, lists, counts):
    levels, nodes, rows, columns = noise.shape
    wide, half = columns // CHUNKS, owners // 2
    width = coupling.shape[2]
    shape = lambda *dims, kind=BF16: jax.ShapeDtypeStruct(dims, kind)
    block = shape(rows, wide)
    message = shape(2, rows, wide)
    part = shape(nodes, rows, wide)
    table = lambda level: pltpu.VMEM((level * owners + 1, rows, wide), BF16)
    blocks_here = pltpu.VMEM((draws, nodes, width, rows, rows), BF16)
    inv = pltpu.VMEM((nodes, rows, rows), BF16)
    chunk_here = pltpu.VMEM((nodes, rows, wide), BF16)
    leaf = lambda value, step: hop(value, "leaf", owners, step)
    near = lambda values: [leaf(value, step) for step, value in enumerate(values, 1)]
    gather = lambda value: gather_parts(value, "draw", draws)

    chunks = range(CHUNKS)
    far_inverse = leaf(inverse[0], half)
    far = [leaf(noise[0, :, :, :wide], half)]
    inverse_all = gather(inverse)
    far_inverse_all = gather(far_inverse)

    out, own, first, *sends = call(
        functools.partial(own_first, owners, draws, wide),
        [shape(levels, nodes, rows, columns), shape(nodes, rows, columns), shape(*coupling.shape[1:])]
        + [part] * (CHUNKS - 1) + [block] * (half - 1),
        [pltpu.VMEM((nodes, rows, columns), BF16), inv, pltpu.VMEM((nodes, rows, columns), BF16)],
        (picks,),
        (noise, coupling, *inverse_all),
    )
    blocks = [gather(first)]
    far += [leaf(piece, half) for piece in sends[:CHUNKS - 1]]
    got = [near(sends[CHUNKS - 1:])]
    mine = []
    for at in chunks:
        last = at == CHUNKS - 1
        kept, *sends = call(
            functools.partial(far_first, owners, draws, wide, at, last),
            [block] + ([shape(*coupling.shape[1:])] * (levels - 2) if at == 0 else [])
            + [shape(1, rows, wide) if last else message] * (half - 1),
            [chunk_here, inv, chunk_here],
            (picks,),
            (far[at], own, coupling, *far_inverse_all),
        )
        mine.append(kept)
        if at == 0:
            blocks += [gather(value) for value in sends[:levels - 2]]
            sends = sends[levels - 2:]
        got.append(near(sends))
    pieces = [[(own, mine[at], *got[at], *got[at + 1]) for at in chunks]]

    for level in range(1, levels):
        solved, sends = [], []
        for at in chunks:
            sending = at == 0 and level < levels - 1
            out, here, *sent = call(
                functools.partial(level_kernel, level, owners, draws, wide, at, sending),
                [shape(*out.shape), part] + ([block] * (half - 1) if sending else []),
                [table(level), blocks_here, inv, chunk_here, chunk_here],
                (picks, lists, counts),
                (
                    noise, out, *inverse_all, *blocks[level - 1],
                    *(ref for source in range(level) for ref in pieces[source][at]),
                ),
                aliases={4: 0},
            )
            solved.append(here)
            sends += sent
        if level == levels - 1:
            break
        far = [leaf(here, half) for here in solved]
        got = [near(sends)]
        for at in chunks:
            last = at == CHUNKS - 1
            sends = call(
                functools.partial(far_next, owners, level, last),
                [shape(1, rows, wide) if last else message] * (half - 1),
                [],
                (picks,),
                (far[at],) if last else (far[at], solved[at + 1]),
            )
            got.append(near(sends))
        pieces.append([(solved[at], far[at], *got[at], *got[at + 1]) for at in chunks])
    return out


def solution(mesh):
    placed = (
        P(None, "leaf", None, "draw"),
        P(None, "leaf", "draw", None),
        P(None, "leaf", "draw", None, None),
        P(),
        P(None, "leaf", None),
        P(None, "leaf"),
    )
    return jax.shard_map(
        functools.partial(on_device, mesh.shape["leaf"], mesh.shape["draw"]),
        mesh=mesh,
        in_specs=placed,
        out_specs=P(None, "leaf", None, "draw"),
        check_vma=False,
    )
```

```python
import functools

import jax
import jax.numpy as jnp
from jax import lax
from jax.experimental import pallas as pl
from jax.experimental.pallas import tpu as pltpu
from jax.sharding import PartitionSpec as P

CHUNKS = 2
VMEM = pl.BlockSpec(memory_space=pltpu.VMEM)
SMEM = pl.BlockSpec(memory_space=pltpu.SMEM)
ANY = pl.BlockSpec(memory_space=pl.ANY)
BF16, F32 = jnp.bfloat16, jnp.float32


def hop(value, axis, size, step):
    return lax.ppermute(value, axis, [(at, at ^ step) for at in range(size)])


def gather_parts(value, axis, size):
    parts = {0: value}
    step = size // 2
    while step:
        for have in sorted(parts):
            parts[have ^ step] = hop(parts[have], axis, size, step)
        step //= 2
    return [parts[at] for at in range(size)]


def transposed_dot(left, right):
    return lax.dot_general(left, right, (((0,), (0,)), ((), ())), preferred_element_type=F32)


def take(refs, count):
    return list(refs[:count]), list(refs[count:])


def call(kernel, outs, scratch, small, arrays, out_spec=VMEM, flops=0):
    size = sum(value.size * value.dtype.itemsize for value in (*arrays, *outs))
    return pl.pallas_call(
        kernel,
        out_shape=outs,
        in_specs=[SMEM] * len(small) + [VMEM] * len(arrays),
        out_specs=[out_spec] * len(outs),
        scratch_shapes=scratch,
        cost_estimate=pl.CostEstimate(flops=flops, bytes_accessed=size, transcendentals=0),
        compiler_params=pltpu.CompilerParams(vmem_limit_bytes=16 * 1024 * 1024),
    )(*small, *arrays)


def first_kernel(sides, picks, noise, inverse, *refs):
    *refs, inv = refs
    solved, sends = refs[:-sides], refs[-sides:]
    myself = lax.axis_index("leaf")
    draws, nodes, rows = inverse.shape[:3]
    wide = solved[0].shape[-1]
    for part in range(draws):
        inv[:, part * rows:(part + 1) * rows, :] = inverse[part]
    for at, target in enumerate(solved):
        for node in range(nodes):
            right = noise[node, :, at * wide:(at + 1) * wide]
            target[node] = transposed_dot(inv[node], right).astype(BF16)
    for step, send in enumerate(sends, 1):
        send[0] = solved[0][picks[0, myself ^ step, myself]]


def relay_kernel(half, source, last, picks, far, *refs):
    own, sends = (None, refs) if last else (refs[0], refs[1:])
    myself = lax.axis_index("leaf")
    for step, send in enumerate(sends, 1):
        send[0] = far[picks[source, myself ^ step, myself ^ half]]
        if not last:
            send[1] = own[picks[source, myself ^ step, myself]]


def level_kernel(
    level, owners, draws, chunk, waits, sides, earlier, width, picks, lists, counts, noise, *refs
):
    half = owners // 2
    _, refs = take(refs, waits)
    packs, refs = take(refs, draws)
    pieces = []
    for _ in range(level):
        piece, refs = take(refs, owners)
        pieces.append(piece)
    done, refs = take(refs, earlier)
    target, refs = refs[0], refs[1:]
    sends, (table, inv, *refs) = take(refs, sides)
    myself, draw = lax.axis_index("leaf"), lax.axis_index("draw")
    nodes, wide = noise.shape[1], table.shape[-1]
    depth = inv.shape[1]
    rows = depth // draws
    copies = []
    solved = target
    if earlier:
        solved, sems = refs
        per_level = (earlier + 1) // (level + 1)
        for at, ref in enumerate(done):
            here = target.at[at // per_level, :, :, pl.ds(at % per_level * wide, wide)]
            copies.append(pltpu.make_async_copy(ref, here, sems.at[at]))
            copies[-1].start()
    for source, (own, far, *others) in enumerate(pieces):
        first = source * owners
        table[first] = own[picks[source, myself, myself]]
        table[first + half] = far[picks[source, myself, myself ^ half]]
        for step in range(1, half):
            near, distant = others[step - 1], others[half + step - 2]
            table[first + step] = near[near.shape[0] - 1]
            table[first + (half ^ step)] = distant[0]
    empty = level * owners
    table[empty] = jnp.zeros_like(table[empty])
    for step, pack in enumerate(packs):
        start = pl.multiple_of((draw ^ step) * rows, rows)
        for node in range(nodes):
            at = nodes * width * depth + node * rows
            inv[node, pl.ds(start, rows), :] = pack[at:at + rows, :]
    for node in range(nodes):
        total = None
        for step, pack in enumerate(packs):
            for offset in range(width):
                slot = (draw ^ step) * width + offset
                live = slot < counts[level - 1, node]
                entry = jnp.where(live, lists[level - 1, node, slot] ^ myself, empty)
                at = (node * width + offset) * depth
                term = transposed_dot(pack[at:at + depth, :], table[entry])
                total = term if total is None else total + term
        side = noise[level, node, :, chunk * wide:(chunk + 1) * wide].astype(F32) - total
        solved[node] = transposed_dot(inv[node], side.astype(BF16)).astype(BF16)
    for step, send in enumerate(sends, 1):
        send[0] = solved[picks[level, myself ^ step, myself]]
    if earlier:
        here = target.at[level, :, :, pl.ds(chunk * wide, wide)]
        copies.append(pltpu.make_async_copy(solved, here, sems.at[earlier]))
        copies[-1].start()
    for copy in copies:
        copy.wait()


def on_device(owners, draws, noise, inverse, coupling, picks, lists, counts):
    levels, nodes, rows, columns = noise.shape
    wide, half, chunks = columns // CHUNKS, owners // 2, range(CHUNKS)
    width, last_level = coupling.shape[2], levels - 1
    shape = lambda *dims: jax.ShapeDtypeStruct(dims, BF16)
    part = shape(nodes, rows, wide)
    leaf = lambda value, step: hop(value, "leaf", owners, step)
    near = lambda values: [leaf(value, step) for step, value in enumerate(values, 1)]
    inv_here = pltpu.VMEM((nodes, rows, rows), BF16)
    dot_flops = 2 * rows * rows * wide

    inverse_first = lax.all_gather(inverse[0], "draw", axis=0)
    packs = [
        gather_parts(
            jnp.concatenate([coupling[level - 1].reshape(-1, rows), inverse[level].reshape(-1, rows)]),
            "draw", draws,
        )
        for level in range(1, levels)
    ]
    solved = call(
        functools.partial(first_kernel, half - 1),
        [part] * CHUNKS + [shape(1, rows, wide)] * (half - 1),
        [inv_here],
        (picks,),
        (noise[0], inverse_first),
        flops=nodes * CHUNKS * dot_flops,
    )
    solved, sends = solved[:CHUNKS], solved[CHUNKS:]
    done, pieces = [solved], []
    for level in range(1, levels):
        far = [leaf(value, half) for value in solved]
        got = [near(sends)]
        for at in chunks:
            last = at == CHUNKS - 1
            sends = call(
                functools.partial(relay_kernel, half, level - 1, last),
                [shape(1 if last else 2, rows, wide)] * (half - 1),
                [],
                (picks,),
                (far[at],) if last else (far[at], solved[at + 1]),
            )
            got.append(near(sends))
        pieces.append([(solved[at], far[at], *got[at], *got[at + 1]) for at in chunks])
        token = sends[:1]
        solved, sends = [], []
        for at in chunks:
            sides = half - 1 if at == 0 and level < last_level else 0
            final = level == last_level and at == CHUNKS - 1
            earlier = [value for values in done for value in values] + solved if final else []
            waits = token if at == 0 else []
            scratch = [pltpu.VMEM((level * owners + 1, rows, wide), BF16), inv_here]
            if final:
                scratch += [
                    pltpu.VMEM((nodes, rows, wide), BF16),
                    pltpu.SemaphoreType.DMA((len(earlier) + 1,)),
                ]
            here, *sent = call(
                functools.partial(
                    level_kernel, level, owners, draws, at, len(waits), sides, len(earlier), width
                ),
                [shape(levels, nodes, rows, columns) if final else part]
                + [shape(1, rows, wide)] * sides,
                scratch,
                (picks, lists, counts),
                (
                    noise, *waits, *packs[level - 1],
                    *(ref for source in range(level) for ref in pieces[source][at]),
                    *earlier,
                ),
                out_spec=ANY if final else VMEM,
                flops=nodes * (draws * width + 1) * dot_flops,
            )
            solved.append(here)
            sends += sent
        done.append(solved)
    return here


def solution(mesh):
    placed = (
        P(None, "leaf", None, "draw"),
        P(None, "leaf", "draw", None),
        P(None, "leaf", "draw", None, None),
        P(),
        P(None, "leaf", None),
        P(None, "leaf"),
    )
    return jax.shard_map(
        functools.partial(on_device, mesh.shape["leaf"], mesh.shape["draw"]),
        mesh=mesh,
        in_specs=placed,
        out_specs=P(None, "leaf", None, "draw"),
        check_vma=False,
    )
```

```python
import functools

import jax
import jax.numpy as jnp
from jax import lax
from jax.experimental import pallas as pl
from jax.experimental.pallas import tpu as pltpu
from jax.sharding import PartitionSpec as P

CHUNKS = 2
VMEM = pl.BlockSpec(memory_space=pltpu.VMEM)
SMEM = pl.BlockSpec(memory_space=pltpu.SMEM)
ANY = pl.BlockSpec(memory_space=pl.ANY)
BF16, F32 = jnp.bfloat16, jnp.float32


def hop(value, axis, size, step):
    return lax.ppermute(value, axis, [(at, at ^ step) for at in range(size)])


def gather_parts(value, axis, size):
    parts = {0: value}
    step = size // 2
    while step:
        for have in sorted(parts):
            parts[have ^ step] = hop(parts[have], axis, size, step)
        step //= 2
    return [parts[at] for at in range(size)]


def transposed_dot(left, right):
    return lax.dot_general(left, right, (((0,), (0,)), ((), ())), preferred_element_type=F32)


def take(refs, count):
    return list(refs[:count]), list(refs[count:])


def call(kernel, outs, scratch, small, arrays, out_spec=VMEM, flops=0):
    size = sum(value.size * value.dtype.itemsize for value in (*arrays, *outs))
    return pl.pallas_call(
        kernel,
        out_shape=outs,
        in_specs=[SMEM] * len(small) + [VMEM] * len(arrays),
        out_specs=[out_spec] * len(outs),
        scratch_shapes=scratch,
        cost_estimate=pl.CostEstimate(flops=flops, bytes_accessed=size, transcendentals=0),
        compiler_params=pltpu.CompilerParams(vmem_limit_bytes=16 * 1024 * 1024),
    )(*small, *arrays)


def write_pack(target, level, inverse, coupling):
    nodes, width, depth = coupling.shape[1:4]
    rows = inverse.shape[2]
    for node in range(nodes):
        for offset in range(width):
            at = (node * width + offset) * depth
            target[at:at + depth, :] = coupling[level - 1, node, offset]
        at = nodes * width * depth + node * rows
        target[at:at + rows, :] = inverse[level, node]


def first_kernel(chunks, picks, noise, inverse, coupling, gathered, *refs):
    pack, *refs, inv = refs
    solved, sends = take(refs, chunks)
    myself = lax.axis_index("leaf")
    draws, nodes, rows = gathered.shape[:3]
    wide = solved[0].shape[-1]
    for part in range(draws):
        inv[:, part * rows:(part + 1) * rows, :] = gathered[part]
    for at, target in enumerate(solved):
        for node in range(nodes):
            right = noise[0, node, :, at * wide:(at + 1) * wide]
            target[node] = transposed_dot(inv[node], right).astype(BF16)
    for step, send in enumerate(sends, 1):
        node = picks[0, myself ^ step, myself]
        for at, target in enumerate(solved):
            send[at] = target[node]
    write_pack(pack, 1, inverse, coupling)


def relay_kernel(owners, source, follow, pack_level, waits, picks, far, *refs):
    half = owners // 2
    if pack_level:
        inverse, coupling, *refs = refs
    own, refs = take(refs, follow)
    _, refs = take(refs, waits)
    sends, refs = take(refs, half - 1)
    myself = lax.axis_index("leaf")
    for step, send in enumerate(sends, 1):
        send[0] = far[picks[source, myself ^ step, myself ^ half]]
        if own:
            send[1] = own[0][picks[source, myself ^ step, myself]]
    if pack_level:
        write_pack(refs[0], pack_level, inverse, coupling)


def level_kernel(
    level, owners, draws, width, chunk, places, sides, earlier, waits,
    picks, lists, counts, noise, *refs,
):
    half = owners // 2
    packs, refs = take(refs, draws)
    known, refs = take(refs, level * owners)
    done, refs = take(refs, earlier)
    _, refs = take(refs, waits)
    target, *refs = refs
    sends, (table, inv, *refs) = take(refs, sides)
    myself, draw = lax.axis_index("leaf"), lax.axis_index("draw")
    nodes, wide = noise.shape[1], table.shape[-1]
    depth = inv.shape[1]
    rows = depth // draws
    copies = []
    solved = target
    if earlier:
        solved, sems = refs
        per_level = (earlier + 1) // (level + 1)
        for at, ref in enumerate(done):
            here = target.at[at // per_level, :, :, pl.ds(at % per_level * wide, wide)]
            copies.append(pltpu.make_async_copy(ref, here, sems.at[at]))
            copies[-1].start()
    for at, (ref, place) in enumerate(zip(known, places, strict=True)):
        step = at % owners
        if step % half == 0:
            place = picks[at // owners, myself, myself ^ step]
        table[at] = ref[place]
    empty = level * owners
    table[empty] = jnp.zeros_like(table[empty])
    for step, pack in enumerate(packs):
        start = pl.multiple_of((draw ^ step) * rows, rows)
        for node in range(nodes):
            at = nodes * width * depth + node * rows
            inv[node, pl.ds(start, rows), :] = pack[at:at + rows, :]
    for node in range(nodes):
        total = None
        for step, pack in enumerate(packs):
            for offset in range(width):
                slot = (draw ^ step) * width + offset
                live = slot < counts[level - 1, node]
                entry = jnp.where(live, lists[level - 1, node, slot] ^ myself, empty)
                at = (node * width + offset) * depth
                term = transposed_dot(pack[at:at + depth, :], table[entry])
                total = term if total is None else total + term
        side = noise[level, node, :, chunk * wide:(chunk + 1) * wide].astype(F32) - total
        solved[node] = transposed_dot(inv[node], side.astype(BF16)).astype(BF16)
    for step, send in enumerate(sends, 1):
        send[0] = solved[picks[level, myself ^ step, myself]]
    if earlier:
        here = target.at[level, :, :, pl.ds(chunk * wide, wide)]
        copies.append(pltpu.make_async_copy(solved, here, sems.at[earlier]))
        copies[-1].start()
    for copy in copies:
        copy.wait()


def on_device(owners, draws, noise, inverse, coupling, picks, lists, counts):
    levels, nodes, rows, columns = noise.shape
    wide, half, chunks = columns // CHUNKS, owners // 2, range(CHUNKS)
    width, last_level = coupling.shape[2], levels - 1
    shape = lambda *dims: jax.ShapeDtypeStruct(dims, BF16)
    part = shape(nodes, rows, wide)
    pack_shape = shape(nodes * (width * rows + inverse.shape[2]), rows)
    leaf = lambda value, step: hop(value, "leaf", owners, step)
    near = lambda values: [leaf(value, step) for step, value in enumerate(values, 1)]
    gather = lambda value: gather_parts(value, "draw", draws)
    inv_here = pltpu.VMEM((nodes, rows, rows), BF16)
    dot_flops = 2 * rows * rows * wide

    pack, *refs = call(
        functools.partial(first_kernel, CHUNKS),
        [pack_shape] + [part] * CHUNKS + [shape(CHUNKS, rows, wide)] * (half - 1),
        [inv_here],
        (picks,),
        (noise, inverse, coupling, lax.all_gather(inverse[0], "draw", axis=0)),
        flops=nodes * CHUNKS * dot_flops,
    )
    solved, sends = take(refs, CHUNKS)
    packs = [gather(pack)]
    done, pieces = [solved], []
    for level in range(1, levels):
        source = level - 1
        far = [leaf(value, half) for value in solved]
        got = near(sends)
        close = [[(ref, at) for ref in got] for at in chunks] if source == 0 else [[(ref, 0) for ref in got]]
        distant, waits = [], packs[source] if source == 0 else got
        for at in chunks:
            follow = source > 0 and at < CHUNKS - 1
            pack_level = source + 2 if at == 0 and source + 2 < levels else 0
            sends = list(call(
                functools.partial(relay_kernel, owners, source, int(follow), pack_level, len(waits)),
                [shape(1 + follow, rows, wide)] * (half - 1) + [pack_shape] * bool(pack_level),
                [],
                (picks,),
                (
                    far[at], *((inverse, coupling) if pack_level else ()),
                    *([solved[at + 1]] if follow else []), *waits,
                ),
            ))
            if pack_level:
                packs.append(gather(sends.pop()))
            got = near(sends)
            distant.append([(ref, 0) for ref in got])
            if follow:
                close.append([(ref, 1) for ref in got])
            waits = []
        pieces.append([
            [(solved[at], 0), *close[at], (far[at], 0), *distant[at]] for at in chunks
        ])
        waits = sends[:1]
        solved, sends = [], []
        for at in chunks:
            sides = half - 1 if at == 0 and level < last_level else 0
            final = level == last_level and at == CHUNKS - 1
            earlier = [value for values in done for value in values] + solved if final else []
            known = [entry for below in range(level) for entry in pieces[below][at]]
            scratch = [pltpu.VMEM((level * owners + 1, rows, wide), BF16), inv_here]
            if final:
                scratch += [
                    pltpu.VMEM((nodes, rows, wide), BF16),
                    pltpu.SemaphoreType.DMA((len(earlier) + 1,)),
                ]
            here, *sent = call(
                functools.partial(
                    level_kernel, level, owners, draws, width, at,
                    [place for _, place in known], sides, len(earlier), len(waits),
                ),
                [shape(levels, nodes, rows, columns) if final else part]
                + [shape(1, rows, wide)] * sides,
                scratch,
                (picks, lists, counts),
                (noise, *packs[level - 1], *(ref for ref, _ in known), *earlier, *waits),
                out_spec=ANY if final else VMEM,
                flops=nodes * (draws * width + 1) * dot_flops,
            )
            solved.append(here)
            sends += sent
            waits = packs[level] if at == 0 and level < last_level else []
        done.append(solved)
    return here


def solution(mesh):
    placed = (
        P(None, "leaf", None, "draw"),
        P(None, "leaf", "draw", None),
        P(None, "leaf", "draw", None, None),
        P(),
        P(None, "leaf", None),
        P(None, "leaf"),
    )
    return jax.shard_map(
        functools.partial(on_device, mesh.shape["leaf"], mesh.shape["draw"]),
        mesh=mesh,
        in_specs=placed,
        out_specs=P(None, "leaf", None, "draw"),
        check_vma=False,
    )
```

```python
import functools

import jax
import jax.numpy as jnp
from jax import lax
from jax.experimental import pallas as pl
from jax.experimental.pallas import tpu as pltpu
from jax.sharding import PartitionSpec as P

CHUNKS = 2
VMEM = pl.BlockSpec(memory_space=pltpu.VMEM)
SMEM = pl.BlockSpec(memory_space=pltpu.SMEM)
ANY = pl.BlockSpec(memory_space=pl.ANY)
BF16, F32 = jnp.bfloat16, jnp.float32


def hop(value, axis, size, step):
    return lax.ppermute(value, axis, [(at, at ^ step) for at in range(size)])


def gather_parts(value, axis, size):
    parts = {0: value}
    step = size // 2
    while step:
        for have in sorted(parts):
            parts[have ^ step] = hop(parts[have], axis, size, step)
        step //= 2
    return [parts[at] for at in range(size)]


def transposed_dot(left, right):
    return lax.dot_general(left, right, (((0,), (0,)), ((), ())), preferred_element_type=F32)


def take(refs, count):
    return list(refs[:count]), list(refs[count:])


def call(kernel, outs, scratch, small, arrays, out_spec=VMEM, flops=0):
    size = sum(value.size * value.dtype.itemsize for value in (*arrays, *outs))
    return pl.pallas_call(
        kernel,
        out_shape=outs,
        in_specs=[SMEM] * len(small) + [VMEM] * len(arrays),
        out_specs=[out_spec] * len(outs),
        scratch_shapes=scratch,
        cost_estimate=pl.CostEstimate(flops=flops, bytes_accessed=size, transcendentals=0),
        compiler_params=pltpu.CompilerParams(vmem_limit_bytes=16 * 1024 * 1024),
    )(*small, *arrays)


def write_pack(target, level, inverse, coupling):
    nodes, width, depth = coupling.shape[1:4]
    rows = inverse.shape[2]
    for node in range(nodes):
        for offset in range(width):
            at = (node * width + offset) * depth
            target[at:at + depth, :] = coupling[level - 1, node, offset]
        at = nodes * width * depth + node * rows
        target[at:at + rows, :] = inverse[level, node]


def first_kernel(chunks, draws, picks, noise, *refs):
    *refs, inv = refs
    parts, refs = take(refs, draws)
    solved, sends = take(refs, chunks)
    myself, draw = lax.axis_index("leaf"), lax.axis_index("draw")
    nodes, rows = parts[0].shape[:2]
    wide = solved[0].shape[-1]
    for step, part in enumerate(parts):
        inv[:, pl.ds(pl.multiple_of((draw ^ step) * rows, rows), rows), :] = part[...]
    for at, target in enumerate(solved):
        for node in range(nodes):
            right = noise[0, node, :, at * wide:(at + 1) * wide]
            target[node] = transposed_dot(inv[node], right).astype(BF16)
    for step, send in enumerate(sends, 1):
        node = picks[0, myself ^ step, myself]
        for at, target in enumerate(solved):
            send[at] = target[node]


def relay_kernel(owners, source, follow, pack_level, waits, picks, far, *refs):
    half = owners // 2
    if pack_level:
        inverse, coupling, *refs = refs
    own, refs = take(refs, follow)
    _, refs = take(refs, waits)
    sends, refs = take(refs, half - 1)
    myself = lax.axis_index("leaf")
    for step, send in enumerate(sends, 1):
        send[0] = far[picks[source, myself ^ step, myself ^ half]]
        if own:
            send[1] = own[0][picks[source, myself ^ step, myself]]
    if pack_level:
        write_pack(refs[0], pack_level, inverse, coupling)


def level_kernel(
    level, owners, draws, width, chunk, places, sides, earlier, waits,
    picks, lists, counts, noise, *refs,
):
    half = owners // 2
    packs, refs = take(refs, draws)
    known, refs = take(refs, level * owners)
    done, refs = take(refs, earlier)
    _, refs = take(refs, waits)
    target, *refs = refs
    sends, (table, inv, *refs) = take(refs, sides)
    myself, draw = lax.axis_index("leaf"), lax.axis_index("draw")
    nodes, wide = noise.shape[1], table.shape[-1]
    depth = inv.shape[1]
    rows = depth // draws
    copies = []
    solved = target
    if earlier:
        solved, sems = refs
        per_level = (earlier + 1) // (level + 1)
        for at, ref in enumerate(done):
            here = target.at[at // per_level, :, :, pl.ds(at % per_level * wide, wide)]
            copies.append(pltpu.make_async_copy(ref, here, sems.at[at]))
            copies[-1].start()
    for at, (ref, place) in enumerate(zip(known, places, strict=True)):
        step = at % owners
        if step % half == 0:
            place = picks[at // owners, myself, myself ^ step]
        table[at] = ref[place]
    empty = level * owners
    table[empty] = jnp.zeros_like(table[empty])
    for step, pack in enumerate(packs):
        start = pl.multiple_of((draw ^ step) * rows, rows)
        for node in range(nodes):
            at = nodes * width * depth + node * rows
            inv[node, pl.ds(start, rows), :] = pack[at:at + rows, :]
    for node in range(nodes):
        total = None
        for step, pack in enumerate(packs):
            for offset in range(width):
                slot = (draw ^ step) * width + offset
                live = slot < counts[level - 1, node]
                entry = jnp.where(live, lists[level - 1, node, slot] ^ myself, empty)
                at = (node * width + offset) * depth
                term = transposed_dot(pack[at:at + depth, :], table[entry])
                total = term if total is None else total + term
        side = noise[level, node, :, chunk * wide:(chunk + 1) * wide].astype(F32) - total
        solved[node] = transposed_dot(inv[node], side.astype(BF16)).astype(BF16)
    for step, send in enumerate(sends, 1):
        send[0] = solved[picks[level, myself ^ step, myself]]
    if earlier:
        here = target.at[level, :, :, pl.ds(chunk * wide, wide)]
        copies.append(pltpu.make_async_copy(solved, here, sems.at[earlier]))
        copies[-1].start()
    for copy in copies:
        copy.wait()


def on_device(owners, draws, noise, inverse, coupling, picks, lists, counts):
    levels, nodes, rows, columns = noise.shape
    wide, half, chunks = columns // CHUNKS, owners // 2, range(CHUNKS)
    width, last_level = coupling.shape[2], levels - 1
    shape = lambda *dims: jax.ShapeDtypeStruct(dims, BF16)
    part = shape(nodes, rows, wide)
    pack_shape = shape(nodes * (width * rows + inverse.shape[2]), rows)
    leaf = lambda value, step: hop(value, "leaf", owners, step)
    near = lambda values: [leaf(value, step) for step, value in enumerate(values, 1)]
    gather = lambda value: gather_parts(value, "draw", draws)
    inv_here = pltpu.VMEM((nodes, rows, rows), BF16)
    dot_flops = 2 * rows * rows * wide

    refs = call(
        functools.partial(first_kernel, CHUNKS, draws),
        [part] * CHUNKS + [shape(CHUNKS, rows, wide)] * (half - 1),
        [inv_here],
        (picks,),
        (noise, *gather(inverse[0])),
        flops=nodes * CHUNKS * dot_flops,
    )
    solved, sends = take(refs, CHUNKS)
    packs = [gather(jnp.concatenate([coupling[0].reshape(-1, rows), inverse[1].reshape(-1, rows)]))]
    done, pieces = [solved], []
    for level in range(1, levels):
        source = level - 1
        far = [leaf(value, half) for value in solved]
        got = near(sends)
        close = [[(ref, at) for ref in got] for at in chunks] if source == 0 else [[(ref, 0) for ref in got]]
        distant, waits = [], packs[source] + got if source == 0 else got
        for at in chunks:
            follow = source > 0 and at < CHUNKS - 1
            pack_level = source + 2 if at == 0 and source + 2 < levels else 0
            sends = list(call(
                functools.partial(relay_kernel, owners, source, int(follow), pack_level, len(waits)),
                [shape(1 + follow, rows, wide)] * (half - 1) + [pack_shape] * bool(pack_level),
                [],
                (picks,),
                (
                    far[at], *((inverse, coupling) if pack_level else ()),
                    *([solved[at + 1]] if follow else []), *waits,
                ),
            ))
            if pack_level:
                packs.append(gather(sends.pop()))
            got = near(sends)
            distant.append([(ref, 0) for ref in got])
            if follow:
                close.append([(ref, 1) for ref in got])
            waits = []
        pieces.append([
            [(solved[at], 0), *close[at], (far[at], 0), *distant[at]] for at in chunks
        ])
        waits = sends[:1]
        solved, sends = [], []
        for at in chunks:
            sides = half - 1 if at == 0 and level < last_level else 0
            final = level == last_level and at == CHUNKS - 1
            earlier = [value for values in done for value in values] + solved if final else []
            known = [entry for below in range(level) for entry in pieces[below][at]]
            scratch = [pltpu.VMEM((level * owners + 1, rows, wide), BF16), inv_here]
            if final:
                scratch += [
                    pltpu.VMEM((nodes, rows, wide), BF16),
                    pltpu.SemaphoreType.DMA((len(earlier) + 1,)),
                ]
            here, *sent = call(
                functools.partial(
                    level_kernel, level, owners, draws, width, at,
                    [place for _, place in known], sides, len(earlier), len(waits),
                ),
                [shape(levels, nodes, rows, columns) if final else part]
                + [shape(1, rows, wide)] * sides,
                scratch,
                (picks, lists, counts),
                (noise, *packs[level - 1], *(ref for ref, _ in known), *earlier, *waits),
                out_spec=ANY if final else VMEM,
                flops=nodes * (draws * width + 1) * dot_flops,
            )
            solved.append(here)
            sends += sent
            waits = packs[level] if at == 0 and level < last_level else []
        done.append(solved)
    return here


def solution(mesh):
    placed = (
        P(None, "leaf", None, "draw"),
        P(None, "leaf", "draw", None),
        P(None, "leaf", "draw", None, None),
        P(),
        P(None, "leaf", None),
        P(None, "leaf"),
    )
    return jax.shard_map(
        functools.partial(on_device, mesh.shape["leaf"], mesh.shape["draw"]),
        mesh=mesh,
        in_specs=placed,
        out_specs=P(None, "leaf", None, "draw"),
        check_vma=False,
    )
```

```python
import functools

import jax
import jax.numpy as jnp
from jax import lax
from jax.experimental import pallas as pl
from jax.experimental.pallas import tpu as pltpu
from jax.sharding import PartitionSpec as P

CHUNKS = 2
VMEM = pl.BlockSpec(memory_space=pltpu.VMEM)
SMEM = pl.BlockSpec(memory_space=pltpu.SMEM)
ANY = pl.BlockSpec(memory_space=pl.ANY)
BF16, F32 = jnp.bfloat16, jnp.float32


def hop(value, axis, size, step):
    return lax.ppermute(value, axis, [(at, at ^ step) for at in range(size)])


def gather_parts(value, axis, size):
    parts = {0: value}
    step = size // 2
    while step:
        for have in sorted(parts):
            parts[have ^ step] = hop(parts[have], axis, size, step)
        step //= 2
    return [parts[at] for at in range(size)]


def transposed_dot(left, right):
    return lax.dot_general(left, right, (((0,), (0,)), ((), ())), preferred_element_type=F32)


def take(refs, count):
    return list(refs[:count]), list(refs[count:])


def call(kernel, outs, scratch, small, arrays, out_spec=VMEM, flops=0):
    size = sum(value.size * value.dtype.itemsize for value in (*arrays, *outs))
    return pl.pallas_call(
        kernel,
        out_shape=outs,
        in_specs=[SMEM] * len(small) + [VMEM] * len(arrays),
        out_specs=[out_spec] * len(outs),
        scratch_shapes=scratch,
        cost_estimate=pl.CostEstimate(flops=flops, bytes_accessed=size, transcendentals=0),
        compiler_params=pltpu.CompilerParams(vmem_limit_bytes=16 * 1024 * 1024),
    )(*small, *arrays)


def write_pack(target, level, inverse, coupling):
    nodes, width, depth = coupling.shape[1:4]
    rows = inverse.shape[2]
    for node in range(nodes):
        for offset in range(width):
            at = (node * width + offset) * depth
            target[at:at + depth, :] = coupling[level - 1, node, offset]
        at = nodes * width * depth + node * rows
        target[at:at + rows, :] = inverse[level, node]


def first_kernel(chunks, draws, picks, noise, inverse, coupling, *refs):
    *refs, pack, inv = refs
    parts, refs = take(refs, draws)
    solved, sends = take(refs, chunks)
    myself, draw = lax.axis_index("leaf"), lax.axis_index("draw")
    nodes, rows = parts[0].shape[:2]
    wide = solved[0].shape[-1]
    for step, part in enumerate(parts):
        inv[:, pl.ds(pl.multiple_of((draw ^ step) * rows, rows), rows), :] = part[...]
    for at, target in enumerate(solved):
        for node in range(nodes):
            right = noise[0, node, :, at * wide:(at + 1) * wide]
            target[node] = transposed_dot(inv[node], right).astype(BF16)
    for step, send in enumerate(sends, 1):
        node = picks[0, myself ^ step, myself]
        for at, target in enumerate(solved):
            send[at] = target[node]
    write_pack(pack, 1, inverse, coupling)


def relay_kernel(owners, source, follow, waits, picks, far, *refs):
    half = owners // 2
    own, refs = take(refs, follow)
    sends = refs[waits:]
    myself = lax.axis_index("leaf")
    for step, send in enumerate(sends, 1):
        send[0] = far[picks[source, myself ^ step, myself ^ half]]
        if own:
            send[1] = own[0][picks[source, myself ^ step, myself]]


def level_kernel(
    level, owners, draws, width, chunk, places, sides, earlier, waits, packing,
    picks, lists, counts, noise, *refs,
):
    half = owners // 2
    packs, refs = take(refs, draws)
    known, refs = take(refs, level * owners)
    done, refs = take(refs, earlier)
    _, refs = take(refs, waits)
    if packing:
        inverse, coupling, *refs = refs
    target, *refs = refs
    sends, refs = take(refs, sides)
    if packing:
        write_pack(refs[0], level + 1, inverse, coupling)
        refs = refs[1:]
    table, inv, *refs = refs
    myself, draw = lax.axis_index("leaf"), lax.axis_index("draw")
    nodes, wide = noise.shape[1], table.shape[-1]
    depth = inv.shape[1]
    rows = depth // draws
    copies = []
    solved = target
    if earlier:
        solved, sems = refs
        per_level = (earlier + 1) // (level + 1)
        for at, ref in enumerate(done):
            here = target.at[at // per_level, :, :, pl.ds(at % per_level * wide, wide)]
            copies.append(pltpu.make_async_copy(ref, here, sems.at[at]))
            copies[-1].start()
    for at, (ref, place) in enumerate(zip(known, places, strict=True)):
        step = at % owners
        if step % half == 0:
            place = picks[at // owners, myself, myself ^ step]
        table[at] = ref[place]
    empty = level * owners
    table[empty] = jnp.zeros_like(table[empty])
    for step, pack in enumerate(packs):
        start = pl.multiple_of((draw ^ step) * rows, rows)
        for node in range(nodes):
            at = nodes * width * depth + node * rows
            inv[node, pl.ds(start, rows), :] = pack[at:at + rows, :]
    for node in range(nodes):
        total = None
        for step, pack in enumerate(packs):
            for offset in range(width):
                slot = (draw ^ step) * width + offset
                live = slot < counts[level - 1, node]
                entry = jnp.where(live, lists[level - 1, node, slot] ^ myself, empty)
                at = (node * width + offset) * depth
                term = transposed_dot(pack[at:at + depth, :], table[entry])
                total = term if total is None else total + term
        side = noise[level, node, :, chunk * wide:(chunk + 1) * wide].astype(F32) - total
        solved[node] = transposed_dot(inv[node], side.astype(BF16)).astype(BF16)
    for step, send in enumerate(sends, 1):
        send[0] = solved[picks[level, myself ^ step, myself]]
    if earlier:
        here = target.at[level, :, :, pl.ds(chunk * wide, wide)]
        copies.append(pltpu.make_async_copy(solved, here, sems.at[earlier]))
        copies[-1].start()
    for copy in copies:
        copy.wait()


def on_device(owners, draws, noise, inverse, coupling, picks, lists, counts):
    levels, nodes, rows, columns = noise.shape
    wide, half, chunks = columns // CHUNKS, owners // 2, range(CHUNKS)
    width, last_level = coupling.shape[2], levels - 1
    shape = lambda *dims: jax.ShapeDtypeStruct(dims, BF16)
    part = shape(nodes, rows, wide)
    pack_shape = shape(nodes * (width * rows + inverse.shape[2]), rows)
    leaf = lambda value, step: hop(value, "leaf", owners, step)
    near = lambda values: [leaf(value, step) for step, value in enumerate(values, 1)]
    gather = lambda value: gather_parts(value, "draw", draws)
    inv_here = pltpu.VMEM((nodes, rows, rows), BF16)
    dot_flops = 2 * rows * rows * wide

    *refs, pack = call(
        functools.partial(first_kernel, CHUNKS, draws),
        [part] * CHUNKS + [shape(CHUNKS, rows, wide)] * (half - 1) + [pack_shape],
        [inv_here],
        (picks,),
        (noise, inverse, coupling, *gather(inverse[0])),
        flops=nodes * CHUNKS * dot_flops,
    )
    solved, sends = take(refs, CHUNKS)
    packs = [gather(pack)]
    done, pieces = [solved], []
    for level in range(1, levels):
        source = level - 1
        far = [leaf(value, half) for value in solved]
        got = near(sends)
        close = [[(ref, at) for ref in got] for at in chunks] if source == 0 else [[(ref, 0) for ref in got]]
        distant, waits = [], got
        for at in chunks:
            follow = source > 0 and at < CHUNKS - 1
            sends = call(
                functools.partial(relay_kernel, owners, source, int(follow), len(waits)),
                [shape(1 + follow, rows, wide)] * (half - 1),
                [],
                (picks,),
                (far[at], *([solved[at + 1]] if follow else []), *waits),
            )
            got = near(sends)
            distant.append([(ref, 0) for ref in got])
            if follow:
                close.append([(ref, 1) for ref in got])
            waits = packs[source]
        pieces.append([
            [(solved[at], 0), *close[at], (far[at], 0), *distant[at]] for at in chunks
        ])
        waits = sends[:1]
        solved, sends = [], []
        for at in chunks:
            packing = at == 0 and level < last_level
            sides = half - 1 if packing else 0
            final = level == last_level and at == CHUNKS - 1
            earlier = [value for values in done for value in values] + solved if final else []
            known = [entry for below in range(level) for entry in pieces[below][at]]
            scratch = [pltpu.VMEM((level * owners + 1, rows, wide), BF16), inv_here]
            if final:
                scratch += [
                    pltpu.VMEM((nodes, rows, wide), BF16),
                    pltpu.SemaphoreType.DMA((len(earlier) + 1,)),
                ]
            here, *sent = call(
                functools.partial(
                    level_kernel, level, owners, draws, width, at,
                    [place for _, place in known], sides, len(earlier), len(waits), packing,
                ),
                [shape(levels, nodes, rows, columns) if final else part]
                + [shape(1, rows, wide)] * sides + [pack_shape] * packing,
                scratch,
                (picks, lists, counts),
                (noise, *packs[level - 1], *(ref for ref, _ in known), *earlier, *waits)
                + ((inverse, coupling) if packing else ()),
                out_spec=ANY if final else VMEM,
                flops=nodes * (draws * width + 1) * dot_flops,
            )
            solved.append(here)
            if packing:
                packs.append(gather(sent.pop()))
            sends += sent
            waits = []
        done.append(solved)
    return here


def solution(mesh):
    placed = (
        P(None, "leaf", None, "draw"),
        P(None, "leaf", "draw", None),
        P(None, "leaf", "draw", None, None),
        P(),
        P(None, "leaf", None),
        P(None, "leaf"),
    )
    return jax.shard_map(
        functools.partial(on_device, mesh.shape["leaf"], mesh.shape["draw"]),
        mesh=mesh,
        in_specs=placed,
        out_specs=P(None, "leaf", None, "draw"),
        check_vma=False,
    )
```

```python
import functools

import jax
import jax.numpy as jnp
from jax import lax
from jax.experimental import pallas as pl
from jax.experimental.pallas import tpu as pltpu
from jax.sharding import PartitionSpec as P

CHUNKS = 1
VMEM = pl.BlockSpec(memory_space=pltpu.VMEM)
SMEM = pl.BlockSpec(memory_space=pltpu.SMEM)
ANY = pl.BlockSpec(memory_space=pl.ANY)
BF16, F32 = jnp.bfloat16, jnp.float32


def hop(value, axis, size, step):
    return lax.ppermute(value, axis, [(at, at ^ step) for at in range(size)])


def gather_rows(value, axis, size):
    steps, step = [0], size // 2
    while step:
        other, others = hop(value, axis, size, step), [have ^ step for have in steps]
        if step == 1:
            return [value, other], [steps, others]
        value, steps = jnp.concatenate([value, other]), steps + others
        step //= 2
    return [value], [steps]


def transposed_dot(left, right):
    return lax.dot_general(left, right, (((0,), (0,)), ((), ())), preferred_element_type=F32)


def take(refs, count):
    return list(refs[:count]), list(refs[count:])


def call(kernel, outs, scratch, small, arrays, out_spec=VMEM, flops=0, aliases={}):
    size = sum(value.size * value.dtype.itemsize for value in (*arrays, *outs))
    return pl.pallas_call(
        kernel,
        out_shape=outs,
        in_specs=[SMEM] * len(small) + [VMEM] * len(arrays),
        out_specs=[out_spec] * len(outs),
        scratch_shapes=scratch,
        input_output_aliases=aliases,
        cost_estimate=pl.CostEstimate(flops=flops, bytes_accessed=size, transcendentals=0),
        compiler_params=pltpu.CompilerParams(vmem_limit_bytes=16 * 1024 * 1024),
    )(*small, *arrays)


def row_blocks(refs, steps, block):
    return [
        (ref, at * block, step)
        for ref, held in zip(refs, steps, strict=True) for at, step in enumerate(held)
    ]


def fill_inverse(target, found, offset, rows, draw):
    for ref, at, step in found:
        start = pl.multiple_of((draw ^ step) * rows, rows)
        for node in range(target.shape[0]):
            first = at + offset + node * rows
            target[node, pl.ds(start, rows), :] = ref[first:first + rows, :]


def first_kernel(chunks, steps, picks, noise, *refs):
    *refs, _, inv = refs
    parts, refs = take(refs, len(steps))
    solved, sends = take(refs[1:], chunks)
    myself, draw = lax.axis_index("leaf"), lax.axis_index("draw")
    nodes, wide = noise.shape[0], solved[0].shape[-1]
    draws = sum(map(len, steps))
    rows = inv.shape[1] // draws
    fill_inverse(inv, row_blocks(parts, steps, nodes * rows), 0, rows, draw)
    for at, target in enumerate(solved):
        for node in range(nodes):
            right = noise[node, :, at * wide:(at + 1) * wide]
            target[node] = transposed_dot(inv[node], right).astype(BF16)
    for step, send in enumerate(sends, 1):
        node = picks[0, myself ^ step, myself]
        for at, target in enumerate(solved):
            send[at] = target[node]


def relay_kernel(owners, source, follow, waits, picks, far, *refs):
    half = owners // 2
    own, refs = take(refs, follow)
    sends = refs[waits:]
    myself = lax.axis_index("leaf")
    for step, send in enumerate(sends, 1):
        send[0] = far[picks[source, myself ^ step, myself ^ half]]
        if own:
            send[1] = own[0][picks[source, myself ^ step, myself]]


def level_kernel(
    level, owners, steps, width, chunk, places, sides, earlier, waits, packing,
    picks, lists, counts, noise, *refs,
):
    half = owners // 2
    packs, refs = take(refs, len(steps))
    known, refs = take(refs, level * owners)
    done, refs = take(refs, earlier)
    _, refs = take(refs, waits)
    if packing:
        refs = refs[1:]
    target, *refs = refs
    sends, refs = take(refs, sides)
    if packing:
        refs = refs[1:]
    table, inv, *refs = refs
    myself, draw = lax.axis_index("leaf"), lax.axis_index("draw")
    nodes, wide = noise.shape[1], table.shape[-1]
    depth = inv.shape[1]
    rows = depth // sum(map(len, steps))
    found = row_blocks(packs, steps, nodes * (width * depth + rows))
    copies = []
    solved = target
    if earlier:
        solved, sems = refs
        per_level = (earlier + 1) // (level + 1)
        for at, ref in enumerate(done):
            here = target.at[at // per_level, :, :, pl.ds(at % per_level * wide, wide)]
            copies.append(pltpu.make_async_copy(ref, here, sems.at[at]))
            copies[-1].start()
    for at, (ref, place) in enumerate(zip(known, places, strict=True)):
        step = at % owners
        if step % half == 0:
            place = picks[at // owners, myself, myself ^ step]
        table[at] = ref[place]
    empty = level * owners
    table[empty] = jnp.zeros_like(table[empty])
    fill_inverse(inv, found, nodes * width * depth, rows, draw)
    for node in range(nodes):
        total = None
        for pack, start, step in found:
            for offset in range(width):
                slot = (draw ^ step) * width + offset
                live = slot < counts[level - 1, node]
                entry = jnp.where(live, lists[level - 1, node, slot] ^ myself, empty)
                at = start + (node * width + offset) * depth
                term = transposed_dot(pack[at:at + depth, :], table[entry])
                total = term if total is None else total + term
        side = noise[level, node, :, chunk * wide:(chunk + 1) * wide].astype(F32) - total
        solved[node] = transposed_dot(inv[node], side.astype(BF16)).astype(BF16)
    for step, send in enumerate(sends, 1):
        send[0] = solved[picks[level, myself ^ step, myself]]
    if earlier:
        here = target.at[level, :, :, pl.ds(chunk * wide, wide)]
        copies.append(pltpu.make_async_copy(solved, here, sems.at[earlier]))
        copies[-1].start()
    for copy in copies:
        copy.wait()


def on_device(owners, draws, noise, inverse, coupling, picks, lists, counts):
    levels, nodes, rows, columns = noise.shape
    wide, half, chunks = columns // CHUNKS, owners // 2, range(CHUNKS)
    width, last_level = coupling.shape[2], levels - 1
    shape = lambda *dims: jax.ShapeDtypeStruct(dims, BF16)
    part = shape(nodes, rows, wide)
    flat = lambda value: value.reshape(-1, rows)
    raw = [
        jnp.concatenate([flat(coupling[level - 1]), flat(inverse[level])])
        for level in range(1, levels)
    ]
    pack_shape = shape(*raw[0].shape)
    leaf = lambda value, step: hop(value, "leaf", owners, step)
    near = lambda values: [leaf(value, step) for step, value in enumerate(values, 1)]
    gather = lambda value: gather_rows(value, "draw", draws)
    inv_here = pltpu.VMEM((nodes, rows, rows), BF16)
    dot_flops = 2 * rows * rows * wide

    parts, steps = gather(flat(inverse[0]))
    *refs, pack = call(
        functools.partial(first_kernel, CHUNKS, steps),
        [part] * CHUNKS + [shape(CHUNKS, rows, wide)] * (half - 1) + [pack_shape],
        [inv_here],
        (picks,),
        (noise[0], *parts, raw[0]),
        flops=nodes * CHUNKS * dot_flops,
        aliases={2 + len(parts): CHUNKS + half - 1},
    )
    solved, sends = take(refs, CHUNKS)
    packs = [gather(pack)[0]]
    done, pieces = [solved], []
    for level in range(1, levels):
        source = level - 1
        far = [leaf(value, half) for value in solved]
        got = near(sends)
        close = [[(ref, at) for ref in got] for at in chunks] if source == 0 else [[(ref, 0) for ref in got]]
        distant, waits = [], got + packs[source][:1]
        for at in chunks:
            follow = source > 0 and at < CHUNKS - 1
            sends = call(
                functools.partial(relay_kernel, owners, source, int(follow), len(waits)),
                [shape(1 + follow, rows, wide)] * (half - 1),
                [],
                (picks,),
                (far[at], *([solved[at + 1]] if follow else []), *waits),
            )
            got = near(sends)
            distant.append([(ref, 0) for ref in got])
            if follow:
                close.append([(ref, 1) for ref in got])
            waits = []
        pieces.append([
            [(solved[at], 0), *close[at], (far[at], 0), *distant[at]] for at in chunks
        ])
        waits = sends[:1]
        solved, sends = [], []
        for at in chunks:
            packing = at == 0 and level < last_level
            sides = half - 1 if packing else 0
            final = level == last_level and at == CHUNKS - 1
            earlier = [value for values in done for value in values] + solved if final else []
            known = [entry for below in range(level) for entry in pieces[below][at]]
            scratch = [pltpu.VMEM((level * owners + 1, rows, wide), BF16), inv_here]
            if final:
                scratch += [
                    pltpu.VMEM((nodes, rows, wide), BF16),
                    pltpu.SemaphoreType.DMA((len(earlier) + 1,)),
                ]
            here, *sent = call(
                functools.partial(
                    level_kernel, level, owners, steps, width, at,
                    [place for _, place in known], sides, len(earlier), len(waits), packing,
                ),
                [shape(levels, nodes, rows, columns) if final else part]
                + [shape(1, rows, wide)] * sides + [pack_shape] * packing,
                scratch,
                (picks, lists, counts),
                (noise, *packs[level - 1], *(ref for ref, _ in known), *earlier, *waits)
                + ((raw[level],) if packing else ()),
                out_spec=ANY if final else VMEM,
                aliases={
                    4 + len(packs[level - 1]) + len(known) + len(earlier) + len(waits): 1 + sides
                } if packing else {},
                flops=nodes * (draws * width + 1) * dot_flops,
            )
            solved.append(here)
            if packing:
                packs.append(gather(sent.pop())[0])
            sends += sent
            waits = []
        done.append(solved)
    return here


def solution(mesh):
    placed = (
        P(None, "leaf", None, "draw"),
        P(None, "leaf", "draw", None),
        P(None, "leaf", "draw", None, None),
        P(),
        P(None, "leaf", None),
        P(None, "leaf"),
    )
    return jax.shard_map(
        functools.partial(on_device, mesh.shape["leaf"], mesh.shape["draw"]),
        mesh=mesh,
        in_specs=placed,
        out_specs=P(None, "leaf", None, "draw"),
        check_vma=False,
    )
```

```python
import functools

import jax
import jax.numpy as jnp
from jax import lax
from jax.experimental import pallas as pl
from jax.experimental.pallas import tpu as pltpu
from jax.sharding import PartitionSpec as P

CHUNKS = 1
VMEM = pl.BlockSpec(memory_space=pltpu.VMEM)
SMEM = pl.BlockSpec(memory_space=pltpu.SMEM)
ANY = pl.BlockSpec(memory_space=pl.ANY)
BF16, F32 = jnp.bfloat16, jnp.float32


def hop(value, axis, size, step):
    return lax.ppermute(value, axis, [(at, at ^ step) for at in range(size)])


def far_rows(value, axis, size):
    steps, step, other = [0], size // 2, None
    while step > 1:
        value = value if other is None else jnp.concatenate([value, other])
        other = hop(value, axis, size, step)
        steps = steps + [have ^ step for have in steps]
        step //= 2
    return [value] if other is None else [value, other], steps


def near_rows(value, steps, axis, size):
    return [value, hop(value, axis, size, 1)], [steps, [have ^ 1 for have in steps]]


def transposed_dot(left, right):
    return lax.dot_general(left, right, (((0,), (0,)), ((), ())), preferred_element_type=F32)


def take(refs, count):
    return list(refs[:count]), list(refs[count:])


def call(kernel, outs, scratch, small, arrays, out_spec=VMEM, flops=0, aliases={}):
    size = sum(value.size * value.dtype.itemsize for value in (*arrays, *outs))
    return pl.pallas_call(
        kernel,
        out_shape=outs,
        in_specs=[SMEM] * len(small) + [VMEM] * len(arrays),
        out_specs=[out_spec] * len(outs),
        scratch_shapes=scratch,
        input_output_aliases=aliases,
        cost_estimate=pl.CostEstimate(flops=flops, bytes_accessed=size, transcendentals=0),
        compiler_params=pltpu.CompilerParams(vmem_limit_bytes=16 * 1024 * 1024),
    )(*small, *arrays)


def row_blocks(refs, steps, block):
    return [
        (ref, at * block, step)
        for ref, held in zip(refs, steps, strict=True) for at, step in enumerate(held)
    ]


def fill_inverse(target, found, offset, rows, draw):
    for ref, at, step in found:
        start = pl.multiple_of((draw ^ step) * rows, rows)
        for node in range(target.shape[0]):
            first = at + offset + node * rows
            target[node, pl.ds(start, rows), :] = ref[first:first + rows, :]


def first_kernel(chunks, steps, picks, noise, *refs):
    *refs, _, inv = refs
    parts, refs = take(refs, len(steps))
    solved, sends = take(refs[1:], chunks)
    myself, draw = lax.axis_index("leaf"), lax.axis_index("draw")
    nodes, wide = noise.shape[0], solved[0].shape[-1]
    draws = sum(map(len, steps))
    rows = inv.shape[1] // draws
    fill_inverse(inv, row_blocks(parts, steps, nodes * rows), 0, rows, draw)
    for at, target in enumerate(solved):
        for node in range(nodes):
            right = noise[node, :, at * wide:(at + 1) * wide]
            target[node] = transposed_dot(inv[node], right).astype(BF16)
    for step, send in enumerate(sends, 1):
        node = picks[0, myself ^ step, myself]
        for at, target in enumerate(solved):
            send[at] = target[node]


def relay_kernel(owners, source, follow, waits, joined, picks, far, *refs):
    half = owners // 2
    own, refs = take(refs, follow)
    _, refs = take(refs, waits)
    parts, refs = take(refs, joined)
    sends, joint = take(refs, half - 1)
    myself = lax.axis_index("leaf")
    for step, send in enumerate(sends, 1):
        send[0] = far[picks[source, myself ^ step, myself ^ half]]
        if own:
            send[1] = own[0][picks[source, myself ^ step, myself]]
    at = 0
    for part in parts:
        joint[0][at:at + part.shape[0], :] = part[...]
        at += part.shape[0]


def level_kernel(
    level, owners, steps, width, chunk, places, sides, earlier, waits, packing,
    picks, lists, counts, noise, *refs,
):
    half = owners // 2
    packs, refs = take(refs, len(steps))
    known, refs = take(refs, level * owners)
    done, refs = take(refs, earlier)
    _, refs = take(refs, waits)
    if packing:
        refs = refs[1:]
    target, *refs = refs
    sends, refs = take(refs, sides)
    if packing:
        refs = refs[1:]
    table, inv, *refs = refs
    myself, draw = lax.axis_index("leaf"), lax.axis_index("draw")
    nodes, wide = noise.shape[1], table.shape[-1]
    depth = inv.shape[1]
    rows = depth // sum(map(len, steps))
    found = row_blocks(packs, steps, nodes * (width * depth + rows))
    copies = []
    solved = target
    if earlier:
        solved, sems = refs
        per_level = (earlier + 1) // (level + 1)
        for at, ref in enumerate(done):
            here = target.at[at // per_level, :, :, pl.ds(at % per_level * wide, wide)]
            copies.append(pltpu.make_async_copy(ref, here, sems.at[at]))
            copies[-1].start()
    for at, (ref, place) in enumerate(zip(known, places, strict=True)):
        step = at % owners
        if step % half == 0:
            place = picks[at // owners, myself, myself ^ step]
        table[at] = ref[place]
    empty = level * owners
    table[empty] = jnp.zeros_like(table[empty])
    fill_inverse(inv, found, nodes * width * depth, rows, draw)
    for node in range(nodes):
        total = None
        for pack, start, step in found:
            for offset in range(width):
                slot = (draw ^ step) * width + offset
                live = slot < counts[level - 1, node]
                entry = jnp.where(live, lists[level - 1, node, slot] ^ myself, empty)
                at = start + (node * width + offset) * depth
                term = transposed_dot(pack[at:at + depth, :], table[entry])
                total = term if total is None else total + term
        side = noise[level, node, :, chunk * wide:(chunk + 1) * wide].astype(F32) - total
        solved[node] = transposed_dot(inv[node], side.astype(BF16)).astype(BF16)
    for step, send in enumerate(sends, 1):
        send[0] = solved[picks[level, myself ^ step, myself]]
    if earlier:
        here = target.at[level, :, :, pl.ds(chunk * wide, wide)]
        copies.append(pltpu.make_async_copy(solved, here, sems.at[earlier]))
        copies[-1].start()
    for copy in copies:
        copy.wait()


def on_device(owners, draws, noise, inverse, coupling, picks, lists, counts):
    levels, nodes, rows, columns = noise.shape
    wide, half, chunks = columns // CHUNKS, owners // 2, range(CHUNKS)
    width, last_level = coupling.shape[2], levels - 1
    shape = lambda *dims: jax.ShapeDtypeStruct(dims, BF16)
    part = shape(nodes, rows, wide)
    flat = lambda value: value.reshape(-1, rows)
    raw = [
        jnp.concatenate([flat(coupling[level - 1]), flat(inverse[level])])
        for level in range(1, levels)
    ]
    pack_shape = shape(*raw[0].shape)
    leaf = lambda value, step: hop(value, "leaf", owners, step)
    near = lambda values: [leaf(value, step) for step, value in enumerate(values, 1)]
    inv_here = pltpu.VMEM((nodes, rows, rows), BF16)
    dot_flops = 2 * rows * rows * wide

    parts, steps = far_rows(flat(inverse[0]), "draw", draws)
    parts, steps = near_rows(jnp.concatenate(parts), steps, "draw", draws)
    *refs, pack = call(
        functools.partial(first_kernel, CHUNKS, steps),
        [part] * CHUNKS + [shape(CHUNKS, rows, wide)] * (half - 1) + [pack_shape],
        [inv_here],
        (picks,),
        (noise[0], *parts, raw[0]),
        flops=nodes * CHUNKS * dot_flops,
        aliases={2 + len(parts): CHUNKS + half - 1},
    )
    solved, sends = take(refs, CHUNKS)
    packs = []
    done, pieces = [solved], []
    for level in range(1, levels):
        source = level - 1
        far = [leaf(value, half) for value in solved]
        got = near(sends)
        close = [[(ref, at) for ref in got] for at in chunks] if source == 0 else [[(ref, 0) for ref in got]]
        distant, waits = [], got
        joined, far_steps = far_rows(pack, "draw", draws)
        joint = sum(value.shape[0] for value in joined)
        for at in chunks:
            follow = source > 0 and at < CHUNKS - 1
            sends = call(
                functools.partial(relay_kernel, owners, source, int(follow), len(waits), len(joined)),
                [shape(1 + follow, rows, wide)] * (half - 1) + [shape(joint, rows)] * bool(joined),
                [],
                (picks,),
                (far[at], *([solved[at + 1]] if follow else []), *waits, *joined),
            )
            if joined:
                *sends, joint = sends
                packs.append(near_rows(joint, far_steps, "draw", draws)[0])
                joined = []
            got = near(sends)
            distant.append([(ref, 0) for ref in got])
            if follow:
                close.append([(ref, 1) for ref in got])
            waits = []
        pieces.append([
            [(solved[at], 0), *close[at], (far[at], 0), *distant[at]] for at in chunks
        ])
        waits = sends[:1]
        solved, sends = [], []
        for at in chunks:
            packing = at == 0 and level < last_level
            sides = half - 1 if packing else 0
            final = level == last_level and at == CHUNKS - 1
            earlier = [value for values in done for value in values] + solved if final else []
            known = [entry for below in range(level) for entry in pieces[below][at]]
            scratch = [pltpu.VMEM((level * owners + 1, rows, wide), BF16), inv_here]
            if final:
                scratch += [
                    pltpu.VMEM((nodes, rows, wide), BF16),
                    pltpu.SemaphoreType.DMA((len(earlier) + 1,)),
                ]
            here, *sent = call(
                functools.partial(
                    level_kernel, level, owners, steps, width, at,
                    [place for _, place in known], sides, len(earlier), len(waits), packing,
                ),
                [shape(levels, nodes, rows, columns) if final else part]
                + [shape(1, rows, wide)] * sides + [pack_shape] * packing,
                scratch,
                (picks, lists, counts),
                (noise, *packs[level - 1], *(ref for ref, _ in known), *earlier, *waits)
                + ((raw[level],) if packing else ()),
                out_spec=ANY if final else VMEM,
                aliases={
                    4 + len(packs[level - 1]) + len(known) + len(earlier) + len(waits): 1 + sides
                } if packing else {},
                flops=nodes * (draws * width + 1) * dot_flops,
            )
            solved.append(here)
            if packing:
                pack = sent.pop()
            sends += sent
            waits = []
        done.append(solved)
    return here


def solution(mesh):
    placed = (
        P(None, "leaf", None, "draw"),
        P(None, "leaf", "draw", None),
        P(None, "leaf", "draw", None, None),
        P(),
        P(None, "leaf", None),
        P(None, "leaf"),
    )
    return jax.shard_map(
        functools.partial(on_device, mesh.shape["leaf"], mesh.shape["draw"]),
        mesh=mesh,
        in_specs=placed,
        out_specs=P(None, "leaf", None, "draw"),
        check_vma=False,
    )
```

```python
import functools

import jax
import jax.numpy as jnp
from jax import lax
from jax.experimental import pallas as pl
from jax.experimental.pallas import tpu as pltpu
from jax.sharding import PartitionSpec as P

CHUNKS = 2
VMEM = pl.BlockSpec(memory_space=pltpu.VMEM)
SMEM = pl.BlockSpec(memory_space=pltpu.SMEM)
ANY = pl.BlockSpec(memory_space=pl.ANY)
BF16, F32 = jnp.bfloat16, jnp.float32


def hop(value, axis, size, step):
    return lax.ppermute(value, axis, [(at, at ^ step) for at in range(size)])


def far_rows(value, axis, size):
    steps, step, other = [0], size // 2, None
    while step > 1:
        value = value if other is None else jnp.concatenate([value, other])
        other = hop(value, axis, size, step)
        steps = steps + [have ^ step for have in steps]
        step //= 2
    return [value] if other is None else [value, other], steps


def near_rows(value, steps, axis, size):
    return [value, hop(value, axis, size, 1)], [steps, [have ^ 1 for have in steps]]


def transposed_dot(left, right):
    return lax.dot_general(left, right, (((0,), (0,)), ((), ())), preferred_element_type=F32)


def take(refs, count):
    return list(refs[:count]), list(refs[count:])


def call(kernel, outs, scratch, small, arrays, out_spec=VMEM, flops=0, aliases={}):
    size = sum(value.size * value.dtype.itemsize for value in (*arrays, *outs))
    return pl.pallas_call(
        kernel,
        out_shape=outs,
        in_specs=[SMEM] * len(small) + [VMEM] * len(arrays),
        out_specs=[out_spec] * len(outs),
        scratch_shapes=scratch,
        input_output_aliases=aliases,
        cost_estimate=pl.CostEstimate(flops=flops, bytes_accessed=size, transcendentals=0),
        compiler_params=pltpu.CompilerParams(vmem_limit_bytes=16 * 1024 * 1024),
    )(*small, *arrays)


def row_blocks(refs, steps, block):
    return [
        (ref, at * block, step)
        for ref, held in zip(refs, steps, strict=True) for at, step in enumerate(held)
    ]


def fill_inverse(target, found, offset, rows, draw):
    for ref, at, step in found:
        start = pl.multiple_of((draw ^ step) * rows, rows)
        for node in range(target.shape[0]):
            first = at + offset + node * rows
            target[node, pl.ds(start, rows), :] = ref[first:first + rows, :]


def first_kernel(steps, picks, noise, *refs):
    *refs, _, inv = refs
    parts, refs = take(refs, len(steps))
    solved, draw = refs[1:], lax.axis_index("draw")
    nodes, wide = noise.shape[0], solved[0].shape[-1]
    draws = sum(map(len, steps))
    rows = inv.shape[1] // draws
    fill_inverse(inv, row_blocks(parts, steps, nodes * rows), 0, rows, draw)
    for at, target in enumerate(solved):
        for node in range(nodes):
            right = noise[node, :, at * wide:(at + 1) * wide]
            target[node] = transposed_dot(inv[node], right).astype(BF16)


def relay_kernel(owners, source, joined, picks, own, far, *refs):
    half = owners // 2
    parts, refs = take(refs, joined)
    sends, joint = take(refs, half - 1)
    myself = lax.axis_index("leaf")
    for step, send in enumerate(sends, 1):
        send[0] = own[picks[source, myself ^ step, myself]]
        send[1] = far[picks[source, myself ^ step, myself ^ half]]
    at = 0
    for part in parts:
        joint[0][at:at + part.shape[0], :] = part[...]
        at += part.shape[0]


def level_kernel(
    level, owners, steps, width, chunk, places, earlier, packing,
    picks, lists, counts, noise, *refs,
):
    half = owners // 2
    packs, refs = take(refs, len(steps))
    known, refs = take(refs, level * owners)
    done, refs = take(refs, earlier)
    if packing:
        refs = refs[1:]
    target, *refs = refs
    if packing:
        refs = refs[1:]
    table, inv, *refs = refs
    myself, draw = lax.axis_index("leaf"), lax.axis_index("draw")
    nodes, wide = noise.shape[1], table.shape[-1]
    depth = inv.shape[1]
    rows = depth // sum(map(len, steps))
    found = row_blocks(packs, steps, nodes * (width * depth + rows))
    copies = []
    solved = target
    if earlier:
        solved, sems = refs
        per_level = (earlier + 1) // (level + 1)
        for at, ref in enumerate(done):
            here = target.at[at // per_level, :, :, pl.ds(at % per_level * wide, wide)]
            copies.append(pltpu.make_async_copy(ref, here, sems.at[at]))
            copies[-1].start()
    for at, (ref, place) in enumerate(zip(known, places, strict=True)):
        step = at % owners
        if step % half == 0:
            place = picks[at // owners, myself, myself ^ step]
        table[at] = ref[place]
    empty = level * owners
    table[empty] = jnp.zeros_like(table[empty])
    fill_inverse(inv, found, nodes * width * depth, rows, draw)
    for node in range(nodes):
        total = None
        for pack, start, step in found:
            for offset in range(width):
                slot = (draw ^ step) * width + offset
                live = slot < counts[level - 1, node]
                entry = jnp.where(live, lists[level - 1, node, slot] ^ myself, empty)
                at = start + (node * width + offset) * depth
                term = transposed_dot(pack[at:at + depth, :], table[entry])
                total = term if total is None else total + term
        side = noise[level, node, :, chunk * wide:(chunk + 1) * wide].astype(F32) - total
        solved[node] = transposed_dot(inv[node], side.astype(BF16)).astype(BF16)
    if earlier:
        here = target.at[level, :, :, pl.ds(chunk * wide, wide)]
        copies.append(pltpu.make_async_copy(solved, here, sems.at[earlier]))
        copies[-1].start()
    for copy in copies:
        copy.wait()


def on_device(owners, draws, noise, inverse, coupling, picks, lists, counts):
    levels, nodes, rows, columns = noise.shape
    wide, half, chunks = columns // CHUNKS, owners // 2, range(CHUNKS)
    width, last_level = coupling.shape[2], levels - 1
    shape = lambda *dims: jax.ShapeDtypeStruct(dims, BF16)
    part = shape(nodes, rows, wide)
    flat = lambda value: value.reshape(-1, rows)
    raw = [
        jnp.concatenate([flat(coupling[level - 1]), flat(inverse[level])])
        for level in range(1, levels)
    ]
    pack_shape = shape(*raw[0].shape)
    leaf = lambda value, step: hop(value, "leaf", owners, step)
    inv_here = pltpu.VMEM((nodes, rows, rows), BF16)
    dot_flops = 2 * rows * rows * wide

    parts, steps = far_rows(flat(inverse[0]), "draw", draws)
    parts, steps = near_rows(jnp.concatenate(parts), steps, "draw", draws)
    *solved, pack = call(
        functools.partial(first_kernel, steps),
        [part] * CHUNKS + [pack_shape],
        [inv_here],
        (picks,),
        (noise[0], *parts, raw[0]),
        flops=nodes * CHUNKS * dot_flops,
        aliases={2 + len(parts): CHUNKS},
    )
    packs, done, pieces = [], [], []
    for level in range(1, levels):
        source = level - 1
        done.append(solved)
        far = [leaf(value, half) for value in solved]
        joined, far_steps = far_rows(pack, "draw", draws)
        joint = shape(sum(value.shape[0] for value in joined), rows)
        pieces.append([])
        for at in chunks:
            joining = joined if at == 0 else []
            sends = call(
                functools.partial(relay_kernel, owners, source, len(joining)),
                [shape(2, rows, wide)] * (half - 1) + [joint] * bool(joining),
                [],
                (picks,),
                (solved[at], far[at], *joining),
            )
            if joining:
                *sends, pack = sends
                packs.append(near_rows(pack, far_steps, "draw", draws)[0])
            got = [leaf(value, step) for step, value in enumerate(sends, 1)]
            pieces[source].append([
                (solved[at], 0), *((ref, 0) for ref in got),
                (far[at], 0), *((ref, 1) for ref in got),
            ])
        solved = []
        for at in chunks:
            packing = at == 0 and level < last_level
            final = level == last_level and at == CHUNKS - 1
            earlier = [value for values in done for value in values] + solved if final else []
            known = [entry for below in range(level) for entry in pieces[below][at]]
            scratch = [pltpu.VMEM((level * owners + 1, rows, wide), BF16), inv_here]
            if final:
                scratch += [
                    pltpu.VMEM((nodes, rows, wide), BF16),
                    pltpu.SemaphoreType.DMA((len(earlier) + 1,)),
                ]
            here, *passed = call(
                functools.partial(
                    level_kernel, level, owners, steps, width, at,
                    [place for _, place in known], len(earlier), packing,
                ),
                [shape(levels, nodes, rows, columns) if final else part] + [pack_shape] * packing,
                scratch,
                (picks, lists, counts),
                (noise, *packs[level - 1], *(ref for ref, _ in known), *earlier)
                + ((raw[level],) if packing else ()),
                out_spec=ANY if final else VMEM,
                flops=nodes * (draws * width + 1) * dot_flops,
                aliases={4 + len(packs[level - 1]) + len(known) + len(earlier): 1} if packing else {},
            )
            solved.append(here)
            if packing:
                pack, = passed
    return here


def solution(mesh):
    placed = (
        P(None, "leaf", None, "draw"),
        P(None, "leaf", "draw", None),
        P(None, "leaf", "draw", None, None),
        P(),
        P(None, "leaf", None),
        P(None, "leaf"),
    )
    return jax.shard_map(
        functools.partial(on_device, mesh.shape["leaf"], mesh.shape["draw"]),
        mesh=mesh,
        in_specs=placed,
        out_specs=P(None, "leaf", None, "draw"),
        check_vma=False,
    )
```

```python
import functools

import jax
import jax.numpy as jnp
from jax import lax
from jax.experimental import pallas as pl
from jax.experimental.pallas import tpu as pltpu
from jax.sharding import PartitionSpec as P

CHUNKS = 1
VMEM = pl.BlockSpec(memory_space=pltpu.VMEM)
SMEM = pl.BlockSpec(memory_space=pltpu.SMEM)
ANY = pl.BlockSpec(memory_space=pl.ANY)
BF16, F32 = jnp.bfloat16, jnp.float32


def hop(value, axis, size, step):
    return lax.ppermute(value, axis, [(at, at ^ step) for at in range(size)])


def far_rows(value, axis, size):
    steps, step, other = [0], size // 2, None
    while step > 1:
        value = value if other is None else jnp.concatenate([value, other])
        other = hop(value, axis, size, step)
        steps = steps + [have ^ step for have in steps]
        step //= 2
    return [value] if other is None else [value, other], steps


def near_rows(value, steps, axis, size):
    return [value, hop(value, axis, size, 1)], [steps, [have ^ 1 for have in steps]]


def transposed_dot(left, right):
    return lax.dot_general(left, right, (((0,), (0,)), ((), ())), preferred_element_type=F32)


def take(refs, count):
    return list(refs[:count]), list(refs[count:])


def call(kernel, outs, scratch, small, arrays, out_spec=VMEM, flops=0, aliases={}):
    size = sum(value.size * value.dtype.itemsize for value in (*arrays, *outs))
    return pl.pallas_call(
        kernel,
        out_shape=outs,
        in_specs=[SMEM] * len(small) + [VMEM] * len(arrays),
        out_specs=[out_spec] * len(outs),
        scratch_shapes=scratch,
        input_output_aliases=aliases,
        cost_estimate=pl.CostEstimate(flops=flops, bytes_accessed=size, transcendentals=0),
        compiler_params=pltpu.CompilerParams(vmem_limit_bytes=16 * 1024 * 1024),
    )(*small, *arrays)


def row_blocks(refs, steps, block):
    return [
        (ref, at * block, step)
        for ref, held in zip(refs, steps, strict=True) for at, step in enumerate(held)
    ]


def fill_inverse(target, found, offset, rows, draw):
    for ref, at, step in found:
        start = pl.multiple_of((draw ^ step) * rows, rows)
        for node in range(target.shape[0]):
            first = at + offset + node * rows
            target[node, pl.ds(start, rows), :] = ref[first:first + rows, :]


def first_kernel(chunks, steps, picks, noise, *refs):
    *refs, _, inv = refs
    parts, refs = take(refs, len(steps))
    solved, sends = take(refs[1:], chunks)
    myself, draw = lax.axis_index("leaf"), lax.axis_index("draw")
    nodes, wide = noise.shape[0], solved[0].shape[-1]
    draws = sum(map(len, steps))
    rows = inv.shape[1] // draws
    fill_inverse(inv, row_blocks(parts, steps, 2 * nodes * rows), 0, rows, draw)
    for at, target in enumerate(solved):
        for node in range(nodes):
            right = noise[node, :, at * wide:(at + 1) * wide]
            target[node] = transposed_dot(inv[node], right).astype(BF16)
    for step, send in enumerate(sends, 1):
        node = picks[0, myself ^ step, myself]
        for at, target in enumerate(solved):
            send[at] = target[node]


def relay_kernel(owners, source, waits, joined, steps, picks, far, *refs):
    half = owners // 2
    _, refs = take(refs, waits)
    parts, refs = take(refs, joined)
    inverse, refs = take(refs, len(steps))
    sends, (joint, *refs) = take(refs, half - 1)
    myself, draw = lax.axis_index("leaf"), lax.axis_index("draw")
    at = 0
    for part in parts:
        joint[at:at + part.shape[0], :] = part[...]
        at += part.shape[0]
    if inverse:
        solved, inv = refs
        nodes = far.shape[0]
        rows = inv.shape[1] // sum(map(len, steps))
        found = row_blocks(inverse, steps, 2 * nodes * rows)
        fill_inverse(inv, found, nodes * rows, rows, draw)
        for node in range(nodes):
            solved[node] = transposed_dot(inv[node], far[node]).astype(BF16)
        far = solved
    for step, send in enumerate(sends, 1):
        send[0] = far[picks[source, myself ^ step, myself ^ half]]


def level_kernel(
    level, owners, steps, width, chunk, places, sides, earlier, waits, packing,
    picks, lists, counts, noise, *refs,
):
    half = owners // 2
    packs, refs = take(refs, len(steps))
    known, refs = take(refs, level * owners)
    done, refs = take(refs, earlier)
    _, refs = take(refs, waits)
    if packing:
        refs = refs[1:]
    target, *refs = refs
    sends, refs = take(refs, sides)
    if packing:
        refs = refs[1:]
    table, inv, *refs = refs
    myself, draw = lax.axis_index("leaf"), lax.axis_index("draw")
    nodes, wide = noise.shape[1], table.shape[-1]
    depth = inv.shape[1]
    rows = depth // sum(map(len, steps))
    found = row_blocks(packs, steps, nodes * (width * depth + rows))
    copies = []
    solved = target
    if earlier:
        solved, sems = refs
        per_level = (earlier + 1) // (level + 1)
        for at, ref in enumerate(done):
            here = target.at[at // per_level, :, :, pl.ds(at % per_level * wide, wide)]
            copies.append(pltpu.make_async_copy(ref, here, sems.at[at]))
            copies[-1].start()
    for at, (ref, place) in enumerate(zip(known, places, strict=True)):
        step = at % owners
        if step % half == 0:
            place = picks[at // owners, myself, myself ^ step]
        table[at] = ref[place]
    empty = level * owners
    table[empty] = jnp.zeros_like(table[empty])
    fill_inverse(inv, found, nodes * width * depth, rows, draw)
    for node in range(nodes):
        total = None
        for pack, start, step in found:
            for offset in range(width):
                slot = (draw ^ step) * width + offset
                live = slot < counts[level - 1, node]
                entry = jnp.where(live, lists[level - 1, node, slot] ^ myself, empty)
                at = start + (node * width + offset) * depth
                term = transposed_dot(pack[at:at + depth, :], table[entry])
                total = term if total is None else total + term
        side = noise[level, node, :, chunk * wide:(chunk + 1) * wide].astype(F32) - total
        solved[node] = transposed_dot(inv[node], side.astype(BF16)).astype(BF16)
    for step, send in enumerate(sends, 1):
        send[0] = solved[picks[level, myself ^ step, myself]]
    if earlier:
        here = target.at[level, :, :, pl.ds(chunk * wide, wide)]
        copies.append(pltpu.make_async_copy(solved, here, sems.at[earlier]))
        copies[-1].start()
    for copy in copies:
        copy.wait()


def on_device(owners, draws, noise, inverse, coupling, picks, lists, counts):
    levels, nodes, rows, columns = noise.shape
    wide, half, chunks = columns // CHUNKS, owners // 2, range(CHUNKS)
    width, last_level = coupling.shape[2], levels - 1
    shape = lambda *dims: jax.ShapeDtypeStruct(dims, BF16)
    part = shape(nodes, rows, wide)
    flat = lambda value: value.reshape(-1, rows)
    raw = [
        jnp.concatenate([flat(coupling[level - 1]), flat(inverse[level])])
        for level in range(1, levels)
    ]
    pack_shape = shape(*raw[0].shape)
    leaf = lambda value, step: hop(value, "leaf", owners, step)
    near = lambda values: [leaf(value, step) for step, value in enumerate(values, 1)]
    inv_here = pltpu.VMEM((nodes, rows, rows), BF16)
    dot_flops = 2 * rows * rows * wide

    far = leaf(noise[0], half)
    both = jnp.concatenate([flat(inverse[0]), leaf(flat(inverse[0]), half)])
    parts, steps = far_rows(both, "draw", draws)
    parts, steps = near_rows(jnp.concatenate(parts), steps, "draw", draws)
    *refs, pack = call(
        functools.partial(first_kernel, CHUNKS, steps),
        [part] * CHUNKS + [shape(CHUNKS, rows, wide)] * (half - 1) + [pack_shape],
        [inv_here],
        (picks,),
        (noise[0], *parts, raw[0]),
        flops=nodes * CHUNKS * dot_flops,
        aliases={2 + len(parts): CHUNKS + half - 1},
    )
    solved, sends = take(refs, CHUNKS)
    packs = []
    done, pieces = [solved], []
    for level in range(1, levels):
        source = level - 1
        if source:
            far = leaf(solved[0], half)
        got = near(sends)
        joined, far_steps = far_rows(pack, "draw", draws)
        outs = call(
            functools.partial(
                relay_kernel, owners, source, len(got), len(joined), [] if source else steps
            ),
            [shape(1, rows, wide)] * (half - 1)
            + [shape(sum(value.shape[0] for value in joined), rows)]
            + ([] if source else [part]),
            [] if source else [inv_here],
            (picks,),
            (far, *got, *joined, *([] if source else parts)),
            flops=0 if source else nodes * dot_flops,
        )
        sends, joint = outs[:half - 1], outs[half - 1]
        far = far if source else outs[half]
        packs.append(near_rows(joint, far_steps, "draw", draws)[0])
        pieces.append([[
            (solved[0], 0), *((ref, 0) for ref in got),
            (far, 0), *((ref, 0) for ref in near(sends)),
        ]])
        waits = []
        solved, sends = [], []
        for at in chunks:
            packing = at == 0 and level < last_level
            sides = half - 1 if packing else 0
            final = level == last_level and at == CHUNKS - 1
            earlier = [value for values in done for value in values] + solved if final else []
            known = [entry for below in range(level) for entry in pieces[below][at]]
            scratch = [pltpu.VMEM((level * owners + 1, rows, wide), BF16), inv_here]
            if final:
                scratch += [
                    pltpu.VMEM((nodes, rows, wide), BF16),
                    pltpu.SemaphoreType.DMA((len(earlier) + 1,)),
                ]
            here, *sent = call(
                functools.partial(
                    level_kernel, level, owners, steps, width, at,
                    [place for _, place in known], sides, len(earlier), len(waits), packing,
                ),
                [shape(levels, nodes, rows, columns) if final else part]
                + [shape(1, rows, wide)] * sides + [pack_shape] * packing,
                scratch,
                (picks, lists, counts),
                (noise, *packs[level - 1], *(ref for ref, _ in known), *earlier, *waits)
                + ((raw[level],) if packing else ()),
                out_spec=ANY if final else VMEM,
                aliases={
                    4 + len(packs[level - 1]) + len(known) + len(earlier) + len(waits): 1 + sides
                } if packing else {},
                flops=nodes * (draws * width + 1) * dot_flops,
            )
            solved.append(here)
            if packing:
                pack = sent.pop()
            sends += sent
            waits = []
        done.append(solved)
    return here


def solution(mesh):
    placed = (
        P(None, "leaf", None, "draw"),
        P(None, "leaf", "draw", None),
        P(None, "leaf", "draw", None, None),
        P(),
        P(None, "leaf", None),
        P(None, "leaf"),
    )
    return jax.shard_map(
        functools.partial(on_device, mesh.shape["leaf"], mesh.shape["draw"]),
        mesh=mesh,
        in_specs=placed,
        out_specs=P(None, "leaf", None, "draw"),
        check_vma=False,
    )
```

```python
import functools

import jax
import jax.numpy as jnp
from jax import lax
from jax.experimental import pallas as pl
from jax.experimental.pallas import tpu as pltpu
from jax.sharding import PartitionSpec as P

CHUNKS = 2
VMEM = pl.BlockSpec(memory_space=pltpu.VMEM)
SMEM = pl.BlockSpec(memory_space=pltpu.SMEM)
ANY = pl.BlockSpec(memory_space=pl.ANY)
BF16, F32 = jnp.bfloat16, jnp.float32


def hop(value, axis, size, step):
    return lax.ppermute(value, axis, [(at, at ^ step) for at in range(size)])


def far_rows(value, axis, size):
    values, held, step = [value], [[0]], size // 2
    while step > 1:
        if len(values) > 1:
            values, held = [jnp.concatenate(values)], [held[0] + held[1]]
        values.append(hop(values[0], axis, size, step))
        held.append([have ^ step for have in held[0]])
        step //= 2
    return values, held


def near_rows(values, held, axis, size):
    others = [hop(value, axis, size, 1) for value in values]
    return values + others, held + [[have ^ 1 for have in steps] for steps in held]


def transposed_dot(left, right):
    return lax.dot_general(left, right, (((0,), (0,)), ((), ())), preferred_element_type=F32)


def take(refs, count):
    return list(refs[:count]), list(refs[count:])


def shape(*dims):
    return jax.ShapeDtypeStruct(dims, BF16)


def call(kernel, outs, scratch, small, arrays, out_spec=VMEM, flops=0, aliases={}):
    size = sum(value.size * value.dtype.itemsize for value in (*arrays, *outs))
    return list(pl.pallas_call(
        kernel,
        out_shape=outs,
        in_specs=[SMEM] * len(small) + [VMEM] * len(arrays),
        out_specs=[out_spec] * len(outs),
        scratch_shapes=scratch,
        input_output_aliases=aliases,
        cost_estimate=pl.CostEstimate(flops=flops, bytes_accessed=size, transcendentals=0),
        compiler_params=pltpu.CompilerParams(vmem_limit_bytes=16 * 1024 * 1024),
    )(*small, *arrays))


def row_blocks(refs, held, block):
    return [
        (ref, at * block, step)
        for ref, steps in zip(refs, held, strict=True) for at, step in enumerate(steps)
    ]


def fill_inverse(target, found, offset, draw):
    rows = target.shape[1] // len(found)
    for ref, at, step in found:
        start = pl.multiple_of((draw ^ step) * rows, rows)
        for node in range(target.shape[0]):
            first = at + offset + node * rows
            target[node, pl.ds(start, rows), :] = ref[first:first + rows, :]


def first_kernel(held, picks, noise, *refs):
    parts, (_, solved, *sends, _, inv) = take(refs, len(held))
    myself, draw = lax.axis_index("leaf"), lax.axis_index("draw")
    nodes = noise.shape[0]
    draws = sum(map(len, held))
    rows = inv.shape[1] // draws
    fill_inverse(inv, row_blocks(parts, held, nodes * rows), 0, draw)
    for node in range(nodes):
        solved[node] = transposed_dot(inv[node], noise[node]).astype(BF16)
    for step, send in enumerate(sends, 1):
        send[0] = solved[picks[0, myself ^ step, myself]]


def relay_kernel(half, source, follow, waits, through, picks, far, *refs):
    own, refs = take(refs, follow)
    sends = refs[waits + through:][:half - 1]
    myself = lax.axis_index("leaf")
    for step, send in enumerate(sends, 1):
        send[0] = far[picks[source, myself ^ step, myself ^ half]]
        if follow:
            send[1] = own[0][picks[source, myself ^ step, myself]]


def level_kernel(
    level, owners, held, width, chunk, places, stored, sides, picks, lists, counts, noise, *refs
):
    half = owners // 2
    packs, refs = take(refs, len(held))
    known, refs = take(refs, level * owners)
    done, refs = take(refs, len(stored))
    target, *refs = refs
    sends, (table, inv, *refs) = take(refs, sides)
    myself, draw = lax.axis_index("leaf"), lax.axis_index("draw")
    levels, nodes = noise.shape[:2]
    wide = table.shape[-1]
    columns = slice(chunk * wide, (chunk + 1) * wide)
    depth = inv.shape[1]
    rows = depth // sum(map(len, held))
    span = nodes * (width * depth + rows)
    found = row_blocks(packs, held, (levels - 1) * span)
    offset = (level - 1) * span
    copies = []
    solved = target
    if done:
        solved, sems = refs
        for at, (ref, (into, first)) in enumerate(zip(done, stored, strict=True)):
            here = target.at[into, :, :, pl.ds(first, ref.shape[-1])]
            copies.append(pltpu.make_async_copy(ref, here, sems.at[at]))
            copies[-1].start()
    for at, (ref, place) in enumerate(zip(known, places, strict=True)):
        step = at % owners
        if step % half == 0:
            place = picks[at // owners, myself, myself ^ step]
        table[at] = ref[place] if ref.shape[-1] == wide else ref[place, :, columns]
    empty = level * owners
    table[empty] = jnp.zeros_like(table[empty])
    fill_inverse(inv, found, offset + nodes * width * depth, draw)
    for node in range(nodes):
        total = None
        for pack, start, step in found:
            for slot in range(width):
                entry = (draw ^ step) * width + slot
                live = entry < counts[level - 1, node]
                entry = jnp.where(live, lists[level - 1, node, entry] ^ myself, empty)
                at = start + offset + (node * width + slot) * depth
                term = transposed_dot(pack[at:at + depth, :], table[entry])
                total = term if total is None else total + term
        right_side = (noise[level, node, :, columns].astype(F32) - total).astype(BF16)
        solved[node] = transposed_dot(inv[node], right_side).astype(BF16)
    for step, send in enumerate(sends, 1):
        send[0] = solved[picks[level, myself ^ step, myself]]
    if done:
        here = target.at[level, :, :, pl.ds(chunk * wide, wide)]
        copies.append(pltpu.make_async_copy(solved, here, sems.at[len(done)]))
        copies[-1].start()
    for copy in copies:
        copy.wait()


def on_device(owners, draws, noise, inverse, coupling, picks, lists, counts):
    levels, nodes, rows, columns = noise.shape
    wide, half, chunks = columns // CHUNKS, owners // 2, range(CHUNKS)
    width = coupling.shape[2]
    part = shape(nodes, rows, wide)
    flat = lambda value: value.reshape(-1, rows)
    leaf = lambda value, step: hop(value, "leaf", owners, step)
    near = lambda values: [leaf(value, step) for step, value in enumerate(values, 1)]
    inv_here = pltpu.VMEM((nodes, rows, rows), BF16)
    dot_flops = 2 * rows * rows * wide

    raw = jnp.concatenate([
        flat(value) for level in range(1, levels) for value in (coupling[level - 1], inverse[level])
    ])
    values, steps = far_rows(flat(inverse[0]), "draw", draws)
    values, steps = near_rows(values, steps, "draw", draws)
    solved, *sends, raw = call(
        functools.partial(first_kernel, steps),
        [shape(nodes, rows, columns)] + [shape(1, rows, columns)] * (half - 1) + [shape(*raw.shape)],
        [inv_here],
        (picks,),
        (noise[0], *values, raw),
        flops=nodes * CHUNKS * dot_flops,
        aliases={2 + len(values): half},
    )
    far, got = leaf(solved, half), near(sends)
    values, steps = far_rows(raw, "draw", draws)
    sends = call(
        functools.partial(relay_kernel, half, 0, 0, len(got), len(values)),
        [shape(1, rows, columns)] * (half - 1) + [shape(*value.shape) for value in values],
        [],
        (picks,),
        (far, *got, *values),
        aliases={2 + len(got) + at: half - 1 + at for at in range(len(values))},
    )
    sends, values = take(sends, half - 1)
    packs, steps = near_rows(values, steps, "draw", draws)
    entries = [(solved, 0), *((ref, 0) for ref in got), (far, 0), *((ref, 0) for ref in near(sends))]
    pieces, done = [[entries] * CHUNKS], [(solved, (0, 0))]

    for level in range(1, levels):
        last_level = level == levels - 1
        solved, sends = [], []
        for at in chunks:
            sides = half - 1 if at == 0 and not last_level else 0
            final = last_level and at == CHUNKS - 1
            known = [entry for below in range(level) for entry in pieces[below][at]]
            stored = done if final else []
            scratch = [pltpu.VMEM((level * owners + 1, rows, wide), BF16), inv_here]
            if final:
                scratch += [
                    pltpu.VMEM((nodes, rows, wide), BF16),
                    pltpu.SemaphoreType.DMA((len(stored) + 1,)),
                ]
            here, *sent = call(
                functools.partial(
                    level_kernel, level, owners, steps, width, at,
                    [place for _, place in known], [place for _, place in stored], sides,
                ),
                [shape(*noise.shape) if final else part] + [shape(1, rows, wide)] * sides,
                scratch,
                (picks, lists, counts),
                (noise, *packs, *(ref for ref, _ in known), *(ref for ref, _ in stored)),
                out_spec=ANY if final else VMEM,
                flops=nodes * (draws * width + 1) * dot_flops,
            )
            solved.append(here)
            done.append((here, (level, at * wide)))
            sends += sent
        if last_level:
            return here
        far = [leaf(value, half) for value in solved]
        got = near(sends)
        close, distant, waits = [[(ref, 0) for ref in got]], [], got
        for at in chunks:
            follow = solved[at + 1:at + 2]
            sends = call(
                functools.partial(relay_kernel, half, level, len(follow), len(waits), 0),
                [shape(1 + len(follow), rows, wide)] * (half - 1),
                [],
                (picks,),
                (far[at], *follow, *waits),
            )
            got, waits = near(sends), []
            distant.append([(ref, 0) for ref in got])
            close.append([(ref, 1) for ref in got])
        pieces.append([
            [(solved[at], 0), *close[at], (far[at], 0), *distant[at]] for at in chunks
        ])


def solution(mesh):
    placed = (
        P(None, "leaf", None, "draw"),
        P(None, "leaf", "draw", None),
        P(None, "leaf", "draw", None, None),
        P(),
        P(None, "leaf", None),
        P(None, "leaf"),
    )
    return jax.shard_map(
        functools.partial(on_device, mesh.shape["leaf"], mesh.shape["draw"]),
        mesh=mesh,
        in_specs=placed,
        out_specs=P(None, "leaf", None, "draw"),
        check_vma=False,
    )
```

```python
import functools

import jax
import jax.numpy as jnp
from jax import lax
from jax.experimental import pallas as pl
from jax.experimental.pallas import tpu as pltpu
from jax.sharding import PartitionSpec as P

CHUNKS = 2
VMEM = pl.BlockSpec(memory_space=pltpu.VMEM)
SMEM = pl.BlockSpec(memory_space=pltpu.SMEM)
ANY = pl.BlockSpec(memory_space=pl.ANY)
BF16, F32 = jnp.bfloat16, jnp.float32


def hop(value, axis, size, step):
    return lax.ppermute(value, axis, [(at, at ^ step) for at in range(size)])


def far_rows(value, axis, size):
    values, held, step = [value], [[0]], size // 2
    while step > 1:
        if len(values) > 1:
            values, held = [jnp.concatenate(values)], [held[0] + held[1]]
        values.append(hop(values[0], axis, size, step))
        held.append([have ^ step for have in held[0]])
        step //= 2
    return values, held


def near_rows(values, held, axis, size):
    others = [hop(value, axis, size, 1) for value in values]
    return values + others, held + [[have ^ 1 for have in steps] for steps in held]


def transposed_dot(left, right):
    return lax.dot_general(left, right, (((0,), (0,)), ((), ())), preferred_element_type=F32)


def take(refs, count):
    return list(refs[:count]), list(refs[count:])


def shape(*dims):
    return jax.ShapeDtypeStruct(dims, BF16)


def call(kernel, outs, scratch, small, arrays, out_spec=VMEM, flops=0, aliases={}):
    size = sum(value.size * value.dtype.itemsize for value in (*arrays, *outs))
    return list(pl.pallas_call(
        kernel,
        out_shape=outs,
        in_specs=[SMEM] * len(small) + [VMEM] * len(arrays),
        out_specs=[out_spec] * len(outs),
        scratch_shapes=scratch,
        input_output_aliases=aliases,
        cost_estimate=pl.CostEstimate(flops=flops, bytes_accessed=size, transcendentals=0),
        compiler_params=pltpu.CompilerParams(vmem_limit_bytes=16 * 1024 * 1024),
    )(*small, *arrays))


def row_blocks(refs, held, block):
    return [
        (ref, at * block, step)
        for ref, steps in zip(refs, held, strict=True) for at, step in enumerate(steps)
    ]


def fill_inverse(target, found, offset, draw):
    rows = target.shape[1] // len(found)
    for ref, at, step in found:
        start = pl.multiple_of((draw ^ step) * rows, rows)
        for node in range(target.shape[0]):
            first = at + offset + node * rows
            target[node, pl.ds(start, rows), :] = ref[first:first + rows, :]


def first_kernel(held, picks, noise, *refs):
    parts, (_, solved, *sends, _, inv) = take(refs, len(held))
    myself, draw = lax.axis_index("leaf"), lax.axis_index("draw")
    nodes = noise.shape[0]
    draws = sum(map(len, held))
    rows = inv.shape[1] // draws
    fill_inverse(inv, row_blocks(parts, held, nodes * rows), 0, draw)
    for node in range(nodes):
        solved[node] = transposed_dot(inv[node], noise[node]).astype(BF16)
    for step, send in enumerate(sends, 1):
        send[0] = solved[picks[0, myself ^ step, myself]]


def relay_kernel(half, source, waits, through, picks, far, *refs):
    sends = refs[waits + through:][:half - 1]
    myself = lax.axis_index("leaf")
    for step, send in enumerate(sends, 1):
        send[0] = far[picks[source, myself ^ step, myself ^ half]]


def level_kernel(
    level, owners, held, width, chunk, places, stored, sides, mates,
    picks, lists, counts, noise, *refs,
):
    half = owners // 2
    packs, refs = take(refs, len(held))
    known, refs = take(refs, level * owners)
    done, refs = take(refs, len(stored))
    chunks, refs = take(refs, mates)
    target, *refs = refs
    sends, (table, inv, *refs) = take(refs, sides)
    myself, draw = lax.axis_index("leaf"), lax.axis_index("draw")
    levels, nodes = noise.shape[:2]
    wide = table.shape[-1]
    columns = slice(chunk * wide, (chunk + 1) * wide)
    depth = inv.shape[1]
    rows = depth // sum(map(len, held))
    span = nodes * (width * depth + rows)
    found = row_blocks(packs, held, (levels - 1) * span)
    offset = (level - 1) * span
    copies = []
    solved = target
    if done:
        solved, sems = refs
        for at, (ref, (into, first)) in enumerate(zip(done, stored, strict=True)):
            here = target.at[into, :, :, pl.ds(first, ref.shape[-1])]
            copies.append(pltpu.make_async_copy(ref, here, sems.at[at]))
            copies[-1].start()
    for at, (ref, place) in enumerate(zip(known, places, strict=True)):
        step = at % owners
        if step % half == 0:
            place = picks[at // owners, myself, myself ^ step]
        table[at] = ref[place] if ref.shape[-1] == wide else ref[place, :, columns]
    empty = level * owners
    table[empty] = jnp.zeros_like(table[empty])
    fill_inverse(inv, found, offset + nodes * width * depth, draw)
    for node in range(nodes):
        total = None
        for pack, start, step in found:
            for slot in range(width):
                entry = (draw ^ step) * width + slot
                live = entry < counts[level - 1, node]
                entry = jnp.where(live, lists[level - 1, node, entry] ^ myself, empty)
                at = start + offset + (node * width + slot) * depth
                term = transposed_dot(pack[at:at + depth, :], table[entry])
                total = term if total is None else total + term
        right_side = (noise[level, node, :, columns].astype(F32) - total).astype(BF16)
        solved[node] = transposed_dot(inv[node], right_side).astype(BF16)
    for step, send in enumerate(sends, 1):
        node = picks[level, myself ^ step, myself]
        for at, ref in enumerate([*chunks, solved]):
            send[at] = ref[node]
    if done:
        here = target.at[level, :, :, pl.ds(chunk * wide, wide)]
        copies.append(pltpu.make_async_copy(solved, here, sems.at[len(done)]))
        copies[-1].start()
    for copy in copies:
        copy.wait()


def on_device(owners, draws, noise, inverse, coupling, picks, lists, counts):
    levels, nodes, rows, columns = noise.shape
    wide, half, chunks = columns // CHUNKS, owners // 2, range(CHUNKS)
    width = coupling.shape[2]
    part = shape(nodes, rows, wide)
    flat = lambda value: value.reshape(-1, rows)
    leaf = lambda value, step: hop(value, "leaf", owners, step)
    near = lambda values: [leaf(value, step) for step, value in enumerate(values, 1)]
    inv_here = pltpu.VMEM((nodes, rows, rows), BF16)
    dot_flops = 2 * rows * rows * wide

    raw = jnp.concatenate([
        flat(value) for level in range(1, levels) for value in (coupling[level - 1], inverse[level])
    ])
    values, steps = far_rows(flat(inverse[0]), "draw", draws)
    values, steps = near_rows(values, steps, "draw", draws)
    solved, *sends, raw = call(
        functools.partial(first_kernel, steps),
        [shape(nodes, rows, columns)] + [shape(1, rows, columns)] * (half - 1) + [shape(*raw.shape)],
        [inv_here],
        (picks,),
        (noise[0], *values, raw),
        flops=nodes * CHUNKS * dot_flops,
        aliases={2 + len(values): half},
    )
    far, got = leaf(solved, half), near(sends)
    values, steps = far_rows(raw, "draw", draws)
    sends = call(
        functools.partial(relay_kernel, half, 0, len(got), len(values)),
        [shape(1, rows, columns)] * (half - 1) + [shape(*value.shape) for value in values],
        [],
        (picks,),
        (far, *got, *values),
        aliases={2 + len(got) + at: half - 1 + at for at in range(len(values))},
    )
    sends, values = take(sends, half - 1)
    packs, steps = near_rows(values, steps, "draw", draws)
    entries = [(solved, 0), *((ref, 0) for ref in got), (far, 0), *((ref, 0) for ref in near(sends))]
    pieces, done = [[entries] * CHUNKS], [(solved, (0, 0))]

    for level in range(1, levels):
        last_level = level == levels - 1
        solved, sends = [], []
        for at in chunks:
            ends = at == CHUNKS - 1 and not last_level
            sides, mates = (half - 1, list(solved)) if ends else (0, [])
            final = last_level and at == CHUNKS - 1
            known = [entry for below in range(level) for entry in pieces[below][at]]
            stored = done if final else []
            scratch = [pltpu.VMEM((level * owners + 1, rows, wide), BF16), inv_here]
            if final:
                scratch += [
                    pltpu.VMEM((nodes, rows, wide), BF16),
                    pltpu.SemaphoreType.DMA((len(stored) + 1,)),
                ]
            here, *sent = call(
                functools.partial(
                    level_kernel, level, owners, steps, width, at,
                    [place for _, place in known], [place for _, place in stored], sides, len(mates),
                ),
                [shape(*noise.shape) if final else part] + [shape(CHUNKS, rows, wide)] * sides,
                scratch,
                (picks, lists, counts),
                (noise, *packs, *(ref for ref, _ in known), *(ref for ref, _ in stored), *mates),
                out_spec=ANY if final else VMEM,
                flops=nodes * (draws * width + 1) * dot_flops,
            )
            solved.append(here)
            done.append((here, (level, at * wide)))
            sends += sent
        if last_level:
            return here
        far = [leaf(value, half) for value in solved]
        got = near(sends)
        pieces.append([])
        for at in chunks:
            waits = got if at == CHUNKS - 1 else []
            sends = call(
                functools.partial(relay_kernel, half, level, len(waits), 0),
                [shape(1, rows, wide)] * (half - 1),
                [],
                (picks,),
                (far[at], *waits),
            )
            pieces[level].append([
                (solved[at], 0), *((ref, at) for ref in got),
                (far[at], 0), *((ref, 0) for ref in near(sends)),
            ])


def solution(mesh):
    placed = (
        P(None, "leaf", None, "draw"),
        P(None, "leaf", "draw", None),
        P(None, "leaf", "draw", None, None),
        P(),
        P(None, "leaf", None),
        P(None, "leaf"),
    )
    return jax.shard_map(
        functools.partial(on_device, mesh.shape["leaf"], mesh.shape["draw"]),
        mesh=mesh,
        in_specs=placed,
        out_specs=P(None, "leaf", None, "draw"),
        check_vma=False,
    )
```

```python
import functools

import jax
import jax.numpy as jnp
from jax import lax
from jax.experimental import pallas as pl
from jax.experimental.pallas import tpu as pltpu
from jax.sharding import PartitionSpec as P

CHUNKS = 2
VMEM = pl.BlockSpec(memory_space=pltpu.VMEM)
SMEM = pl.BlockSpec(memory_space=pltpu.SMEM)
ANY = pl.BlockSpec(memory_space=pl.ANY)
BF16, F32 = jnp.bfloat16, jnp.float32


def hop(value, axis, size, step):
    return lax.ppermute(value, axis, [(at, at ^ step) for at in range(size)])


def far_rows(value, axis, size):
    values, held, step = [value], [[0]], size // 2
    while step > 1:
        if len(values) > 1:
            values, held = [jnp.concatenate(values)], [held[0] + held[1]]
        values.append(hop(values[0], axis, size, step))
        held.append([have ^ step for have in held[0]])
        step //= 2
    return values, held


def near_rows(values, held, axis, size):
    others = [hop(value, axis, size, 1) for value in values]
    return values + others, held + [[have ^ 1 for have in steps] for steps in held]


def transposed_dot(left, right):
    return lax.dot_general(left, right, (((0,), (0,)), ((), ())), preferred_element_type=F32)


def take(refs, count):
    return list(refs[:count]), list(refs[count:])


def shape(*dims):
    return jax.ShapeDtypeStruct(dims, BF16)


def call(kernel, outs, scratch, small, arrays, out_spec=VMEM, flops=0, aliases={}):
    size = sum(value.size * value.dtype.itemsize for value in (*arrays, *outs))
    return list(pl.pallas_call(
        kernel,
        out_shape=outs,
        in_specs=[SMEM] * len(small) + [VMEM] * len(arrays),
        out_specs=[out_spec] * len(outs),
        scratch_shapes=scratch,
        input_output_aliases=aliases,
        cost_estimate=pl.CostEstimate(flops=flops, bytes_accessed=size, transcendentals=0),
        compiler_params=pltpu.CompilerParams(vmem_limit_bytes=16 * 1024 * 1024),
    )(*small, *arrays))


def row_blocks(refs, held, block):
    return [
        (ref, at * block, step)
        for ref, steps in zip(refs, held, strict=True) for at, step in enumerate(steps)
    ]


def fill_inverse(target, found, offset, draw):
    rows = target.shape[1] // len(found)
    for ref, at, step in found:
        start = pl.multiple_of((draw ^ step) * rows, rows)
        for node in range(target.shape[0]):
            first = at + offset + node * rows
            target[node, pl.ds(start, rows), :] = ref[first:first + rows, :]


def first_kernel(held, picks, noise, *refs):
    parts, (_, solved, *sends, _, inv) = take(refs, len(held))
    myself, draw = lax.axis_index("leaf"), lax.axis_index("draw")
    nodes = noise.shape[0]
    draws = sum(map(len, held))
    rows = inv.shape[1] // draws
    fill_inverse(inv, row_blocks(parts, held, nodes * rows), 0, draw)
    for node in range(nodes):
        solved[node] = transposed_dot(inv[node], noise[node]).astype(BF16)
    for step, send in enumerate(sends, 1):
        send[0] = solved[picks[0, myself ^ step, myself]]


def relay_kernel(half, source, waits, through, picks, far, *refs):
    sends = refs[waits + through:len(refs) - through]
    myself = lax.axis_index("leaf")
    for at, send in enumerate(sends):
        chunk, step = divmod(at, half - 1)
        wide = send.shape[-1]
        node = picks[source, myself ^ (step + 1), myself ^ half]
        send[0] = far[node, :, chunk * wide:(chunk + 1) * wide]


def level_kernel(
    level, owners, held, width, chunk, places, stored, sides, mates,
    picks, lists, counts, noise, *refs,
):
    half = owners // 2
    packs, refs = take(refs, len(held))
    known, refs = take(refs, level * owners)
    done, refs = take(refs, len(stored))
    chunks, refs = take(refs, mates)
    target, *refs = refs
    sends, (table, inv, *refs) = take(refs, sides)
    myself, draw = lax.axis_index("leaf"), lax.axis_index("draw")
    levels, nodes = noise.shape[:2]
    wide = table.shape[-1]
    columns = slice(chunk * wide, (chunk + 1) * wide)
    depth = inv.shape[1]
    rows = depth // sum(map(len, held))
    span = nodes * (width * depth + rows)
    found = row_blocks(packs, held, (levels - 1) * span)
    offset = (level - 1) * span
    copies = []
    solved = target
    if done:
        solved, sems = refs
        for at, (ref, (into, first)) in enumerate(zip(done, stored, strict=True)):
            here = target.at[into, :, :, pl.ds(first, ref.shape[-1])]
            copies.append(pltpu.make_async_copy(ref, here, sems.at[at]))
            copies[-1].start()
    for at, (ref, place) in enumerate(zip(known, places, strict=True)):
        step = at % owners
        if step % half == 0:
            place = picks[at // owners, myself, myself ^ step]
        table[at] = ref[place] if ref.shape[-1] == wide else ref[place, :, columns]
    empty = level * owners
    table[empty] = jnp.zeros_like(table[empty])
    fill_inverse(inv, found, offset + nodes * width * depth, draw)
    for node in range(nodes):
        total = None
        for pack, start, step in found:
            for slot in range(width):
                entry = (draw ^ step) * width + slot
                live = entry < counts[level - 1, node]
                entry = jnp.where(live, lists[level - 1, node, entry] ^ myself, empty)
                at = start + offset + (node * width + slot) * depth
                term = transposed_dot(pack[at:at + depth, :], table[entry])
                total = term if total is None else total + term
        right_side = (noise[level, node, :, columns].astype(F32) - total).astype(BF16)
        solved[node] = transposed_dot(inv[node], right_side).astype(BF16)
    for step, send in enumerate(sends, 1):
        node = picks[level, myself ^ step, myself]
        for at, ref in enumerate([*chunks, solved]):
            send[at] = ref[node]
    if done:
        here = target.at[level, :, :, pl.ds(chunk * wide, wide)]
        copies.append(pltpu.make_async_copy(solved, here, sems.at[len(done)]))
        copies[-1].start()
    for copy in copies:
        copy.wait()


def on_device(owners, draws, noise, inverse, coupling, picks, lists, counts):
    levels, nodes, rows, columns = noise.shape
    wide, half, chunks = columns // CHUNKS, owners // 2, range(CHUNKS)
    width = coupling.shape[2]
    part = shape(nodes, rows, wide)
    flat = lambda value: value.reshape(-1, rows)
    leaf = lambda value, step: hop(value, "leaf", owners, step)
    near = lambda values: [leaf(value, step) for step, value in enumerate(values, 1)]
    inv_here = pltpu.VMEM((nodes, rows, rows), BF16)
    dot_flops = 2 * rows * rows * wide

    raw = jnp.concatenate([
        flat(value) for level in range(1, levels) for value in (coupling[level - 1], inverse[level])
    ])
    values, steps = far_rows(flat(inverse[0]), "draw", draws)
    values, steps = near_rows(values, steps, "draw", draws)
    solved, *sends, raw = call(
        functools.partial(first_kernel, steps),
        [shape(nodes, rows, columns)] + [shape(1, rows, columns)] * (half - 1) + [shape(*raw.shape)],
        [inv_here],
        (picks,),
        (noise[0], *values, raw),
        flops=nodes * CHUNKS * dot_flops,
        aliases={2 + len(values): half},
    )
    far, got = leaf(solved, half), near(sends)
    values, steps = far_rows(raw, "draw", draws)
    sends = call(
        functools.partial(relay_kernel, half, 0, len(got), len(values)),
        [shape(1, rows, wide)] * (CHUNKS * (half - 1)) + [shape(*value.shape) for value in values],
        [],
        (picks,),
        (far, *got, *values),
        aliases={2 + len(got) + at: CHUNKS * (half - 1) + at for at in range(len(values))},
    )
    sends, values = take(sends, CHUNKS * (half - 1))
    packs, steps = near_rows(values, steps, "draw", draws)
    pieces, done = [[]], [(solved, (0, 0))]
    for at in chunks:
        distant, sends = take(sends, half - 1)
        pieces[0].append([
            (solved, 0), *((ref, 0) for ref in got),
            (far, 0), *((ref, 0) for ref in near(distant)),
        ])

    for level in range(1, levels):
        last_level = level == levels - 1
        solved, sends = [], []
        for at in chunks:
            ends = at == CHUNKS - 1 and not last_level
            sides, mates = (half - 1, list(solved)) if ends else (0, [])
            final = last_level and at == CHUNKS - 1
            known = [entry for below in range(level) for entry in pieces[below][at]]
            stored = done if final else []
            scratch = [pltpu.VMEM((level * owners + 1, rows, wide), BF16), inv_here]
            if final:
                scratch += [
                    pltpu.VMEM((nodes, rows, wide), BF16),
                    pltpu.SemaphoreType.DMA((len(stored) + 1,)),
                ]
            here, *sent = call(
                functools.partial(
                    level_kernel, level, owners, steps, width, at,
                    [place for _, place in known], [place for _, place in stored], sides, len(mates),
                ),
                [shape(*noise.shape) if final else part] + [shape(CHUNKS, rows, wide)] * sides,
                scratch,
                (picks, lists, counts),
                (noise, *packs, *(ref for ref, _ in known), *(ref for ref, _ in stored), *mates),
                out_spec=ANY if final else VMEM,
                flops=nodes * (draws * width + 1) * dot_flops,
            )
            solved.append(here)
            done.append((here, (level, at * wide)))
            sends += sent
        if last_level:
            return here
        far = [leaf(value, half) for value in solved]
        got = near(sends)
        pieces.append([])
        for at in chunks:
            waits = got if at == CHUNKS - 1 else []
            sends = call(
                functools.partial(relay_kernel, half, level, len(waits), 0),
                [shape(1, rows, wide)] * (half - 1),
                [],
                (picks,),
                (far[at], *waits),
            )
            pieces[level].append([
                (solved[at], 0), *((ref, at) for ref in got),
                (far[at], 0), *((ref, 0) for ref in near(sends)),
            ])


def solution(mesh):
    placed = (
        P(None, "leaf", None, "draw"),
        P(None, "leaf", "draw", None),
        P(None, "leaf", "draw", None, None),
        P(),
        P(None, "leaf", None),
        P(None, "leaf"),
    )
    return jax.shard_map(
        functools.partial(on_device, mesh.shape["leaf"], mesh.shape["draw"]),
        mesh=mesh,
        in_specs=placed,
        out_specs=P(None, "leaf", None, "draw"),
        check_vma=False,
    )
```

```python
import functools

import jax
import jax.numpy as jnp
from jax import lax
from jax.experimental import pallas as pl
from jax.experimental.pallas import tpu as pltpu
from jax.sharding import PartitionSpec as P

CHUNKS = 2
VMEM = pl.BlockSpec(memory_space=pltpu.VMEM)
SMEM = pl.BlockSpec(memory_space=pltpu.SMEM)
ANY = pl.BlockSpec(memory_space=pl.ANY)
BF16, F32 = jnp.bfloat16, jnp.float32


def hop(value, axis, size, step):
    return lax.ppermute(value, axis, [(at, at ^ step) for at in range(size)])


def far_rows(value, axis, size):
    values, held, step = [value], [[0]], size // 2
    while step > 1:
        if len(values) > 1:
            values, held = [jnp.concatenate(values)], [held[0] + held[1]]
        values.append(hop(values[0], axis, size, step))
        held.append([have ^ step for have in held[0]])
        step //= 2
    return values, held


def near_rows(values, held, axis, size):
    others = [hop(value, axis, size, 1) for value in values]
    return values + others, held + [[have ^ 1 for have in steps] for steps in held]


def transposed_dot(left, right):
    return lax.dot_general(left, right, (((0,), (0,)), ((), ())), preferred_element_type=F32)


def take(refs, count):
    return list(refs[:count]), list(refs[count:])


def shape(*dims):
    return jax.ShapeDtypeStruct(dims, BF16)


def call(kernel, outs, scratch, small, arrays, out_spec=VMEM, flops=0, aliases={}):
    size = sum(value.size * value.dtype.itemsize for value in (*arrays, *outs))
    return list(pl.pallas_call(
        kernel,
        out_shape=outs,
        in_specs=[SMEM] * len(small) + [VMEM] * len(arrays),
        out_specs=[out_spec] * len(outs),
        scratch_shapes=scratch,
        input_output_aliases=aliases,
        cost_estimate=pl.CostEstimate(flops=flops, bytes_accessed=size, transcendentals=0),
        compiler_params=pltpu.CompilerParams(vmem_limit_bytes=16 * 1024 * 1024),
    )(*small, *arrays))


def row_blocks(refs, held, block):
    return [
        (ref, at * block, step)
        for ref, steps in zip(refs, held, strict=True) for at, step in enumerate(steps)
    ]


def fill_inverse(target, found, offset, draw):
    rows = target.shape[1] // len(found)
    for ref, at, step in found:
        start = pl.multiple_of((draw ^ step) * rows, rows)
        for node in range(target.shape[0]):
            first = at + offset + node * rows
            target[node, pl.ds(start, rows), :] = ref[first:first + rows, :]


def first_kernel(held, picks, noise, *refs):
    parts, (_, solved, *sends, _, inv) = take(refs, len(held))
    myself, draw = lax.axis_index("leaf"), lax.axis_index("draw")
    nodes = noise.shape[0]
    draws = sum(map(len, held))
    rows = inv.shape[1] // draws
    fill_inverse(inv, row_blocks(parts, held, nodes * rows), 0, draw)
    for node in range(nodes):
        solved[node] = transposed_dot(inv[node], noise[node]).astype(BF16)
    for step, send in enumerate(sends, 1):
        send[0] = solved[picks[0, myself ^ step, myself]]


def relay_kernel(half, source, waits, through, picks, far, *refs):
    sends = refs[waits + through:len(refs) - through]
    myself = lax.axis_index("leaf")
    for at, send in enumerate(sends):
        chunk, step = divmod(at, half - 1)
        wide = send.shape[-1]
        node = picks[source, myself ^ (step + 1), myself ^ half]
        send[0] = far[node, :, chunk * wide:(chunk + 1) * wide]


def level_kernel(
    level, owners, held, width, chunk, places, stored, sides, mates,
    picks, lists, counts, noise, *refs,
):
    half = owners // 2
    packs, refs = take(refs, len(held))
    known, refs = take(refs, level * owners)
    done, refs = take(refs, len(stored))
    chunks, refs = take(refs, mates)
    target, *refs = refs
    sends, (table, inv, *refs) = take(refs, sides)
    myself, draw = lax.axis_index("leaf"), lax.axis_index("draw")
    levels, nodes = noise.shape[:2]
    wide = table.shape[-1]
    columns = slice(chunk * wide, (chunk + 1) * wide)
    depth = inv.shape[1]
    rows = depth // sum(map(len, held))
    span = nodes * (width * depth + rows)
    found = row_blocks(packs, held, (levels - 1) * span)
    offset = (level - 1) * span
    copies = []
    solved = target
    if done:
        solved, sems = refs
        for at, (ref, (into, first)) in enumerate(zip(done, stored, strict=True)):
            here = target.at[into, :, :, pl.ds(first, ref.shape[-1])]
            copies.append(pltpu.make_async_copy(ref, here, sems.at[at]))
            copies[-1].start()
    for at, (ref, place) in enumerate(zip(known, places, strict=True)):
        step = at % owners
        if step % half == 0:
            place = picks[at // owners, myself, myself ^ step]
        table[at] = ref[place] if ref.shape[-1] == wide else ref[place, :, columns]
    empty = level * owners
    table[empty] = jnp.zeros_like(table[empty])
    fill_inverse(inv, found, offset + nodes * width * depth, draw)
    for node in range(nodes):
        total = None
        for pack, start, step in found:
            for slot in range(width):
                entry = (draw ^ step) * width + slot
                live = entry < counts[level - 1, node]
                entry = jnp.where(live, lists[level - 1, node, entry] ^ myself, empty)
                at = start + offset + (node * width + slot) * depth
                term = transposed_dot(pack[at:at + depth, :], table[entry])
                total = term if total is None else total + term
        right_side = (noise[level, node, :, columns].astype(F32) - total).astype(BF16)
        solved[node] = transposed_dot(inv[node], right_side).astype(BF16)
        if done:
            here = target.at[level, node, :, pl.ds(chunk * wide, wide)]
            copies.append(pltpu.make_async_copy(solved.at[node], here, sems.at[len(copies)]))
            copies[-1].start()
    for step, send in enumerate(sends, 1):
        node = picks[level, myself ^ step, myself]
        for at, ref in enumerate([*chunks, solved]):
            send[at] = ref[node]
    for copy in copies:
        copy.wait()


def on_device(owners, draws, noise, inverse, coupling, picks, lists, counts):
    levels, nodes, rows, columns = noise.shape
    wide, half, chunks = columns // CHUNKS, owners // 2, range(CHUNKS)
    width = coupling.shape[2]
    part = shape(nodes, rows, wide)
    flat = lambda value: value.reshape(-1, rows)
    leaf = lambda value, step: hop(value, "leaf", owners, step)
    near = lambda values: [leaf(value, step) for step, value in enumerate(values, 1)]
    inv_here = pltpu.VMEM((nodes, rows, rows), BF16)
    dot_flops = 2 * rows * rows * wide

    raw = jnp.concatenate([
        flat(value) for level in range(1, levels) for value in (coupling[level - 1], inverse[level])
    ])
    values, steps = far_rows(flat(inverse[0]), "draw", draws)
    values, steps = near_rows(values, steps, "draw", draws)
    solved, *sends, raw = call(
        functools.partial(first_kernel, steps),
        [shape(nodes, rows, columns)] + [shape(1, rows, columns)] * (half - 1) + [shape(*raw.shape)],
        [inv_here],
        (picks,),
        (noise[0], *values, raw),
        flops=nodes * CHUNKS * dot_flops,
        aliases={2 + len(values): half},
    )
    far, got = leaf(solved, half), near(sends)
    values, steps = far_rows(raw, "draw", draws)
    sends = call(
        functools.partial(relay_kernel, half, 0, len(got), len(values)),
        [shape(1, rows, wide)] * (CHUNKS * (half - 1)) + [shape(*value.shape) for value in values],
        [],
        (picks,),
        (far, *got, *values),
        aliases={2 + len(got) + at: CHUNKS * (half - 1) + at for at in range(len(values))},
    )
    sends, values = take(sends, CHUNKS * (half - 1))
    packs, steps = near_rows(values, steps, "draw", draws)
    pieces, done = [[]], [(solved, (0, 0))]
    for at in chunks:
        distant, sends = take(sends, half - 1)
        pieces[0].append([
            (solved, 0), *((ref, 0) for ref in got),
            (far, 0), *((ref, 0) for ref in near(distant)),
        ])

    for level in range(1, levels):
        last_level = level == levels - 1
        solved, sends = [], []
        for at in chunks:
            ends = at == CHUNKS - 1 and not last_level
            sides, mates = (half - 1, list(solved)) if ends else (0, [])
            final = last_level and at == CHUNKS - 1
            known = [entry for below in range(level) for entry in pieces[below][at]]
            stored = done if final else []
            scratch = [pltpu.VMEM((level * owners + 1, rows, wide), BF16), inv_here]
            if final:
                scratch += [
                    pltpu.VMEM((nodes, rows, wide), BF16),
                    pltpu.SemaphoreType.DMA((len(stored) + nodes,)),
                ]
            here, *sent = call(
                functools.partial(
                    level_kernel, level, owners, steps, width, at,
                    [place for _, place in known], [place for _, place in stored], sides, len(mates),
                ),
                [shape(*noise.shape) if final else part] + [shape(CHUNKS, rows, wide)] * sides,
                scratch,
                (picks, lists, counts),
                (noise, *packs, *(ref for ref, _ in known), *(ref for ref, _ in stored), *mates),
                out_spec=ANY if final else VMEM,
                flops=nodes * (draws * width + 1) * dot_flops,
            )
            solved.append(here)
            done.append((here, (level, at * wide)))
            sends += sent
        if last_level:
            return here
        far = [leaf(value, half) for value in solved]
        got = near(sends)
        pieces.append([])
        for at in chunks:
            sends = call(
                functools.partial(relay_kernel, half, level, 0, 0),
                [shape(1, rows, wide)] * (half - 1),
                [],
                (picks,),
                (far[at],),
            )
            pieces[level].append([
                (solved[at], 0), *((ref, at) for ref in got),
                (far[at], 0), *((ref, 0) for ref in near(sends)),
            ])


def solution(mesh):
    placed = (
        P(None, "leaf", None, "draw"),
        P(None, "leaf", "draw", None),
        P(None, "leaf", "draw", None, None),
        P(),
        P(None, "leaf", None),
        P(None, "leaf"),
    )
    return jax.shard_map(
        functools.partial(on_device, mesh.shape["leaf"], mesh.shape["draw"]),
        mesh=mesh,
        in_specs=placed,
        out_specs=P(None, "leaf", None, "draw"),
        check_vma=False,
    )
```

```python
import functools

import jax
import jax.numpy as jnp
from jax import lax
from jax.experimental import pallas as pl
from jax.experimental.pallas import tpu as pltpu
from jax.sharding import PartitionSpec as P

CHUNKS = 2
VMEM = pl.BlockSpec(memory_space=pltpu.VMEM)
SMEM = pl.BlockSpec(memory_space=pltpu.SMEM)
ANY = pl.BlockSpec(memory_space=pl.ANY)
BF16, F32 = jnp.bfloat16, jnp.float32


def hop(value, axis, size, step):
    return lax.ppermute(value, axis, [(at, at ^ step) for at in range(size)])


def far_rows(value, axis, size):
    values, held, step = [value], [[0]], size // 2
    while step > 1:
        if len(values) > 1:
            values, held = [jnp.concatenate(values)], [held[0] + held[1]]
        values.append(hop(values[0], axis, size, step))
        held.append([have ^ step for have in held[0]])
        step //= 2
    return values, held


def near_rows(values, held, axis, size):
    others = [hop(value, axis, size, 1) for value in values]
    return values + others, held + [[have ^ 1 for have in steps] for steps in held]


def transposed_dot(left, right):
    return lax.dot_general(left, right, (((0,), (0,)), ((), ())), preferred_element_type=F32)


def take(refs, count):
    return list(refs[:count]), list(refs[count:])


def shape(*dims):
    return jax.ShapeDtypeStruct(dims, BF16)


def call(kernel, outs, scratch, small, arrays, out_spec=VMEM, flops=0, aliases={}):
    size = sum(value.size * value.dtype.itemsize for value in (*arrays, *outs))
    return list(pl.pallas_call(
        kernel,
        out_shape=outs,
        in_specs=[SMEM] * len(small) + [VMEM] * len(arrays),
        out_specs=[out_spec] * len(outs),
        scratch_shapes=scratch,
        input_output_aliases=aliases,
        cost_estimate=pl.CostEstimate(flops=flops, bytes_accessed=size, transcendentals=0),
        compiler_params=pltpu.CompilerParams(vmem_limit_bytes=16 * 1024 * 1024),
    )(*small, *arrays))


def row_blocks(refs, held, block):
    return [
        (ref, at * block, step)
        for ref, steps in zip(refs, held, strict=True) for at, step in enumerate(steps)
    ]


def fill_inverse(target, found, offset, draw):
    rows = target.shape[1] // len(found)
    for ref, at, step in found:
        start = pl.multiple_of((draw ^ step) * rows, rows)
        for node in range(target.shape[0]):
            first = at + offset + node * rows
            target[node, pl.ds(start, rows), :] = ref[first:first + rows, :]


def first_kernel(held, picks, noise, *refs):
    parts, (_, *solved, inv) = take(refs, len(held))
    solved, (*sends, _) = take(solved, CHUNKS)
    myself, draw = lax.axis_index("leaf"), lax.axis_index("draw")
    nodes, wide = noise.shape[0], solved[0].shape[-1]
    draws = sum(map(len, held))
    rows = inv.shape[1] // draws
    fill_inverse(inv, row_blocks(parts, held, nodes * rows), 0, draw)
    for at, target in enumerate(solved):
        for node in range(nodes):
            right = noise[node, :, at * wide:(at + 1) * wide]
            target[node] = transposed_dot(inv[node], right).astype(BF16)
    for step, send in enumerate(sends, 1):
        node = picks[0, myself ^ step, myself]
        for at, target in enumerate(solved):
            send[at] = target[node]


def relay_kernel(half, source, late, waits, through, picks, far, *refs):
    own, refs = take(refs, bool(late))
    sends = refs[waits + through:len(refs) - through]
    myself = lax.axis_index("leaf")
    for step, send in enumerate(sends, 1):
        send[0] = far[picks[source, myself ^ step, myself ^ half]]
        if step >= half - late:
            send[1] = own[0][picks[source, myself ^ step, myself]]


def level_kernel(
    level, owners, held, width, chunk, places, stored, sides, mates,
    picks, lists, counts, noise, *refs,
):
    half = owners // 2
    packs, refs = take(refs, len(held))
    known, refs = take(refs, level * owners)
    done, refs = take(refs, len(stored))
    chunks, refs = take(refs, mates)
    target, *refs = refs
    sends, (table, inv, *refs) = take(refs, sides)
    myself, draw = lax.axis_index("leaf"), lax.axis_index("draw")
    levels, nodes = noise.shape[:2]
    wide = table.shape[-1]
    columns = slice(chunk * wide, (chunk + 1) * wide)
    depth = inv.shape[1]
    rows = depth // sum(map(len, held))
    span = nodes * (width * depth + rows)
    found = row_blocks(packs, held, (levels - 1) * span)
    offset = (level - 1) * span
    copies = []
    solved = target
    if done:
        solved, sems = refs
        for at, (ref, (into, first)) in enumerate(zip(done, stored, strict=True)):
            here = target.at[into, :, :, pl.ds(first, ref.shape[-1])]
            copies.append(pltpu.make_async_copy(ref, here, sems.at[at]))
            copies[-1].start()
    for at, (ref, place) in enumerate(zip(known, places, strict=True)):
        step = at % owners
        if step % half == 0:
            place = picks[at // owners, myself, myself ^ step]
        table[at] = ref[place] if ref.shape[-1] == wide else ref[place, :, columns]
    empty = level * owners
    table[empty] = jnp.zeros_like(table[empty])
    fill_inverse(inv, found, offset + nodes * width * depth, draw)
    for node in range(nodes):
        total = None
        for pack, start, step in found:
            for slot in range(width):
                entry = (draw ^ step) * width + slot
                live = entry < counts[level - 1, node]
                entry = jnp.where(live, lists[level - 1, node, entry] ^ myself, empty)
                at = start + offset + (node * width + slot) * depth
                term = transposed_dot(pack[at:at + depth, :], table[entry])
                total = term if total is None else total + term
        right_side = (noise[level, node, :, columns].astype(F32) - total).astype(BF16)
        solved[node] = transposed_dot(inv[node], right_side).astype(BF16)
    for step, send in enumerate(sends, 1):
        node = picks[level, myself ^ step, myself]
        for at, ref in enumerate([*chunks, solved]):
            send[at] = ref[node]
    if done:
        here = target.at[level, :, :, pl.ds(chunk * wide, wide)]
        copies.append(pltpu.make_async_copy(solved, here, sems.at[len(done)]))
        copies[-1].start()
    for copy in copies:
        copy.wait()


def on_device(owners, draws, noise, inverse, coupling, picks, lists, counts):
    levels, nodes, rows, columns = noise.shape
    wide, half, chunks = columns // CHUNKS, owners // 2, range(CHUNKS)
    width = coupling.shape[2]
    part = shape(nodes, rows, wide)
    flat = lambda value: value.reshape(-1, rows)
    leaf = lambda value, step: hop(value, "leaf", owners, step)
    near = lambda values: [leaf(value, step) for step, value in enumerate(values, 1)]
    inv_here = pltpu.VMEM((nodes, rows, rows), BF16)
    dot_flops = 2 * rows * rows * wide

    raw = jnp.concatenate([
        flat(value) for level in range(1, levels) for value in (coupling[level - 1], inverse[level])
    ])
    values, steps = far_rows(flat(inverse[0]), "draw", draws)
    values, steps = near_rows(values, steps, "draw", draws)
    late = 1
    *solved, raw = call(
        functools.partial(first_kernel, steps),
        [part] * CHUNKS + [shape(CHUNKS, rows, wide)] * (half - 1 - late) + [shape(*raw.shape)],
        [inv_here],
        (picks,),
        (noise[0], *values, raw),
        flops=nodes * CHUNKS * dot_flops,
        aliases={2 + len(values): CHUNKS + half - 1 - late},
    )
    solved, sends = take(solved, CHUNKS)
    far, got = [leaf(value, half) for value in solved], near(sends)
    values, steps = far_rows(raw, "draw", draws)
    pieces, done = [[]], [(value, (0, at * wide)) for at, value in enumerate(solved)]
    for at in chunks:
        waits, through = (got, []) if at == 0 else ([], values)
        sends = call(
            functools.partial(relay_kernel, half, 0, late, len(waits), len(through)),
            [shape(1, rows, wide)] * (half - 1 - late) + [shape(2, rows, wide)] * late
            + [shape(*value.shape) for value in through],
            [],
            (picks,),
            (far[at], solved[at], *waits, *through),
            aliases={3 + len(waits) + to: half - 1 + to for to in range(len(through))},
        )
        sends, through = take(sends, half - 1)
        distant = near(sends)
        pieces[0].append([
            (solved[at], 0), *((ref, at) for ref in got), *((ref, 1) for ref in distant[-late:]),
            (far[at], 0), *((ref, 0) for ref in distant),
        ])
    packs, steps = near_rows(through, steps, "draw", draws)

    for level in range(1, levels):
        last_level = level == levels - 1
        solved, sends = [], []
        for at in chunks:
            ends = at == CHUNKS - 1 and not last_level
            sides, mates = (half - 1, list(solved)) if ends else (0, [])
            final = last_level and at == CHUNKS - 1
            known = [entry for below in range(level) for entry in pieces[below][at]]
            stored = done if final else []
            scratch = [pltpu.VMEM((level * owners + 1, rows, wide), BF16), inv_here]
            if final:
                scratch += [
                    pltpu.VMEM((nodes, rows, wide), BF16),
                    pltpu.SemaphoreType.DMA((len(stored) + 1,)),
                ]
            here, *sent = call(
                functools.partial(
                    level_kernel, level, owners, steps, width, at,
                    [place for _, place in known], [place for _, place in stored], sides, len(mates),
                ),
                [shape(*noise.shape) if final else part] + [shape(CHUNKS, rows, wide)] * sides,
                scratch,
                (picks, lists, counts),
                (noise, *packs, *(ref for ref, _ in known), *(ref for ref, _ in stored), *mates),
                out_spec=ANY if final else VMEM,
                flops=nodes * (draws * width + 1) * dot_flops,
            )
            solved.append(here)
            done.append((here, (level, at * wide)))
            sends += sent
        if last_level:
            return here
        far = [leaf(value, half) for value in solved]
        got = near(sends)
        pieces.append([])
        for at in chunks:
            waits = got if at == CHUNKS - 1 else []
            sends = call(
                functools.partial(relay_kernel, half, level, 0, len(waits), 0),
                [shape(1, rows, wide)] * (half - 1),
                [],
                (picks,),
                (far[at], *waits),
            )
            pieces[level].append([
                (solved[at], 0), *((ref, at) for ref in got),
                (far[at], 0), *((ref, 0) for ref in near(sends)),
            ])


def solution(mesh):
    placed = (
        P(None, "leaf", None, "draw"),
        P(None, "leaf", "draw", None),
        P(None, "leaf", "draw", None, None),
        P(),
        P(None, "leaf", None),
        P(None, "leaf"),
    )
    return jax.shard_map(
        functools.partial(on_device, mesh.shape["leaf"], mesh.shape["draw"]),
        mesh=mesh,
        in_specs=placed,
        out_specs=P(None, "leaf", None, "draw"),
        check_vma=False,
    )
```

```python
import functools

import jax
import jax.numpy as jnp
from jax import lax
from jax.experimental import pallas as pl
from jax.experimental.pallas import tpu as pltpu
from jax.sharding import PartitionSpec as P

CHUNKS = 2
VMEM = pl.BlockSpec(memory_space=pltpu.VMEM)
SMEM = pl.BlockSpec(memory_space=pltpu.SMEM)
ANY = pl.BlockSpec(memory_space=pl.ANY)
BF16, F32 = jnp.bfloat16, jnp.float32


def hop(value, axis, size, step):
    return lax.ppermute(value, axis, [(at, at ^ step) for at in range(size)])


def far_rows(value, axis, size):
    values, held, step = [value], [[0]], size // 2
    while step > 1:
        if len(values) > 1:
            values, held = [jnp.concatenate(values)], [held[0] + held[1]]
        values.append(hop(values[0], axis, size, step))
        held.append([have ^ step for have in held[0]])
        step //= 2
    return values, held


def near_rows(values, held, axis, size):
    others = [hop(value, axis, size, 1) for value in values]
    return values + others, held + [[have ^ 1 for have in steps] for steps in held]


def transposed_dot(left, right):
    return lax.dot_general(left, right, (((0,), (0,)), ((), ())), preferred_element_type=F32)


def take(refs, count):
    return list(refs[:count]), list(refs[count:])


def shape(*dims):
    return jax.ShapeDtypeStruct(dims, BF16)


def call(kernel, outs, scratch, small, arrays, out_spec=VMEM, flops=0, aliases={}):
    size = sum(value.size * value.dtype.itemsize for value in (*arrays, *outs))
    return list(pl.pallas_call(
        kernel,
        out_shape=outs,
        in_specs=[SMEM] * len(small) + [VMEM] * len(arrays),
        out_specs=[out_spec] * len(outs),
        scratch_shapes=scratch,
        input_output_aliases=aliases,
        cost_estimate=pl.CostEstimate(flops=flops, bytes_accessed=size, transcendentals=0),
        compiler_params=pltpu.CompilerParams(vmem_limit_bytes=16 * 1024 * 1024),
    )(*small, *arrays))


def row_blocks(refs, held, block):
    return [
        (ref, at * block, step)
        for ref, steps in zip(refs, held, strict=True) for at, step in enumerate(steps)
    ]


def fill_inverse(target, found, offset, draw):
    rows = target.shape[1] // len(found)
    for ref, at, step in found:
        start = pl.multiple_of((draw ^ step) * rows, rows)
        for node in range(target.shape[0]):
            first = at + offset + node * rows
            target[node, pl.ds(start, rows), :] = ref[first:first + rows, :]


def first_kernel(held, picks, noise, *refs):
    parts, (_, *solved, inv) = take(refs, len(held))
    solved, (*sends, _) = take(solved, CHUNKS)
    myself, draw = lax.axis_index("leaf"), lax.axis_index("draw")
    nodes, wide = noise.shape[0], solved[0].shape[-1]
    draws = sum(map(len, held))
    rows = inv.shape[1] // draws
    fill_inverse(inv, row_blocks(parts, held, nodes * rows), 0, draw)
    for at, target in enumerate(solved):
        for node in range(nodes):
            right = noise[node, :, at * wide:(at + 1) * wide]
            target[node] = transposed_dot(inv[node], right).astype(BF16)
    for step, send in enumerate(sends, 1):
        node = picks[0, myself ^ step, myself]
        for at, target in enumerate(solved):
            send[at] = target[node]


def relay_kernel(half, source, late, waits, through, picks, far, *refs):
    own, refs = take(refs, bool(late))
    sends = refs[waits + through:len(refs) - through]
    myself = lax.axis_index("leaf")
    for step, send in enumerate(sends, 1):
        send[0] = far[picks[source, myself ^ step, myself ^ half]]
        if step >= half - late:
            send[1] = own[0][picks[source, myself ^ step, myself]]


def level_kernel(
    level, owners, held, width, chunk, places, stored, sides, mates,
    picks, lists, counts, noise, *refs,
):
    half = owners // 2
    packs, refs = take(refs, len(held))
    known, refs = take(refs, level * owners)
    done, refs = take(refs, len(stored))
    chunks, refs = take(refs, mates)
    target, *refs = refs
    sends, (table, inv, *refs) = take(refs, sides)
    myself, draw = lax.axis_index("leaf"), lax.axis_index("draw")
    levels, nodes = noise.shape[:2]
    wide = table.shape[-1]
    columns = slice(chunk * wide, (chunk + 1) * wide)
    depth = inv.shape[1]
    rows = depth // sum(map(len, held))
    span = nodes * (width * depth + rows)
    found = row_blocks(packs, held, (levels - 1) * span)
    offset = (level - 1) * span
    copies = []
    solved = target
    if done:
        solved, sems = refs
        for at, (ref, (into, first)) in enumerate(zip(done, stored, strict=True)):
            here = target.at[into, :, :, pl.ds(first, ref.shape[-1])]
            copies.append(pltpu.make_async_copy(ref, here, sems.at[at]))
            copies[-1].start()
    for at, (ref, place) in enumerate(zip(known, places, strict=True)):
        step = at % owners
        if step % half == 0:
            place = picks[at // owners, myself, myself ^ step]
        table[at] = ref[place] if ref.shape[-1] == wide else ref[place, :, columns]
    empty = level * owners
    table[empty] = jnp.zeros_like(table[empty])
    fill_inverse(inv, found, offset + nodes * width * depth, draw)
    for node in range(nodes):
        total = None
        for pack, start, step in found:
            for slot in range(width):
                entry = (draw ^ step) * width + slot
                live = entry < counts[level - 1, node]
                entry = jnp.where(live, lists[level - 1, node, entry] ^ myself, empty)
                at = start + offset + (node * width + slot) * depth
                term = transposed_dot(pack[at:at + depth, :], table[entry])
                total = term if total is None else total + term
        right_side = (noise[level, node, :, columns].astype(F32) - total).astype(BF16)
        solved[node] = transposed_dot(inv[node], right_side).astype(BF16)
    for step, send in enumerate(sends, 1):
        node = picks[level, myself ^ step, myself]
        for at, ref in enumerate([*chunks, solved]):
            send[at] = ref[node]
    if done:
        here = target.at[level, :, :, pl.ds(chunk * wide, wide)]
        copies.append(pltpu.make_async_copy(solved, here, sems.at[len(done)]))
        copies[-1].start()
    for copy in copies:
        copy.wait()


def on_device(owners, draws, noise, inverse, coupling, picks, lists, counts):
    levels, nodes, rows, columns = noise.shape
    wide, half, chunks = columns // CHUNKS, owners // 2, range(CHUNKS)
    width = coupling.shape[2]
    part = shape(nodes, rows, wide)
    flat = lambda value: value.reshape(-1, rows)
    leaf = lambda value, step: hop(value, "leaf", owners, step)
    near = lambda values: [leaf(value, step) for step, value in enumerate(values, 1)]
    inv_here = pltpu.VMEM((nodes, rows, rows), BF16)
    dot_flops = 2 * rows * rows * wide

    raw = jnp.concatenate([
        flat(value) for level in range(1, levels) for value in (coupling[level - 1], inverse[level])
    ])
    values, steps = far_rows(flat(inverse[0]), "draw", draws)
    values, steps = near_rows(values, steps, "draw", draws)
    late = 1
    *solved, raw = call(
        functools.partial(first_kernel, steps),
        [part] * CHUNKS + [shape(CHUNKS, rows, wide)] * (half - 1 - late) + [shape(*raw.shape)],
        [inv_here],
        (picks,),
        (noise[0], *values, raw),
        flops=nodes * CHUNKS * dot_flops,
        aliases={2 + len(values): CHUNKS + half - 1 - late},
    )
    solved, sends = take(solved, CHUNKS)
    got = near(sends)
    values, steps = far_rows(raw, "draw", draws)
    pieces = [[]]
    for at in chunks:
        far, later = leaf(solved[at], half), solved[at + 1:]
        waits, through = got if at == 0 else [], later or values
        sends = call(
            functools.partial(relay_kernel, half, 0, late, len(waits), len(through)),
            [shape(1, rows, wide)] * (half - 1 - late) + [shape(2, rows, wide)] * late
            + [shape(*value.shape) for value in through],
            [],
            (picks,),
            (far, solved[at], *waits, *through),
            aliases={3 + len(waits) + to: half - 1 + to for to in range(len(through))},
        )
        sends, through = take(sends, half - 1)
        distant = near(sends)
        if later:
            solved[at + 1:] = through
        pieces[0].append([
            (solved[at], 0), *((ref, at) for ref in got), *((ref, 1) for ref in distant[-late:]),
            (far, 0), *((ref, 0) for ref in distant),
        ])
    done = [(value, (0, at * wide)) for at, value in enumerate(solved)]
    packs, steps = near_rows(through, steps, "draw", draws)

    for level in range(1, levels):
        last_level = level == levels - 1
        solved, sends = [], []
        for at in chunks:
            ends = at == CHUNKS - 1 and not last_level
            sides, mates = (half - 1, list(solved)) if ends else (0, [])
            final = last_level and at == CHUNKS - 1
            known = [entry for below in range(level) for entry in pieces[below][at]]
            stored = done if final else []
            scratch = [pltpu.VMEM((level * owners + 1, rows, wide), BF16), inv_here]
            if final:
                scratch += [
                    pltpu.VMEM((nodes, rows, wide), BF16),
                    pltpu.SemaphoreType.DMA((len(stored) + 1,)),
                ]
            here, *sent = call(
                functools.partial(
                    level_kernel, level, owners, steps, width, at,
                    [place for _, place in known], [place for _, place in stored], sides, len(mates),
                ),
                [shape(*noise.shape) if final else part] + [shape(CHUNKS, rows, wide)] * sides,
                scratch,
                (picks, lists, counts),
                (noise, *packs, *(ref for ref, _ in known), *(ref for ref, _ in stored), *mates),
                out_spec=ANY if final else VMEM,
                flops=nodes * (draws * width + 1) * dot_flops,
            )
            solved.append(here)
            done.append((here, (level, at * wide)))
            sends += sent
        if last_level:
            return here
        far = [leaf(value, half) for value in solved]
        got = near(sends)
        pieces.append([])
        for at in chunks:
            waits = got if at == CHUNKS - 1 else []
            sends = call(
                functools.partial(relay_kernel, half, level, 0, len(waits), 0),
                [shape(1, rows, wide)] * (half - 1),
                [],
                (picks,),
                (far[at], *waits),
            )
            pieces[level].append([
                (solved[at], 0), *((ref, at) for ref in got),
                (far[at], 0), *((ref, 0) for ref in near(sends)),
            ])


def solution(mesh):
    placed = (
        P(None, "leaf", None, "draw"),
        P(None, "leaf", "draw", None),
        P(None, "leaf", "draw", None, None),
        P(),
        P(None, "leaf", None),
        P(None, "leaf"),
    )
    return jax.shard_map(
        functools.partial(on_device, mesh.shape["leaf"], mesh.shape["draw"]),
        mesh=mesh,
        in_specs=placed,
        out_specs=P(None, "leaf", None, "draw"),
        check_vma=False,
    )
```

```python
import functools

import jax
import jax.numpy as jnp
from jax import lax
from jax.experimental import pallas as pl
from jax.experimental.pallas import tpu as pltpu
from jax.sharding import PartitionSpec as P

CHUNKS = 2
VMEM = pl.BlockSpec(memory_space=pltpu.VMEM)
SMEM = pl.BlockSpec(memory_space=pltpu.SMEM)
ANY = pl.BlockSpec(memory_space=pl.ANY)
BF16, F32 = jnp.bfloat16, jnp.float32


def hop(value, axis, size, step):
    return lax.ppermute(value, axis, [(at, at ^ step) for at in range(size)])


def far_rows(value, axis, size):
    values, held, step = [value], [[0]], size // 2
    while step > 1:
        if len(values) > 1:
            values, held = [jnp.concatenate(values)], [held[0] + held[1]]
        values.append(hop(values[0], axis, size, step))
        held.append([have ^ step for have in held[0]])
        step //= 2
    return values, held


def near_rows(values, held, axis, size):
    others = [hop(value, axis, size, 1) for value in values]
    return values + others, held + [[have ^ 1 for have in steps] for steps in held]


def transposed_dot(left, right):
    return lax.dot_general(left, right, (((0,), (0,)), ((), ())), preferred_element_type=F32)


def take(refs, count):
    return list(refs[:count]), list(refs[count:])


def shape(*dims):
    return jax.ShapeDtypeStruct(dims, BF16)


def call(kernel, outs, scratch, small, arrays, out_spec=VMEM, flops=0, aliases={}):
    size = sum(value.size * value.dtype.itemsize for value in (*arrays, *outs))
    return list(pl.pallas_call(
        kernel,
        out_shape=outs,
        in_specs=[SMEM] * len(small) + [VMEM] * len(arrays),
        out_specs=[out_spec] * len(outs),
        scratch_shapes=scratch,
        input_output_aliases=aliases,
        cost_estimate=pl.CostEstimate(flops=flops, bytes_accessed=size, transcendentals=0),
        compiler_params=pltpu.CompilerParams(vmem_limit_bytes=16 * 1024 * 1024),
    )(*small, *arrays))


def row_blocks(refs, held, block):
    return [
        (ref, at * block, step)
        for ref, steps in zip(refs, held, strict=True) for at, step in enumerate(steps)
    ]


def fill_inverse(target, found, offset, draw):
    rows = target.shape[1] // len(found)
    for ref, at, step in found:
        start = pl.multiple_of((draw ^ step) * rows, rows)
        for node in range(target.shape[0]):
            first = at + offset + node * rows
            target[node, pl.ds(start, rows), :] = ref[first:first + rows, :]


def first_kernel(held, picks, noise, *refs):
    parts, (_, *solved, inv) = take(refs, len(held))
    solved, (*sends, _) = take(solved, CHUNKS)
    myself, draw = lax.axis_index("leaf"), lax.axis_index("draw")
    nodes, wide = noise.shape[0], solved[0].shape[-1]
    draws = sum(map(len, held))
    rows = inv.shape[1] // draws
    fill_inverse(inv, row_blocks(parts, held, nodes * rows), 0, draw)
    for at, target in enumerate(solved):
        for node in range(nodes):
            right = noise[node, :, at * wide:(at + 1) * wide]
            target[node] = transposed_dot(inv[node], right).astype(BF16)
    for step, send in enumerate(sends, 1):
        node = picks[0, myself ^ step, myself]
        for at, target in enumerate(solved):
            send[at] = target[node]


def relay_kernel(half, source, late, waits, through, picks, far, *refs):
    own, refs = take(refs, bool(late))
    sends = refs[waits + through:len(refs) - through]
    myself = lax.axis_index("leaf")
    for step, send in enumerate(sends, 1):
        send[0] = far[picks[source, myself ^ step, myself ^ half]]
        if step >= half - late:
            send[1] = own[0][picks[source, myself ^ step, myself]]


def level_kernel(
    level, owners, held, width, chunk, places, stored, sides, mates,
    picks, lists, counts, noise, *refs,
):
    half = owners // 2
    packs, refs = take(refs, len(held))
    known, refs = take(refs, level * owners)
    done, refs = take(refs, len(stored))
    chunks, refs = take(refs, mates)
    target, *refs = refs
    sends, (table, inv, *refs) = take(refs, sides)
    myself, draw = lax.axis_index("leaf"), lax.axis_index("draw")
    levels, nodes = noise.shape[:2]
    wide = table.shape[-1]
    columns = slice(chunk * wide, (chunk + 1) * wide)
    depth = inv.shape[1]
    rows = depth // sum(map(len, held))
    span = nodes * (width * depth + rows)
    found = row_blocks(packs, held, (levels - 1) * span)
    offset = (level - 1) * span
    copies = []
    solved = target
    if done:
        solved, sems = refs
        for at, (ref, (into, first)) in enumerate(zip(done, stored, strict=True)):
            here = target.at[into, :, :, pl.ds(first, ref.shape[-1])]
            copies.append(pltpu.make_async_copy(ref, here, sems.at[at]))
            copies[-1].start()
    for at, (ref, place) in enumerate(zip(known, places, strict=True)):
        step = at % owners
        if step % half == 0:
            place = picks[at // owners, myself, myself ^ step]
        table[at] = ref[place] if ref.shape[-1] == wide else ref[place, :, columns]
    empty = level * owners
    table[empty] = jnp.zeros_like(table[empty])
    fill_inverse(inv, found, offset + nodes * width * depth, draw)
    for node in range(nodes):
        total = None
        for pack, start, step in found:
            for slot in range(width):
                entry = (draw ^ step) * width + slot
                live = entry < counts[level - 1, node]
                entry = jnp.where(live, lists[level - 1, node, entry] ^ myself, empty)
                at = start + offset + (node * width + slot) * depth
                term = transposed_dot(pack[at:at + depth, :], table[entry])
                total = term if total is None else total + term
        right_side = (noise[level, node, :, columns].astype(F32) - total).astype(BF16)
        solved[node] = transposed_dot(inv[node], right_side).astype(BF16)
    for step, send in enumerate(sends, 1):
        node = picks[level, myself ^ step, myself]
        for at, ref in enumerate([*chunks, solved]):
            send[at] = ref[node]
    if done:
        here = target.at[level, :, :, pl.ds(chunk * wide, wide)]
        copies.append(pltpu.make_async_copy(solved, here, sems.at[len(done)]))
        copies[-1].start()
    for copy in copies:
        copy.wait()


def on_device(owners, draws, noise, inverse, coupling, picks, lists, counts):
    levels, nodes, rows, columns = noise.shape
    wide, half, chunks = columns // CHUNKS, owners // 2, range(CHUNKS)
    width = coupling.shape[2]
    part = shape(nodes, rows, wide)
    flat = lambda value: value.reshape(-1, rows)
    leaf = lambda value, step: hop(value, "leaf", owners, step)
    near = lambda values: [leaf(value, step) for step, value in enumerate(values, 1)]
    inv_here = pltpu.VMEM((nodes, rows, rows), BF16)
    dot_flops = 2 * rows * rows * wide

    raw = jnp.concatenate([
        flat(value) for level in range(1, levels) for value in (coupling[level - 1], inverse[level])
    ])
    values, steps = far_rows(flat(inverse[0]), "draw", draws)
    values, steps = near_rows(values, steps, "draw", draws)
    late = 1
    *solved, raw = call(
        functools.partial(first_kernel, steps),
        [part] * CHUNKS + [shape(CHUNKS, rows, wide)] * (half - 1 - late) + [shape(*raw.shape)],
        [inv_here],
        (picks,),
        (noise[0], *values, raw),
        flops=nodes * CHUNKS * dot_flops,
        aliases={2 + len(values): CHUNKS + half - 1 - late},
    )
    solved, sends = take(solved, CHUNKS)
    got = near(sends)
    values, steps = far_rows(raw, "draw", draws)
    pieces = [[]]
    for at in chunks:
        far, later = leaf(solved[at], half), solved[at + 1:]
        waits, through = distant if at else got, later or values
        sends = call(
            functools.partial(relay_kernel, half, 0, late, len(waits), len(through)),
            [shape(1, rows, wide)] * (half - 1 - late) + [shape(2, rows, wide)] * late
            + [shape(*value.shape) for value in through],
            [],
            (picks,),
            (far, solved[at], *waits, *through),
            aliases={3 + len(waits) + to: half - 1 + to for to in range(len(through))},
        )
        sends, through = take(sends, half - 1)
        distant = near(sends)
        if later:
            solved[at + 1:] = through
        pieces[0].append([
            (solved[at], 0), *((ref, at) for ref in got), *((ref, 1) for ref in distant[-late:]),
            (far, 0), *((ref, 0) for ref in distant),
        ])
    done = [(value, (0, at * wide)) for at, value in enumerate(solved)]
    packs, steps = near_rows(through, steps, "draw", draws)

    for level in range(1, levels):
        last_level = level == levels - 1
        solved, sends = [], []
        for at in chunks:
            ends = at == CHUNKS - 1 and not last_level
            sides, mates = (half - 1, list(solved)) if ends else (0, [])
            final = last_level and at == CHUNKS - 1
            known = [entry for below in range(level) for entry in pieces[below][at]]
            stored = done if final else []
            scratch = [pltpu.VMEM((level * owners + 1, rows, wide), BF16), inv_here]
            if final:
                scratch += [
                    pltpu.VMEM((nodes, rows, wide), BF16),
                    pltpu.SemaphoreType.DMA((len(stored) + 1,)),
                ]
            here, *sent = call(
                functools.partial(
                    level_kernel, level, owners, steps, width, at,
                    [place for _, place in known], [place for _, place in stored], sides, len(mates),
                ),
                [shape(*noise.shape) if final else part] + [shape(CHUNKS, rows, wide)] * sides,
                scratch,
                (picks, lists, counts),
                (noise, *packs, *(ref for ref, _ in known), *(ref for ref, _ in stored), *mates),
                out_spec=ANY if final else VMEM,
                flops=nodes * (draws * width + 1) * dot_flops,
            )
            solved.append(here)
            done.append((here, (level, at * wide)))
            sends += sent
        if last_level:
            return here
        far = [leaf(value, half) for value in solved]
        got = near(sends)
        pieces.append([])
        for at in chunks:
            waits = got if at == CHUNKS - 1 else []
            sends = call(
                functools.partial(relay_kernel, half, level, 0, len(waits), 0),
                [shape(1, rows, wide)] * (half - 1),
                [],
                (picks,),
                (far[at], *waits),
            )
            pieces[level].append([
                (solved[at], 0), *((ref, at) for ref in got),
                (far[at], 0), *((ref, 0) for ref in near(sends)),
            ])


def solution(mesh):
    placed = (
        P(None, "leaf", None, "draw"),
        P(None, "leaf", "draw", None),
        P(None, "leaf", "draw", None, None),
        P(),
        P(None, "leaf", None),
        P(None, "leaf"),
    )
    return jax.shard_map(
        functools.partial(on_device, mesh.shape["leaf"], mesh.shape["draw"]),
        mesh=mesh,
        in_specs=placed,
        out_specs=P(None, "leaf", None, "draw"),
        check_vma=False,
    )
```

```python
import functools

import jax
import jax.numpy as jnp
from jax import lax
from jax.experimental import pallas as pl
from jax.experimental.pallas import tpu as pltpu
from jax.sharding import PartitionSpec as P

CHUNKS = 2
VMEM = pl.BlockSpec(memory_space=pltpu.VMEM)
SMEM = pl.BlockSpec(memory_space=pltpu.SMEM)
ANY = pl.BlockSpec(memory_space=pl.ANY)
BF16, F32 = jnp.bfloat16, jnp.float32


def hop(value, axis, size, step):
    return lax.ppermute(value, axis, [(at, at ^ step) for at in range(size)])


def far_rows(value, axis, size):
    values, held, step = [value], [[0]], size // 2
    while step > 1:
        if len(values) > 1:
            values, held = [jnp.concatenate(values)], [held[0] + held[1]]
        values.append(hop(values[0], axis, size, step))
        held.append([have ^ step for have in held[0]])
        step //= 2
    return values, held


def near_rows(values, held, axis, size):
    others = [hop(value, axis, size, 1) for value in values]
    return values + others, held + [[have ^ 1 for have in steps] for steps in held]


def transposed_dot(left, right):
    return lax.dot_general(left, right, (((0,), (0,)), ((), ())), preferred_element_type=F32)


def take(refs, count):
    return list(refs[:count]), list(refs[count:])


def shape(*dims):
    return jax.ShapeDtypeStruct(dims, BF16)


def call(kernel, outs, scratch, small, arrays, out_spec=VMEM, flops=0, aliases={}):
    size = sum(value.size * value.dtype.itemsize for value in (*arrays, *outs))
    return list(pl.pallas_call(
        kernel,
        out_shape=outs,
        in_specs=[SMEM] * len(small) + [VMEM] * len(arrays),
        out_specs=[out_spec] * len(outs),
        scratch_shapes=scratch,
        input_output_aliases=aliases,
        cost_estimate=pl.CostEstimate(flops=flops, bytes_accessed=size, transcendentals=0),
        compiler_params=pltpu.CompilerParams(vmem_limit_bytes=16 * 1024 * 1024),
    )(*small, *arrays))


def row_blocks(refs, held, block):
    return [
        (ref, at * block, step)
        for ref, steps in zip(refs, held, strict=True) for at, step in enumerate(steps)
    ]


def fill_inverse(target, found, offset, draw):
    rows = target.shape[1] // len(found)
    for ref, at, step in found:
        start = pl.multiple_of((draw ^ step) * rows, rows)
        for node in range(target.shape[0]):
            first = at + offset + node * rows
            target[node, pl.ds(start, rows), :] = ref[first:first + rows, :]


def first_kernel(held, picks, noise, *refs):
    parts, (_, solved, *sends, _, inv) = take(refs, len(held))
    myself, draw = lax.axis_index("leaf"), lax.axis_index("draw")
    nodes = noise.shape[0]
    draws = sum(map(len, held))
    rows = inv.shape[1] // draws
    fill_inverse(inv, row_blocks(parts, held, nodes * rows), 0, draw)
    for node in range(nodes):
        solved[node] = transposed_dot(inv[node], noise[node]).astype(BF16)
    for step, send in enumerate(sends, 1):
        send[0] = solved[picks[0, myself ^ step, myself]]


def relay_kernel(half, source, waits, through, picks, far, *refs):
    sends = refs[waits + through:len(refs) - through]
    myself = lax.axis_index("leaf")
    for at, send in enumerate(sends):
        chunk, step = divmod(at, half - 1)
        wide = send.shape[-1]
        node = picks[source, myself ^ (step + 1), myself ^ half]
        send[0] = far[node, :, chunk * wide:(chunk + 1) * wide]


def level_kernel(
    level, owners, held, width, chunk, places, stored, sides, mates,
    picks, lists, counts, noise, *refs,
):
    half = owners // 2
    packs, refs = take(refs, len(held))
    known, refs = take(refs, level * owners)
    done, refs = take(refs, len(stored))
    chunks, refs = take(refs, mates)
    target, *refs = refs
    sends, (table, inv, *refs) = take(refs, sides)
    myself, draw = lax.axis_index("leaf"), lax.axis_index("draw")
    levels, nodes = noise.shape[:2]
    wide = table.shape[-1]
    columns = slice(chunk * wide, (chunk + 1) * wide)
    depth = inv.shape[1]
    rows = depth // sum(map(len, held))
    span = nodes * (width * depth + rows)
    found = row_blocks(packs, held, (levels - 1) * span)
    offset = (level - 1) * span
    copies = []
    solved = target
    if done:
        solved, sems = refs
        for at, (ref, (into, first)) in enumerate(zip(done, stored, strict=True)):
            here = target.at[into, :, :, pl.ds(first, ref.shape[-1])]
            copies.append(pltpu.make_async_copy(ref, here, sems.at[at]))
            copies[-1].start()
    for at, (ref, place) in enumerate(zip(known, places, strict=True)):
        step = at % owners
        if step % half == 0:
            place = picks[at // owners, myself, myself ^ step]
        table[at] = ref[place] if ref.shape[-1] == wide else ref[place, :, columns]
    empty = level * owners
    table[empty] = jnp.zeros_like(table[empty])
    fill_inverse(inv, found, offset + nodes * width * depth, draw)
    for node in range(nodes):
        total = None
        for pack, start, step in found:
            for slot in range(width):
                entry = (draw ^ step) * width + slot
                live = entry < counts[level - 1, node]
                entry = jnp.where(live, lists[level - 1, node, entry] ^ myself, empty)
                at = start + offset + (node * width + slot) * depth
                term = transposed_dot(pack[at:at + depth, :], table[entry])
                total = term if total is None else total + term
        right_side = (noise[level, node, :, columns].astype(F32) - total).astype(BF16)
        solved[node] = transposed_dot(inv[node], right_side).astype(BF16)
    for step, send in enumerate(sends, 1):
        node = picks[level, myself ^ step, myself]
        for at, ref in enumerate([*chunks, solved]):
            send[at] = ref[node]
    if done:
        here = target.at[level, :, :, pl.ds(chunk * wide, wide)]
        copies.append(pltpu.make_async_copy(solved, here, sems.at[len(done)]))
        copies[-1].start()
    for copy in copies:
        copy.wait()


def on_device(owners, draws, noise, inverse, coupling, picks, lists, counts):
    levels, nodes, rows, columns = noise.shape
    wide, half, chunks = columns // CHUNKS, owners // 2, range(CHUNKS)
    width = coupling.shape[2]
    part = shape(nodes, rows, wide)
    flat = lambda value: value.reshape(-1, rows)
    leaf = lambda value, step: hop(value, "leaf", owners, step)
    near = lambda values: [leaf(value, step) for step, value in enumerate(values, 1)]
    inv_here = pltpu.VMEM((nodes, rows, rows), BF16)
    dot_flops = 2 * rows * rows * wide

    raw = jnp.concatenate([
        flat(value) for level in range(1, levels) for value in (coupling[level - 1], inverse[level])
    ])
    values, steps = far_rows(flat(inverse[0]), "draw", draws)
    values, steps = near_rows(values, steps, "draw", draws)
    solved, *sends, raw = call(
        functools.partial(first_kernel, steps),
        [shape(nodes, rows, columns)] + [shape(1, rows, columns)] * (half - 1) + [shape(*raw.shape)],
        [inv_here],
        (picks,),
        (noise[0], *values, raw),
        flops=nodes * CHUNKS * dot_flops,
        aliases={2 + len(values): half},
    )
    far, got = leaf(solved, half), near(sends)
    values, steps = far_rows(raw, "draw", draws)
    sends = call(
        functools.partial(relay_kernel, half, 0, 0, len(values)),
        [shape(1, rows, wide)] * (CHUNKS * (half - 1)) + [shape(*value.shape) for value in values],
        [],
        (picks,),
        (far, *values),
        aliases={2 + at: CHUNKS * (half - 1) + at for at in range(len(values))},
    )
    sends, values = take(sends, CHUNKS * (half - 1))
    packs, steps = near_rows(values, steps, "draw", draws)
    pieces, done = [[]], [(solved, (0, 0))]
    for at in chunks:
        distant, sends = take(sends, half - 1)
        pieces[0].append([
            (solved, 0), *((ref, 0) for ref in got),
            (far, 0), *((ref, 0) for ref in near(distant)),
        ])

    for level in range(1, levels):
        last_level = level == levels - 1
        solved, sends = [], []
        for at in chunks:
            ends = at == CHUNKS - 1 and not last_level
            sides, mates = (half - 1, list(solved)) if ends else (0, [])
            final = last_level and at == CHUNKS - 1
            known = [entry for below in range(level) for entry in pieces[below][at]]
            stored = done if final else []
            scratch = [pltpu.VMEM((level * owners + 1, rows, wide), BF16), inv_here]
            if final:
                scratch += [
                    pltpu.VMEM((nodes, rows, wide), BF16),
                    pltpu.SemaphoreType.DMA((len(stored) + 1,)),
                ]
            here, *sent = call(
                functools.partial(
                    level_kernel, level, owners, steps, width, at,
                    [place for _, place in known], [place for _, place in stored], sides, len(mates),
                ),
                [shape(*noise.shape) if final else part] + [shape(CHUNKS, rows, wide)] * sides,
                scratch,
                (picks, lists, counts),
                (noise, *packs, *(ref for ref, _ in known), *(ref for ref, _ in stored), *mates),
                out_spec=ANY if final else VMEM,
                flops=nodes * (draws * width + 1) * dot_flops,
            )
            solved.append(here)
            done.append((here, (level, at * wide)))
            sends += sent
        if last_level:
            return here
        far = [leaf(value, half) for value in solved]
        got = near(sends)
        pieces.append([])
        for at in chunks:
            waits = got if at == CHUNKS - 1 else []
            sends = call(
                functools.partial(relay_kernel, half, level, len(waits), 0),
                [shape(1, rows, wide)] * (half - 1),
                [],
                (picks,),
                (far[at], *waits),
            )
            pieces[level].append([
                (solved[at], 0), *((ref, at) for ref in got),
                (far[at], 0), *((ref, 0) for ref in near(sends)),
            ])


def solution(mesh):
    placed = (
        P(None, "leaf", None, "draw"),
        P(None, "leaf", "draw", None),
        P(None, "leaf", "draw", None, None),
        P(),
        P(None, "leaf", None),
        P(None, "leaf"),
    )
    return jax.shard_map(
        functools.partial(on_device, mesh.shape["leaf"], mesh.shape["draw"]),
        mesh=mesh,
        in_specs=placed,
        out_specs=P(None, "leaf", None, "draw"),
        check_vma=False,
    )
```

```python
import functools

import jax
import jax.numpy as jnp
from jax import lax
from jax.experimental import pallas as pl
from jax.experimental.pallas import tpu as pltpu
from jax.sharding import PartitionSpec as P

CHUNKS = 2
VMEM = pl.BlockSpec(memory_space=pltpu.VMEM)
SMEM = pl.BlockSpec(memory_space=pltpu.SMEM)
ANY = pl.BlockSpec(memory_space=pl.ANY)
BF16, F32 = jnp.bfloat16, jnp.float32


def hop(value, axis, size, step):
    return lax.ppermute(value, axis, [(at, at ^ step) for at in range(size)])


def far_rows(value, axis, size):
    values, held, step = [value], [[0]], size // 2
    while step > 1:
        if len(values) > 1:
            values, held = [jnp.concatenate(values)], [held[0] + held[1]]
        values.append(hop(values[0], axis, size, step))
        held.append([have ^ step for have in held[0]])
        step //= 2
    return values, held


def near_rows(values, held, axis, size):
    others = [hop(value, axis, size, 1) for value in values]
    return values + others, held + [[have ^ 1 for have in steps] for steps in held]


def transposed_dot(left, right):
    return lax.dot_general(left, right, (((0,), (0,)), ((), ())), preferred_element_type=F32)


def take(refs, count):
    return list(refs[:count]), list(refs[count:])


def shape(*dims):
    return jax.ShapeDtypeStruct(dims, BF16)


def call(kernel, outs, scratch, small, arrays, out_spec=VMEM, flops=0, aliases={}):
    size = sum(value.size * value.dtype.itemsize for value in (*arrays, *outs))
    return list(pl.pallas_call(
        kernel,
        out_shape=outs,
        in_specs=[SMEM] * len(small) + [VMEM] * len(arrays),
        out_specs=[out_spec] * len(outs),
        scratch_shapes=scratch,
        input_output_aliases=aliases,
        cost_estimate=pl.CostEstimate(flops=flops, bytes_accessed=size, transcendentals=0),
        compiler_params=pltpu.CompilerParams(vmem_limit_bytes=16 * 1024 * 1024),
    )(*small, *arrays))


def row_blocks(refs, held, block):
    return [
        (ref, at * block, step)
        for ref, steps in zip(refs, held, strict=True) for at, step in enumerate(steps)
    ]


def fill_inverse(target, found, offset, draw):
    rows = target.shape[1] // len(found)
    for ref, at, step in found:
        start = pl.multiple_of((draw ^ step) * rows, rows)
        for node in range(target.shape[0]):
            first = at + offset + node * rows
            target[node, pl.ds(start, rows), :] = ref[first:first + rows, :]


def first_kernel(held, picks, noise, *refs):
    parts, (_, solved, *sends, _, inv) = take(refs, len(held))
    myself, draw = lax.axis_index("leaf"), lax.axis_index("draw")
    nodes = noise.shape[0]
    draws = sum(map(len, held))
    rows = inv.shape[1] // draws
    fill_inverse(inv, row_blocks(parts, held, nodes * rows), 0, draw)
    for node in range(nodes):
        solved[node] = transposed_dot(inv[node], noise[node]).astype(BF16)
    for step, send in enumerate(sends, 1):
        send[0] = solved[picks[0, myself ^ step, myself]]


def relay_kernel(half, source, waits, through, picks, far, *refs):
    sends = refs[waits + through:len(refs) - through]
    myself = lax.axis_index("leaf")
    for at, send in enumerate(sends):
        chunk, step = divmod(at, half - 1)
        wide = send.shape[-1]
        node = picks[source, myself ^ (step + 1), myself ^ half]
        send[0] = far[node, :, chunk * wide:(chunk + 1) * wide]


def inverse_kernel(held, span, *refs):
    packs, refs = take(refs, len(held))
    draw = lax.axis_index("draw")
    levels = sum(ref.shape[0] > 1 for ref in refs)
    draws = sum(map(len, held))
    found = row_blocks(packs, held, levels * span)
    for level, target in enumerate(refs[-levels:]):
        nodes, rows = target.shape[0], target.shape[1] // draws
        fill_inverse(target, found, (level + 1) * span - nodes * rows, draw)


def level_kernel(
    level, owners, held, width, chunk, places, stored, sides, mates,
    picks, lists, counts, noise, inv, *refs,
):
    half = owners // 2
    packs, refs = take(refs, len(held))
    known, refs = take(refs, level * owners)
    done, refs = take(refs, len(stored))
    chunks, refs = take(refs, mates)
    target, *refs = refs
    sends, (table, *refs) = take(refs, sides)
    myself, draw = lax.axis_index("leaf"), lax.axis_index("draw")
    levels, nodes = noise.shape[:2]
    wide = table.shape[-1]
    columns = slice(chunk * wide, (chunk + 1) * wide)
    depth = inv.shape[1]
    rows = depth // sum(map(len, held))
    span = nodes * (width * depth + rows)
    found = row_blocks(packs, held, (levels - 1) * span)
    offset = (level - 1) * span
    copies = []
    solved = target
    if done:
        solved, sems = refs
        for at, (ref, (into, first)) in enumerate(zip(done, stored, strict=True)):
            here = target.at[into, :, :, pl.ds(first, ref.shape[-1])]
            copies.append(pltpu.make_async_copy(ref, here, sems.at[at]))
            copies[-1].start()
    for at, (ref, place) in enumerate(zip(known, places, strict=True)):
        step = at % owners
        if step % half == 0:
            place = picks[at // owners, myself, myself ^ step]
        table[at] = ref[place] if ref.shape[-1] == wide else ref[place, :, columns]
    empty = level * owners
    table[empty] = jnp.zeros_like(table[empty])
    for node in range(nodes):
        total = None
        for pack, start, step in found:
            for slot in range(width):
                entry = (draw ^ step) * width + slot
                live = entry < counts[level - 1, node]
                entry = jnp.where(live, lists[level - 1, node, entry] ^ myself, empty)
                at = start + offset + (node * width + slot) * depth
                term = transposed_dot(pack[at:at + depth, :], table[entry])
                total = term if total is None else total + term
        right_side = (noise[level, node, :, columns].astype(F32) - total).astype(BF16)
        solved[node] = transposed_dot(inv[node], right_side).astype(BF16)
    for step, send in enumerate(sends, 1):
        node = picks[level, myself ^ step, myself]
        for at, ref in enumerate([*chunks, solved]):
            send[at] = ref[node]
    if done:
        here = target.at[level, :, :, pl.ds(chunk * wide, wide)]
        copies.append(pltpu.make_async_copy(solved, here, sems.at[len(done)]))
        copies[-1].start()
    for copy in copies:
        copy.wait()


def on_device(owners, draws, noise, inverse, coupling, picks, lists, counts):
    levels, nodes, rows, columns = noise.shape
    wide, half, chunks = columns // CHUNKS, owners // 2, range(CHUNKS)
    width = coupling.shape[2]
    part = shape(nodes, rows, wide)
    flat = lambda value: value.reshape(-1, rows)
    leaf = lambda value, step: hop(value, "leaf", owners, step)
    near = lambda values: [leaf(value, step) for step, value in enumerate(values, 1)]
    inv_here = pltpu.VMEM((nodes, rows, rows), BF16)
    dot_flops = 2 * rows * rows * wide

    raw = jnp.concatenate([
        flat(value) for level in range(1, levels) for value in (coupling[level - 1], inverse[level])
    ])
    values, steps = far_rows(flat(inverse[0]), "draw", draws)
    values, steps = near_rows(values, steps, "draw", draws)
    solved, *sends, raw = call(
        functools.partial(first_kernel, steps),
        [shape(nodes, rows, columns)] + [shape(1, rows, columns)] * (half - 1) + [shape(*raw.shape)],
        [inv_here],
        (picks,),
        (noise[0], *values, raw),
        flops=nodes * CHUNKS * dot_flops,
        aliases={2 + len(values): half},
    )
    far, got = leaf(solved, half), near(sends)
    values, steps = far_rows(raw, "draw", draws)
    sends = call(
        functools.partial(relay_kernel, half, 0, len(got), len(values)),
        [shape(1, rows, wide)] * (CHUNKS * (half - 1)) + [shape(*value.shape) for value in values],
        [],
        (picks,),
        (far, *got, *values),
        aliases={2 + len(got) + at: CHUNKS * (half - 1) + at for at in range(len(values))},
    )
    sends, values = take(sends, CHUNKS * (half - 1))
    packs, steps = near_rows(values, steps, "draw", draws)
    first, later = take(sends, half - 1)
    span = nodes * (width * rows + inverse.shape[2])
    outs = call(
        functools.partial(inverse_kernel, steps, span),
        [shape(*value.shape) for value in later] + [shape(nodes, rows, rows)] * (levels - 1),
        [],
        (),
        (*packs, *later),
        aliases={len(packs) + at: at for at in range(len(later))},
    )
    later, inverses = take(outs, len(later))
    sends = first + later
    pieces, done = [[]], [(solved, (0, 0))]
    for at in chunks:
        distant, sends = take(sends, half - 1)
        pieces[0].append([
            (solved, 0), *((ref, 0) for ref in got),
            (far, 0), *((ref, 0) for ref in near(distant)),
        ])

    for level in range(1, levels):
        last_level = level == levels - 1
        solved, sends = [], []
        for at in chunks:
            ends = at == CHUNKS - 1 and not last_level
            sides, mates = (half - 1, list(solved)) if ends else (0, [])
            final = last_level and at == CHUNKS - 1
            known = [entry for below in range(level) for entry in pieces[below][at]]
            stored = done if final else []
            scratch = [pltpu.VMEM((level * owners + 1, rows, wide), BF16)]
            if final:
                scratch += [
                    pltpu.VMEM((nodes, rows, wide), BF16),
                    pltpu.SemaphoreType.DMA((len(stored) + 1,)),
                ]
            here, *sent = call(
                functools.partial(
                    level_kernel, level, owners, steps, width, at,
                    [place for _, place in known], [place for _, place in stored], sides, len(mates),
                ),
                [shape(*noise.shape) if final else part] + [shape(CHUNKS, rows, wide)] * sides,
                scratch,
                (picks, lists, counts),
                (noise, inverses[level - 1], *packs, *(ref for ref, _ in known), *(ref for ref, _ in stored), *mates),
                out_spec=ANY if final else VMEM,
                flops=nodes * (draws * width + 1) * dot_flops,
            )
            solved.append(here)
            done.append((here, (level, at * wide)))
            sends += sent
        if last_level:
            return here
        far = [leaf(value, half) for value in solved]
        got = near(sends)
        pieces.append([])
        for at in chunks:
            waits = got if at == CHUNKS - 1 else []
            sends = call(
                functools.partial(relay_kernel, half, level, len(waits), 0),
                [shape(1, rows, wide)] * (half - 1),
                [],
                (picks,),
                (far[at], *waits),
            )
            pieces[level].append([
                (solved[at], 0), *((ref, at) for ref in got),
                (far[at], 0), *((ref, 0) for ref in near(sends)),
            ])


def solution(mesh):
    placed = (
        P(None, "leaf", None, "draw"),
        P(None, "leaf", "draw", None),
        P(None, "leaf", "draw", None, None),
        P(),
        P(None, "leaf", None),
        P(None, "leaf"),
    )
    return jax.shard_map(
        functools.partial(on_device, mesh.shape["leaf"], mesh.shape["draw"]),
        mesh=mesh,
        in_specs=placed,
        out_specs=P(None, "leaf", None, "draw"),
        check_vma=False,
    )
```

```python
import functools

import jax
import jax.numpy as jnp
from jax import lax
from jax.experimental import pallas as pl
from jax.experimental.pallas import tpu as pltpu
from jax.sharding import PartitionSpec as P

CHUNKS = 2
VMEM = pl.BlockSpec(memory_space=pltpu.VMEM)
ANY = pl.BlockSpec(memory_space=pl.ANY)
BF16, F32 = jnp.bfloat16, jnp.float32


def hop(value, axis, size, step):
    return lax.ppermute(value, axis, [(at, at ^ step) for at in range(size)])


def far_rows(value, axis, size):
    values, held, step = [value], [[0]], size // 2
    while step > 1:
        if len(values) > 1:
            values, held = [jnp.concatenate(values)], [held[0] + held[1]]
        values.append(hop(values[0], axis, size, step))
        held.append([have ^ step for have in held[0]])
        step //= 2
    return values, held


def near_rows(values, held, axis, size):
    others = [hop(value, axis, size, 1) for value in values]
    return values + others, held + [[have ^ 1 for have in steps] for steps in held]


def transposed_dot(left, right):
    return lax.dot_general(left, right, (((0,), (0,)), ((), ())), preferred_element_type=F32)


def take(refs, count):
    return list(refs[:count]), list(refs[count:])


def shape(*dims):
    return jax.ShapeDtypeStruct(dims, BF16)


def entry_of(tile, row, column):
    rows = lax.broadcasted_iota(jnp.int32, tile.shape, 0)
    columns = lax.broadcasted_iota(jnp.int32, tile.shape, 1)
    return jnp.sum(jnp.where((rows == row) & (columns == column), tile, 0))


def call(kernel, outs, scratch, arrays, out_spec=VMEM, flops=0, aliases={}):
    size = sum(value.size * value.dtype.itemsize for value in (*arrays, *outs))
    return list(pl.pallas_call(
        kernel,
        out_shape=outs,
        in_specs=[VMEM] * len(arrays),
        out_specs=[out_spec] * len(outs),
        scratch_shapes=scratch,
        input_output_aliases=aliases,
        cost_estimate=pl.CostEstimate(flops=flops, bytes_accessed=size, transcendentals=0),
        compiler_params=pltpu.CompilerParams(vmem_limit_bytes=16 * 1024 * 1024),
    )(*arrays))


def row_blocks(refs, held, block):
    return [
        (ref, at * block, step)
        for ref, steps in zip(refs, held, strict=True) for at, step in enumerate(steps)
    ]


def fill_inverse(target, found, offset, draw):
    rows = target.shape[1] // len(found)
    for ref, at, step in found:
        start = pl.multiple_of((draw ^ step) * rows, rows)
        for node in range(target.shape[0]):
            first = at + offset + node * rows
            target[node, pl.ds(start, rows), :] = ref[first:first + rows, :]


def first_kernel(held, picks, noise, *refs):
    parts, (_, solved, *sends, _, inv) = take(refs, len(held))
    myself, draw = lax.axis_index("leaf"), lax.axis_index("draw")
    nodes = noise.shape[0]
    draws = sum(map(len, held))
    rows = inv.shape[1] // draws
    fill_inverse(inv, row_blocks(parts, held, nodes * rows), 0, draw)
    for node in range(nodes):
        solved[node] = transposed_dot(inv[node], noise[node]).astype(BF16)
    for step, send in enumerate(sends, 1):
        send[0] = solved[entry_of(picks[0], myself ^ step, myself)]


def relay_kernel(half, source, waits, through, picks, far, *refs):
    sends = refs[waits + through:len(refs) - through]
    myself = lax.axis_index("leaf")
    for at, send in enumerate(sends):
        chunk, step = divmod(at, half - 1)
        wide = send.shape[-1]
        node = entry_of(picks[source], myself ^ (step + 1), myself ^ half)
        send[0] = far[node, :, chunk * wide:(chunk + 1) * wide]


def inverse_kernel(held, levels, span, *refs):
    packs, refs = take(refs, len(held))
    draw = lax.axis_index("draw")
    draws = sum(map(len, held))
    found = row_blocks(packs, held, levels * span)
    for level, target in enumerate(refs[-levels:]):
        nodes, rows = target.shape[0], target.shape[1] // draws
        fill_inverse(target, found, (level + 1) * span - nodes * rows, draw)


def level_kernel(
    level, owners, held, width, chunk, places, stored, sides, mates,
    picks, lists, counts, noise, inv, *refs,
):
    half = owners // 2
    packs, refs = take(refs, len(held))
    known, refs = take(refs, level * owners)
    done, refs = take(refs, len(stored))
    chunks, refs = take(refs, mates)
    target, *refs = refs
    sends, (table, *refs) = take(refs, sides)
    myself, draw = lax.axis_index("leaf"), lax.axis_index("draw")
    levels, nodes = noise.shape[:2]
    wide = table.shape[-1]
    columns = slice(chunk * wide, (chunk + 1) * wide)
    depth = inv.shape[1]
    rows = depth // sum(map(len, held))
    span = nodes * (width * depth + rows)
    found = row_blocks(packs, held, (levels - 1) * span)
    offset = (level - 1) * span
    copies = []
    solved = target
    if done:
        solved, sems = refs
        for at, (ref, (into, first)) in enumerate(zip(done, stored, strict=True)):
            here = target.at[into, :, :, pl.ds(first, ref.shape[-1])]
            copies.append(pltpu.make_async_copy(ref, here, sems.at[at]))
            copies[-1].start()
    for at, (ref, place) in enumerate(zip(known, places, strict=True)):
        step = at % owners
        if step % half == 0:
            place = entry_of(picks[at // owners], myself, myself ^ step)
        table[at] = ref[place] if ref.shape[-1] == wide else ref[place, :, columns]
    empty = level * owners
    table[empty] = jnp.zeros_like(table[empty])
    entries = lists[level - 1]
    slots = lax.broadcasted_iota(jnp.int32, entries.shape, 1)
    live = jnp.zeros(entries.shape, jnp.int32)
    for node in range(nodes):
        here = lax.broadcasted_iota(jnp.int32, entries.shape, 0) == node
        live = jnp.where(here, entry_of(counts[...], level - 1, node), live)
    entries = jnp.where(slots < live, entries ^ myself, empty)
    for node in range(nodes):
        total = None
        for pack, start, step in found:
            for slot in range(width):
                entry = entry_of(entries, node, (draw ^ step) * width + slot)
                at = start + offset + (node * width + slot) * depth
                term = transposed_dot(pack[at:at + depth, :], table[entry])
                total = term if total is None else total + term
        right_side = (noise[level, node, :, columns].astype(F32) - total).astype(BF16)
        solved[node] = transposed_dot(inv[node], right_side).astype(BF16)
    for step, send in enumerate(sends, 1):
        node = entry_of(picks[level], myself ^ step, myself)
        for at, ref in enumerate([*chunks, solved]):
            send[at] = ref[node]
    if done:
        here = target.at[level, :, :, pl.ds(chunk * wide, wide)]
        copies.append(pltpu.make_async_copy(solved, here, sems.at[len(done)]))
        copies[-1].start()
    for copy in copies:
        copy.wait()


def on_device(owners, draws, noise, inverse, coupling, picks, lists, counts):
    levels, nodes, rows, columns = noise.shape
    wide, half, chunks = columns // CHUNKS, owners // 2, range(CHUNKS)
    width = coupling.shape[2]
    part = shape(nodes, rows, wide)
    flat = lambda value: value.reshape(-1, rows)
    leaf = lambda value, step: hop(value, "leaf", owners, step)
    near = lambda values: [leaf(value, step) for step, value in enumerate(values, 1)]
    inv_here = pltpu.VMEM((nodes, rows, rows), BF16)
    dot_flops = 2 * rows * rows * wide

    raw = jnp.concatenate([
        flat(value) for level in range(1, levels) for value in (coupling[level - 1], inverse[level])
    ])
    values, steps = far_rows(flat(inverse[0]), "draw", draws)
    values, steps = near_rows(values, steps, "draw", draws)
    solved, *sends, raw = call(
        functools.partial(first_kernel, steps),
        [shape(nodes, rows, columns)] + [shape(1, rows, columns)] * (half - 1) + [shape(*raw.shape)],
        [inv_here],
        (picks, noise[0], *values, raw),
        flops=nodes * CHUNKS * dot_flops,
        aliases={2 + len(values): half},
    )
    far, got = leaf(solved, half), near(sends)
    values, steps = far_rows(raw, "draw", draws)
    sends = call(
        functools.partial(relay_kernel, half, 0, len(got), len(values)),
        [shape(1, rows, wide)] * (CHUNKS * (half - 1)) + [shape(*value.shape) for value in values],
        [],
        (picks, far, *got, *values),
        aliases={2 + len(got) + at: CHUNKS * (half - 1) + at for at in range(len(values))},
    )
    sends, values = take(sends, CHUNKS * (half - 1))
    packs, steps = near_rows(values, steps, "draw", draws)
    first, later = take(sends, half - 1)
    span = nodes * (width * rows + inverse.shape[2])
    outs = call(
        functools.partial(inverse_kernel, steps, levels - 1, span),
        [shape(*value.shape) for value in later] + [shape(nodes, rows, rows)] * (levels - 1),
        [],
        (*packs, *later),
        aliases={len(packs) + at: at for at in range(len(later))},
    )
    later, inverses = take(outs, len(later))
    sends = first + later
    pieces, done = [[]], [(solved, (0, 0))]
    for at in chunks:
        distant, sends = take(sends, half - 1)
        pieces[0].append([
            (solved, 0), *((ref, 0) for ref in got),
            (far, 0), *((ref, 0) for ref in near(distant)),
        ])

    for level in range(1, levels):
        last_level = level == levels - 1
        solved, sends = [], []
        for at in chunks:
            ends = at == CHUNKS - 1 and not last_level
            sides, mates = (half - 1, list(solved)) if ends else (0, [])
            final = last_level and at == CHUNKS - 1
            known = [entry for below in range(level) for entry in pieces[below][at]]
            stored = done if final else []
            scratch = [pltpu.VMEM((level * owners + 1, rows, wide), BF16)]
            if final:
                scratch += [
                    pltpu.VMEM((nodes, rows, wide), BF16),
                    pltpu.SemaphoreType.DMA((len(stored) + 1,)),
                ]
            here, *sent = call(
                functools.partial(
                    level_kernel, level, owners, steps, width, at,
                    [place for _, place in known], [place for _, place in stored], sides, len(mates),
                ),
                [shape(*noise.shape) if final else part] + [shape(CHUNKS, rows, wide)] * sides,
                scratch,
                (picks, lists, counts, noise, inverses[level - 1], *packs, *(ref for ref, _ in known), *(ref for ref, _ in stored), *mates),
                out_spec=ANY if final else VMEM,
                flops=nodes * (draws * width + 1) * dot_flops,
            )
            solved.append(here)
            done.append((here, (level, at * wide)))
            sends += sent
        if last_level:
            return here
        far = [leaf(value, half) for value in solved]
        got = near(sends)
        pieces.append([])
        for at in chunks:
            waits = got if at == CHUNKS - 1 else []
            sends = call(
                functools.partial(relay_kernel, half, level, len(waits), 0),
                [shape(1, rows, wide)] * (half - 1),
                [],
                (picks, far[at], *waits),
            )
            pieces[level].append([
                (solved[at], 0), *((ref, at) for ref in got),
                (far[at], 0), *((ref, 0) for ref in near(sends)),
            ])


def solution(mesh):
    placed = (
        P(None, "leaf", None, "draw"),
        P(None, "leaf", "draw", None),
        P(None, "leaf", "draw", None, None),
        P(),
        P(None, "leaf", None),
        P(None, "leaf"),
    )
    return jax.shard_map(
        functools.partial(on_device, mesh.shape["leaf"], mesh.shape["draw"]),
        mesh=mesh,
        in_specs=placed,
        out_specs=P(None, "leaf", None, "draw"),
        check_vma=False,
    )
```

```python
import functools

import jax
import jax.numpy as jnp
from jax import lax
from jax.experimental import pallas as pl
from jax.experimental.pallas import tpu as pltpu
from jax.sharding import PartitionSpec as P

CHUNKS = 2
VMEM = pl.BlockSpec(memory_space=pltpu.VMEM)
ANY = pl.BlockSpec(memory_space=pl.ANY)
BF16, F32 = jnp.bfloat16, jnp.float32


def hop(value, axis, size, step):
    return lax.ppermute(value, axis, [(at, at ^ step) for at in range(size)])


def far_rows(value, axis, size):
    values, held, step = [value], [[0]], size // 2
    while step > 1:
        if len(values) > 1:
            values, held = [jnp.concatenate(values)], [held[0] + held[1]]
        values.append(hop(values[0], axis, size, step))
        held.append([have ^ step for have in held[0]])
        step //= 2
    return values, held


def near_rows(values, held, axis, size):
    others = [hop(value, axis, size, 1) for value in values]
    return values + others, held + [[have ^ 1 for have in steps] for steps in held]


def transposed_dot(left, right):
    return lax.dot_general(left, right, (((0,), (0,)), ((), ())), preferred_element_type=F32)


def take(refs, count):
    return list(refs[:count]), list(refs[count:])


def shape(*dims):
    return jax.ShapeDtypeStruct(dims, BF16)


def entry_of(tile, row, column):
    rows = lax.broadcasted_iota(jnp.int32, tile.shape, 0)
    columns = lax.broadcasted_iota(jnp.int32, tile.shape, 1)
    return jnp.sum(jnp.where((rows == row) & (columns == column), tile, 0))


def call(kernel, outs, scratch, arrays, out_spec=VMEM, flops=0, aliases={}):
    size = sum(value.size * value.dtype.itemsize for value in (*arrays, *outs))
    return list(pl.pallas_call(
        kernel,
        out_shape=outs,
        in_specs=[VMEM] * len(arrays),
        out_specs=[out_spec] * len(outs),
        scratch_shapes=scratch,
        input_output_aliases=aliases,
        cost_estimate=pl.CostEstimate(flops=flops, bytes_accessed=size, transcendentals=0),
        compiler_params=pltpu.CompilerParams(vmem_limit_bytes=16 * 1024 * 1024),
    )(*arrays))


def row_blocks(refs, held, block):
    return [
        (ref, at * block, step)
        for ref, steps in zip(refs, held, strict=True) for at, step in enumerate(steps)
    ]


def fill_inverse(target, found, offset, draw):
    rows = target.shape[1] // len(found)
    for ref, at, step in found:
        start = pl.multiple_of((draw ^ step) * rows, rows)
        for node in range(target.shape[0]):
            first = at + offset + node * rows
            target[node, pl.ds(start, rows), :] = ref[first:first + rows, :]


def first_kernel(held, picks, noise, *refs):
    parts, (_, solved, *sends, _, inv) = take(refs, len(held))
    myself, draw = lax.axis_index("leaf"), lax.axis_index("draw")
    nodes = noise.shape[0]
    draws = sum(map(len, held))
    rows = inv.shape[1] // draws
    fill_inverse(inv, row_blocks(parts, held, nodes * rows), 0, draw)
    for node in range(nodes):
        solved[node] = transposed_dot(inv[node], noise[node]).astype(BF16)
    for step, send in enumerate(sends, 1):
        send[0] = solved[entry_of(picks[0], myself ^ step, myself)]


def relay_kernel(half, source, owned, waits, through, picks, far, *refs):
    own, refs = take(refs, owned)
    sends = refs[waits + through:len(refs) - through]
    myself = lax.axis_index("leaf")
    for at, send in enumerate(sends):
        chunk, step = divmod(at, half - 1)
        wide = send.shape[-1]
        node = entry_of(picks[source], myself ^ (step + 1), myself ^ half)
        send[0] = far[node, :, chunk * wide:(chunk + 1) * wide]
        if send.shape[0] > 1:
            node = entry_of(picks[source], myself ^ (step + 1), myself)
            for to, ref in enumerate(own, 1):
                send[to] = ref[node]


def inverse_kernel(held, levels, span, *refs):
    packs, refs = take(refs, len(held))
    draw = lax.axis_index("draw")
    draws = sum(map(len, held))
    found = row_blocks(packs, held, levels * span)
    for level, target in enumerate(refs[-levels:]):
        nodes, rows = target.shape[0], target.shape[1] // draws
        fill_inverse(target, found, (level + 1) * span - nodes * rows, draw)


def level_kernel(
    level, owners, held, width, chunk, places, stored, sides, mates,
    picks, lists, counts, noise, inv, *refs,
):
    half = owners // 2
    packs, refs = take(refs, len(held))
    known, refs = take(refs, level * owners)
    done, refs = take(refs, len(stored))
    chunks, refs = take(refs, mates)
    target, *refs = refs
    sends, (table, *refs) = take(refs, sides)
    myself, draw = lax.axis_index("leaf"), lax.axis_index("draw")
    levels, nodes = noise.shape[:2]
    wide = table.shape[-1]
    columns = slice(chunk * wide, (chunk + 1) * wide)
    depth = inv.shape[1]
    rows = depth // sum(map(len, held))
    span = nodes * (width * depth + rows)
    found = row_blocks(packs, held, (levels - 1) * span)
    offset = (level - 1) * span
    copies = []
    solved = target
    if done:
        solved, sems = refs
        for at, (ref, (into, first)) in enumerate(zip(done, stored, strict=True)):
            here = target.at[into, :, :, pl.ds(first, ref.shape[-1])]
            copies.append(pltpu.make_async_copy(ref, here, sems.at[at]))
            copies[-1].start()
    for at, (ref, place) in enumerate(zip(known, places, strict=True)):
        step = at % owners
        if step % half == 0:
            place = entry_of(picks[at // owners], myself, myself ^ step)
        table[at] = ref[place] if ref.shape[-1] == wide else ref[place, :, columns]
    empty = level * owners
    table[empty] = jnp.zeros_like(table[empty])
    entries = lists[level - 1]
    slots = lax.broadcasted_iota(jnp.int32, entries.shape, 1)
    live = jnp.zeros(entries.shape, jnp.int32)
    for node in range(nodes):
        here = lax.broadcasted_iota(jnp.int32, entries.shape, 0) == node
        live = jnp.where(here, entry_of(counts[...], level - 1, node), live)
    entries = jnp.where(slots < live, entries ^ myself, empty)
    for node in range(nodes):
        total = None
        for pack, start, step in found:
            for slot in range(width):
                entry = entry_of(entries, node, (draw ^ step) * width + slot)
                at = start + offset + (node * width + slot) * depth
                term = transposed_dot(pack[at:at + depth, :], table[entry])
                total = term if total is None else total + term
        right_side = (noise[level, node, :, columns].astype(F32) - total).astype(BF16)
        solved[node] = transposed_dot(inv[node], right_side).astype(BF16)
    for step, send in enumerate(sends, 1):
        node = entry_of(picks[level], myself ^ step, myself)
        for at, ref in enumerate([*chunks, solved]):
            send[at] = ref[node]
    if done:
        here = target.at[level, :, :, pl.ds(chunk * wide, wide)]
        copies.append(pltpu.make_async_copy(solved, here, sems.at[len(done)]))
        copies[-1].start()
    for copy in copies:
        copy.wait()


def on_device(owners, draws, noise, inverse, coupling, picks, lists, counts):
    levels, nodes, rows, columns = noise.shape
    wide, half, chunks = columns // CHUNKS, owners // 2, range(CHUNKS)
    width = coupling.shape[2]
    part = shape(nodes, rows, wide)
    flat = lambda value: value.reshape(-1, rows)
    leaf = lambda value, step: hop(value, "leaf", owners, step)
    near = lambda values: [leaf(value, step) for step, value in enumerate(values, 1)]
    inv_here = pltpu.VMEM((nodes, rows, rows), BF16)
    dot_flops = 2 * rows * rows * wide

    raw = jnp.concatenate([
        flat(value) for level in range(1, levels) for value in (coupling[level - 1], inverse[level])
    ])
    values, steps = far_rows(flat(inverse[0]), "draw", draws)
    values, steps = near_rows(values, steps, "draw", draws)
    solved, *sends, raw = call(
        functools.partial(first_kernel, steps),
        [shape(nodes, rows, columns)] + [shape(1, rows, columns)] * (half - 1) + [shape(*raw.shape)],
        [inv_here],
        (picks, noise[0], *values, raw),
        flops=nodes * CHUNKS * dot_flops,
        aliases={2 + len(values): half},
    )
    far, got = leaf(solved, half), near(sends)
    values, steps = far_rows(raw, "draw", draws)
    sends = call(
        functools.partial(relay_kernel, half, 0, 0, len(got), len(values)),
        [shape(1, rows, wide)] * (CHUNKS * (half - 1)) + [shape(*value.shape) for value in values],
        [],
        (picks, far, *got, *values),
        aliases={2 + len(got) + at: CHUNKS * (half - 1) + at for at in range(len(values))},
    )
    sends, values = take(sends, CHUNKS * (half - 1))
    packs, steps = near_rows(values, steps, "draw", draws)
    first, later = take(sends, half - 1)
    span = nodes * (width * rows + inverse.shape[2])
    outs = call(
        functools.partial(inverse_kernel, steps, levels - 1, span),
        [shape(*value.shape) for value in later] + [shape(nodes, rows, rows)] * (levels - 1),
        [],
        (*packs, *later),
        aliases={len(packs) + at: at for at in range(len(later))},
    )
    later, inverses = take(outs, len(later))
    sends = first + later
    pieces, done = [[]], [(solved, (0, 0))]
    for at in chunks:
        distant, sends = take(sends, half - 1)
        pieces[0].append([
            (solved, 0), *((ref, 0) for ref in got),
            (far, 0), *((ref, 0) for ref in near(distant)),
        ])

    for level in range(1, levels):
        last_level = level == levels - 1
        solved, sends = [], []
        for at in chunks:
            ends = at == CHUNKS - 1 and not last_level
            sides, mates = (half - 2, list(solved)) if ends else (0, [])
            final = last_level and at == CHUNKS - 1
            known = [entry for below in range(level) for entry in pieces[below][at]]
            stored = done if final else []
            scratch = [pltpu.VMEM((level * owners + 1, rows, wide), BF16)]
            if final:
                scratch += [
                    pltpu.VMEM((nodes, rows, wide), BF16),
                    pltpu.SemaphoreType.DMA((len(stored) + 1,)),
                ]
            here, *sent = call(
                functools.partial(
                    level_kernel, level, owners, steps, width, at,
                    [place for _, place in known], [place for _, place in stored], sides, len(mates),
                ),
                [shape(*noise.shape) if final else part] + [shape(CHUNKS, rows, wide)] * sides,
                scratch,
                (picks, lists, counts, noise, inverses[level - 1], *packs, *(ref for ref, _ in known), *(ref for ref, _ in stored), *mates),
                out_spec=ANY if final else VMEM,
                flops=nodes * (draws * width + 1) * dot_flops,
            )
            solved.append(here)
            done.append((here, (level, at * wide)))
            sends += sent
        if last_level:
            return here
        far = [leaf(value, half) for value in solved]
        got = near(sends)
        pieces.append([])
        for at in chunks:
            own, waits = (solved, []) if at == 0 else ([], got)
            sends = call(
                functools.partial(relay_kernel, half, level, len(own), len(waits), 0),
                [shape(1, rows, wide)] * (half - 2) + [shape(1 + len(own), rows, wide)],
                [],
                (picks, far[at], *own, *waits),
            )
            distant = near(sends)
            late = distant[-1] if at == 0 else late
            pieces[level].append([
                (solved[at], 0), *((ref, at) for ref in got), (late, 1 + at),
                (far[at], 0), *((ref, 0) for ref in distant),
            ])


def solution(mesh):
    placed = (
        P(None, "leaf", None, "draw"),
        P(None, "leaf", "draw", None),
        P(None, "leaf", "draw", None, None),
        P(),
        P(None, "leaf", None),
        P(None, "leaf"),
    )
    return jax.shard_map(
        functools.partial(on_device, mesh.shape["leaf"], mesh.shape["draw"]),
        mesh=mesh,
        in_specs=placed,
        out_specs=P(None, "leaf", None, "draw"),
        check_vma=False,
    )
```

```python
import functools

import jax
import jax.numpy as jnp
from jax import lax
from jax.experimental import pallas as pl
from jax.experimental.pallas import tpu as pltpu
from jax.sharding import PartitionSpec as P

CHUNKS = 2
VMEM = pl.BlockSpec(memory_space=pltpu.VMEM)
ANY = pl.BlockSpec(memory_space=pl.ANY)
BF16, F32 = jnp.bfloat16, jnp.float32


def hop(value, axis, size, step):
    return lax.ppermute(value, axis, [(at, at ^ step) for at in range(size)])


def far_rows(value, axis, size):
    values, held, step = [value], [[0]], size // 2
    while step > 1:
        if len(values) > 1:
            values, held = [jnp.concatenate(values)], [held[0] + held[1]]
        values.append(hop(values[0], axis, size, step))
        held.append([have ^ step for have in held[0]])
        step //= 2
    return values, held


def near_rows(values, held, axis, size):
    others = [hop(value, axis, size, 1) for value in values]
    return values + others, held + [[have ^ 1 for have in steps] for steps in held]


def transposed_dot(left, right):
    return lax.dot_general(left, right, (((0,), (0,)), ((), ())), preferred_element_type=F32)


def take(refs, count):
    return list(refs[:count]), list(refs[count:])


def shape(*dims):
    return jax.ShapeDtypeStruct(dims, BF16)


def entry_of(tile, row, column):
    rows = lax.broadcasted_iota(jnp.int32, tile.shape, 0)
    columns = lax.broadcasted_iota(jnp.int32, tile.shape, 1)
    return jnp.sum(jnp.where((rows == row) & (columns == column), tile, 0))


def call(kernel, outs, scratch, arrays, out_spec=VMEM, flops=0, aliases={}):
    size = sum(value.size * value.dtype.itemsize for value in (*arrays, *outs))
    return list(pl.pallas_call(
        kernel,
        out_shape=outs,
        in_specs=[VMEM] * len(arrays),
        out_specs=[out_spec] * len(outs),
        scratch_shapes=scratch,
        input_output_aliases=aliases,
        cost_estimate=pl.CostEstimate(flops=flops, bytes_accessed=size, transcendentals=0),
        compiler_params=pltpu.CompilerParams(vmem_limit_bytes=16 * 1024 * 1024),
    )(*arrays))


def row_blocks(refs, held, block):
    return [
        (ref, at * block, step)
        for ref, steps in zip(refs, held, strict=True) for at, step in enumerate(steps)
    ]


def fill_inverse(target, found, offset, draw):
    rows = target.shape[1] // len(found)
    for ref, at, step in found:
        start = pl.multiple_of((draw ^ step) * rows, rows)
        for node in range(target.shape[0]):
            first = at + offset + node * rows
            target[node, pl.ds(start, rows), :] = ref[first:first + rows, :]


def first_kernel(held, picks, noise, *refs):
    parts, (_, solved, *sends, _, inv) = take(refs, len(held))
    myself, draw = lax.axis_index("leaf"), lax.axis_index("draw")
    nodes = noise.shape[0]
    draws = sum(map(len, held))
    rows = inv.shape[1] // draws
    fill_inverse(inv, row_blocks(parts, held, nodes * rows), 0, draw)
    for node in range(nodes):
        solved[node] = transposed_dot(inv[node], noise[node]).astype(BF16)
    for step, send in enumerate(sends, 1):
        send[0] = solved[entry_of(picks[0], myself ^ step, myself)]


def relay_kernel(half, source, waits, through, picks, far, *refs):
    sends = refs[waits + through:len(refs) - through]
    myself = lax.axis_index("leaf")
    for at, send in enumerate(sends):
        chunk, step = divmod(at, half - 1)
        wide = send.shape[-1]
        node = entry_of(picks[source], myself ^ (step + 1), myself ^ half)
        send[0] = far[node, :, chunk * wide:(chunk + 1) * wide]


def inverse_kernel(held, levels, span, *refs):
    packs, refs = take(refs, len(held))
    draw = lax.axis_index("draw")
    draws = sum(map(len, held))
    found = row_blocks(packs, held, levels * span)
    for level, target in enumerate(refs[-levels:]):
        nodes, rows = target.shape[0], target.shape[1] // draws
        fill_inverse(target, found, (level + 1) * span - nodes * rows, draw)


def level_kernel(
    level, owners, held, width, chunk, places, stored, sides, mates,
    picks, lists, counts, noise, inv, *refs,
):
    half = owners // 2
    packs, refs = take(refs, len(held))
    known, refs = take(refs, level * owners)
    done, refs = take(refs, len(stored))
    chunks, refs = take(refs, mates)
    target, *refs = refs
    sends, (table, *refs) = take(refs, sides)
    myself, draw = lax.axis_index("leaf"), lax.axis_index("draw")
    levels, nodes = noise.shape[:2]
    wide = table.shape[-1]
    columns = slice(chunk * wide, (chunk + 1) * wide)
    depth = inv.shape[1]
    rows = depth // sum(map(len, held))
    span = nodes * (width * depth + rows)
    found = row_blocks(packs, held, (levels - 1) * span)
    offset = (level - 1) * span
    copies = []
    solved = target
    if done:
        solved, sems = refs
        for at, (ref, (into, first)) in enumerate(zip(done, stored, strict=True)):
            here = target.at[into, :, :, pl.ds(first, ref.shape[-1])]
            copies.append(pltpu.make_async_copy(ref, here, sems.at[at]))
            copies[-1].start()
    steps = [0, half, *range(1, half), *range(half + 1, owners)]
    for at, (ref, place) in enumerate(zip(known, places, strict=True)):
        source, step = at // owners, steps[at % owners]
        if step % half == 0:
            place = entry_of(picks[source], myself, myself ^ step)
        table[source * owners + step] = ref[place] if ref.shape[-1] == wide else ref[place, :, columns]
    empty = level * owners
    table[empty] = jnp.zeros_like(table[empty])
    entries = lists[level - 1]
    slots = lax.broadcasted_iota(jnp.int32, entries.shape, 1)
    live = jnp.zeros(entries.shape, jnp.int32)
    for node in range(nodes):
        here = lax.broadcasted_iota(jnp.int32, entries.shape, 0) == node
        live = jnp.where(here, entry_of(counts[...], level - 1, node), live)
    entries = jnp.where(slots < live, entries ^ myself, empty)
    for node in range(nodes):
        total = None
        for pack, start, step in found:
            for slot in range(width):
                entry = entry_of(entries, node, (draw ^ step) * width + slot)
                at = start + offset + (node * width + slot) * depth
                term = transposed_dot(pack[at:at + depth, :], table[entry])
                total = term if total is None else total + term
        right_side = (noise[level, node, :, columns].astype(F32) - total).astype(BF16)
        solved[node] = transposed_dot(inv[node], right_side).astype(BF16)
    for step, send in enumerate(sends, 1):
        node = entry_of(picks[level], myself ^ step, myself)
        for at, ref in enumerate([*chunks, solved]):
            send[at] = ref[node]
    if done:
        here = target.at[level, :, :, pl.ds(chunk * wide, wide)]
        copies.append(pltpu.make_async_copy(solved, here, sems.at[len(done)]))
        copies[-1].start()
    for copy in copies:
        copy.wait()


def on_device(owners, draws, noise, inverse, coupling, picks, lists, counts):
    levels, nodes, rows, columns = noise.shape
    wide, half, chunks = columns // CHUNKS, owners // 2, range(CHUNKS)
    width = coupling.shape[2]
    part = shape(nodes, rows, wide)
    flat = lambda value: value.reshape(-1, rows)
    leaf = lambda value, step: hop(value, "leaf", owners, step)
    near = lambda values: [leaf(value, step) for step, value in enumerate(values, 1)]
    inv_here = pltpu.VMEM((nodes, rows, rows), BF16)
    dot_flops = 2 * rows * rows * wide

    raw = jnp.concatenate([
        flat(value) for level in range(1, levels) for value in (coupling[level - 1], inverse[level])
    ])
    values, steps = far_rows(flat(inverse[0]), "draw", draws)
    values, steps = near_rows(values, steps, "draw", draws)
    solved, *sends, raw = call(
        functools.partial(first_kernel, steps),
        [shape(nodes, rows, columns)] + [shape(1, rows, columns)] * (half - 1) + [shape(*raw.shape)],
        [inv_here],
        (picks, noise[0], *values, raw),
        flops=nodes * CHUNKS * dot_flops,
        aliases={2 + len(values): half},
    )
    far, got = leaf(solved, half), near(sends)
    values, steps = far_rows(raw, "draw", draws)
    sends = call(
        functools.partial(relay_kernel, half, 0, len(got), len(values)),
        [shape(1, rows, wide)] * (CHUNKS * (half - 1)) + [shape(*value.shape) for value in values],
        [],
        (picks, far, *got, *values),
        aliases={2 + len(got) + at: CHUNKS * (half - 1) + at for at in range(len(values))},
    )
    sends, values = take(sends, CHUNKS * (half - 1))
    packs, steps = near_rows(values, steps, "draw", draws)
    first, later = take(sends, half - 1)
    span = nodes * (width * rows + inverse.shape[2])
    outs = call(
        functools.partial(inverse_kernel, steps, levels - 1, span),
        [shape(*value.shape) for value in later] + [shape(nodes, rows, rows)] * (levels - 1),
        [],
        (*packs, *later),
        aliases={len(packs) + at: at for at in range(len(later))},
    )
    later, inverses = take(outs, len(later))
    sends = first + later
    pieces, done = [[]], [(solved, (0, 0))]
    for at in chunks:
        distant, sends = take(sends, half - 1)
        pieces[0].append([
            (solved, 0), (far, 0), *((ref, 0) for ref in got),
            *((ref, 0) for ref in near(distant)),
        ])

    for level in range(1, levels):
        last_level = level == levels - 1
        solved, sends = [], []
        for at in chunks:
            ends = at == CHUNKS - 1 and not last_level
            sides, mates = (half - 1, list(solved)) if ends else (0, [])
            final = last_level and at == CHUNKS - 1
            known = [entry for below in range(level) for entry in pieces[below][at]]
            stored = done if final else []
            scratch = [pltpu.VMEM((level * owners + 1, rows, wide), BF16)]
            if final:
                scratch += [
                    pltpu.VMEM((nodes, rows, wide), BF16),
                    pltpu.SemaphoreType.DMA((len(stored) + 1,)),
                ]
            here, *sent = call(
                functools.partial(
                    level_kernel, level, owners, steps, width, at,
                    [place for _, place in known], [place for _, place in stored], sides, len(mates),
                ),
                [shape(*noise.shape) if final else part] + [shape(CHUNKS, rows, wide)] * sides,
                scratch,
                (picks, lists, counts, noise, inverses[level - 1], *packs, *(ref for ref, _ in known), *(ref for ref, _ in stored), *mates),
                out_spec=ANY if final else VMEM,
                flops=nodes * (draws * width + 1) * dot_flops,
            )
            solved.append(here)
            done.append((here, (level, at * wide)))
            sends += sent
        if last_level:
            return here
        far = [leaf(value, half) for value in solved]
        got = near(sends)
        pieces.append([])
        for at in chunks:
            waits = got if at == CHUNKS - 1 else []
            sends = call(
                functools.partial(relay_kernel, half, level, len(waits), 0),
                [shape(1, rows, wide)] * (half - 1),
                [],
                (picks, far[at], *waits),
            )
            pieces[level].append([
                (solved[at], 0), (far[at], 0), *((ref, at) for ref in got),
                *((ref, 0) for ref in near(sends)),
            ])


def solution(mesh):
    placed = (
        P(None, "leaf", None, "draw"),
        P(None, "leaf", "draw", None),
        P(None, "leaf", "draw", None, None),
        P(),
        P(None, "leaf", None),
        P(None, "leaf"),
    )
    return jax.shard_map(
        functools.partial(on_device, mesh.shape["leaf"], mesh.shape["draw"]),
        mesh=mesh,
        in_specs=placed,
        out_specs=P(None, "leaf", None, "draw"),
        check_vma=False,
    )
```

```python
import functools

import jax
import jax.numpy as jnp
from jax import lax
from jax.experimental import pallas as pl
from jax.experimental.pallas import tpu as pltpu
from jax.sharding import PartitionSpec as P

SHARES = (3, 1)
LANES = 128
VMEM = pl.BlockSpec(memory_space=pltpu.VMEM)
ANY = pl.BlockSpec(memory_space=pl.ANY)
BF16, F32 = jnp.bfloat16, jnp.float32


def hop(value, axis, size, step):
    return lax.ppermute(value, axis, [(at, at ^ step) for at in range(size)])


def far_rows(value, axis, size):
    values, held, step = [value], [[0]], size // 2
    while step > 1:
        if len(values) > 1:
            values, held = [jnp.concatenate(values)], [held[0] + held[1]]
        values.append(hop(values[0], axis, size, step))
        held.append([have ^ step for have in held[0]])
        step //= 2
    return values, held


def near_rows(values, held, axis, size):
    others = [hop(value, axis, size, 1) for value in values]
    return values + others, held + [[have ^ 1 for have in steps] for steps in held]


def column_chunks(columns):
    chunks, first, left = [], 0, sum(SHARES)
    for share in SHARES:
        wide = max((columns - first) * share // left // LANES, 1) * LANES
        chunks.append((first, wide))
        first, left = first + wide, left - share
    return chunks


def transposed_dot(left, right):
    return lax.dot_general(left, right, (((0,), (0,)), ((), ())), preferred_element_type=F32)


def take(refs, count):
    return list(refs[:count]), list(refs[count:])


def shape(*dims):
    return jax.ShapeDtypeStruct(dims, BF16)


def entry_of(tile, row, column):
    rows = lax.broadcasted_iota(jnp.int32, tile.shape, 0)
    columns = lax.broadcasted_iota(jnp.int32, tile.shape, 1)
    return jnp.sum(jnp.where((rows == row) & (columns == column), tile, 0))


def call(kernel, outs, scratch, arrays, out_spec=VMEM, flops=0, aliases={}):
    size = sum(value.size * value.dtype.itemsize for value in (*arrays, *outs))
    return list(pl.pallas_call(
        kernel,
        out_shape=outs,
        in_specs=[VMEM] * len(arrays),
        out_specs=[out_spec] * len(outs),
        scratch_shapes=scratch,
        input_output_aliases=aliases,
        cost_estimate=pl.CostEstimate(flops=flops, bytes_accessed=size, transcendentals=0),
        compiler_params=pltpu.CompilerParams(vmem_limit_bytes=16 * 1024 * 1024),
    )(*arrays))


def row_blocks(refs, held, block):
    return [
        (ref, at * block, step)
        for ref, steps in zip(refs, held, strict=True) for at, step in enumerate(steps)
    ]


def fill_inverse(target, found, offset, draw):
    rows = target.shape[1] // len(found)
    for ref, at, step in found:
        start = pl.multiple_of((draw ^ step) * rows, rows)
        for node in range(target.shape[0]):
            first = at + offset + node * rows
            target[node, pl.ds(start, rows), :] = ref[first:first + rows, :]


def first_kernel(held, picks, noise, *refs):
    parts, (_, solved, *sends, _, inv) = take(refs, len(held))
    myself, draw = lax.axis_index("leaf"), lax.axis_index("draw")
    nodes = noise.shape[0]
    draws = sum(map(len, held))
    rows = inv.shape[1] // draws
    fill_inverse(inv, row_blocks(parts, held, nodes * rows), 0, draw)
    for node in range(nodes):
        solved[node] = transposed_dot(inv[node], noise[node]).astype(BF16)
    for step, send in enumerate(sends, 1):
        send[0] = solved[entry_of(picks[0], myself ^ step, myself)]


def relay_kernel(half, source, starts, waits, through, picks, far, *refs):
    sends = refs[waits + through:len(refs) - through]
    myself = lax.axis_index("leaf")
    for at, send in enumerate(sends):
        chunk, step = divmod(at, half - 1)
        wide = send.shape[-1]
        node = entry_of(picks[source], myself ^ (step + 1), myself ^ half)
        send[0] = far[node, :, starts[chunk]:starts[chunk] + wide]


def inverse_kernel(held, levels, span, *refs):
    packs, refs = take(refs, len(held))
    draw = lax.axis_index("draw")
    draws = sum(map(len, held))
    found = row_blocks(packs, held, levels * span)
    for level, target in enumerate(refs[-levels:]):
        nodes, rows = target.shape[0], target.shape[1] // draws
        fill_inverse(target, found, (level + 1) * span - nodes * rows, draw)


def level_kernel(
    level, owners, held, width, start, places, stored, sides, mates,
    picks, lists, counts, noise, inv, *refs,
):
    half = owners // 2
    packs, refs = take(refs, len(held))
    known, refs = take(refs, level * owners)
    done, refs = take(refs, len(stored))
    chunks, refs = take(refs, mates)
    target, *refs = refs
    sends, (table, *refs) = take(refs, sides)
    myself, draw = lax.axis_index("leaf"), lax.axis_index("draw")
    levels, nodes = noise.shape[:2]
    wide = table.shape[-1]
    columns = slice(start, start + wide)
    depth = inv.shape[1]
    rows = depth // sum(map(len, held))
    span = nodes * (width * depth + rows)
    found = row_blocks(packs, held, (levels - 1) * span)
    offset = (level - 1) * span
    copies = []
    solved = target
    if done:
        solved, sems = refs
        for at, (ref, (into, first)) in enumerate(zip(done, stored, strict=True)):
            here = target.at[into, :, :, pl.ds(first, ref.shape[-1])]
            copies.append(pltpu.make_async_copy(ref, here, sems.at[at]))
            copies[-1].start()
    for at, (ref, place) in enumerate(zip(known, places, strict=True)):
        step = at % owners
        if step % half == 0:
            place = entry_of(picks[at // owners], myself, myself ^ step)
        table[at] = ref[place] if ref.shape[-1] == wide else ref[place, :, columns]
    empty = level * owners
    table[empty] = jnp.zeros_like(table[empty])
    entries = lists[level - 1]
    slots = lax.broadcasted_iota(jnp.int32, entries.shape, 1)
    live = jnp.zeros(entries.shape, jnp.int32)
    for node in range(nodes):
        here = lax.broadcasted_iota(jnp.int32, entries.shape, 0) == node
        live = jnp.where(here, entry_of(counts[...], level - 1, node), live)
    entries = jnp.where(slots < live, entries ^ myself, empty)
    for node in range(nodes):
        total = None
        for pack, base, step in found:
            for slot in range(width):
                entry = entry_of(entries, node, (draw ^ step) * width + slot)
                at = base + offset + (node * width + slot) * depth
                term = transposed_dot(pack[at:at + depth, :], table[entry])
                total = term if total is None else total + term
        right_side = (noise[level, node, :, columns].astype(F32) - total).astype(BF16)
        solved[node] = transposed_dot(inv[node], right_side).astype(BF16)
        if done:
            here = target.at[level, node, :, pl.ds(start, wide)]
            copies.append(pltpu.make_async_copy(solved.at[node], here, sems.at[len(copies)]))
            copies[-1].start()
    for step, send in enumerate(sends, 1):
        node = entry_of(picks[level], myself ^ step, myself)
        at = 0
        for ref in (*chunks, solved):
            send[0, :, at:at + ref.shape[-1]] = ref[node]
            at += ref.shape[-1]
    for copy in copies:
        copy.wait()


def on_device(owners, draws, noise, inverse, coupling, picks, lists, counts):
    levels, nodes, rows, columns = noise.shape
    half, chunks = owners // 2, column_chunks(columns)
    width = coupling.shape[2]
    flat = lambda value: value.reshape(-1, rows)
    leaf = lambda value, step: hop(value, "leaf", owners, step)
    near = lambda values: [leaf(value, step) for step, value in enumerate(values, 1)]
    inv_here = pltpu.VMEM((nodes, rows, rows), BF16)
    dot_flops = 2 * rows * rows * columns

    raw = jnp.concatenate([
        flat(value) for level in range(1, levels) for value in (coupling[level - 1], inverse[level])
    ])
    values, steps = far_rows(flat(inverse[0]), "draw", draws)
    values, steps = near_rows(values, steps, "draw", draws)
    solved, *sends, raw = call(
        functools.partial(first_kernel, steps),
        [shape(nodes, rows, columns)] + [shape(1, rows, columns)] * (half - 1) + [shape(*raw.shape)],
        [inv_here],
        (picks, noise[0], *values, raw),
        flops=nodes * dot_flops,
        aliases={2 + len(values): half},
    )
    far, got = leaf(solved, half), near(sends)
    values, steps = far_rows(raw, "draw", draws)
    sends = call(
        functools.partial(relay_kernel, half, 0, [at for at, _ in chunks], len(got), len(values)),
        [shape(1, rows, wide) for _, wide in chunks for _ in range(half - 1)]
        + [shape(*value.shape) for value in values],
        [],
        (picks, far, *got, *values),
        aliases={2 + len(got) + at: len(chunks) * (half - 1) + at for at in range(len(values))},
    )
    sends, values = take(sends, len(chunks) * (half - 1))
    packs, steps = near_rows(values, steps, "draw", draws)
    first, later = take(sends, half - 1)
    span = nodes * (width * rows + inverse.shape[2])
    outs = call(
        functools.partial(inverse_kernel, steps, levels - 1, span),
        [shape(*value.shape) for value in later] + [shape(nodes, rows, rows)] * (levels - 1),
        [],
        (*packs, *later),
        aliases={len(packs) + at: at for at in range(len(later))},
    )
    later, inverses = take(outs, len(later))
    sends = first + later
    pieces, done = [[]], [(solved, (0, 0))]
    for _ in chunks:
        distant, sends = take(sends, half - 1)
        pieces[0].append([
            (solved, 0), *((ref, 0) for ref in got),
            (far, 0), *((ref, 0) for ref in near(distant)),
        ])

    for level in range(1, levels):
        last_level = level == levels - 1
        solved, sends = [], []
        for at, (start, wide) in enumerate(chunks):
            ends = at == len(chunks) - 1 and not last_level
            sides, mates = (half - 1, list(solved)) if ends else (0, [])
            final = last_level and at == len(chunks) - 1
            known = [entry for below in range(level) for entry in pieces[below][at]]
            stored = done if final else []
            scratch = [pltpu.VMEM((level * owners + 1, rows, wide), BF16)]
            if final:
                scratch += [
                    pltpu.VMEM((nodes, rows, wide), BF16),
                    pltpu.SemaphoreType.DMA((len(stored) + nodes,)),
                ]
            here, *sent = call(
                functools.partial(
                    level_kernel, level, owners, steps, width, start,
                    [place for _, place in known], [place for _, place in stored], sides, len(mates),
                ),
                [shape(*noise.shape) if final else shape(nodes, rows, wide)]
                + [shape(1, rows, columns)] * sides,
                scratch,
                (picks, lists, counts, noise, inverses[level - 1], *packs, *(ref for ref, _ in known), *(ref for ref, _ in stored), *mates),
                out_spec=ANY if final else VMEM,
                flops=nodes * (draws * width + 1) * dot_flops * wide // columns,
            )
            solved.append(here)
            done.append((here, (level, start)))
            sends += sent
        if last_level:
            return here
        far = [leaf(value, half) for value in solved]
        got = near(sends)
        pieces.append([])
        for at, (_, wide) in enumerate(chunks):
            waits = got if at == len(chunks) - 1 else []
            sends = call(
                functools.partial(relay_kernel, half, level, [0], len(waits), 0),
                [shape(1, rows, wide)] * (half - 1),
                [],
                (picks, far[at], *waits),
            )
            pieces[level].append([
                (solved[at], 0), *((ref, 0) for ref in got),
                (far[at], 0), *((ref, 0) for ref in near(sends)),
            ])


def solution(mesh):
    placed = (
        P(None, "leaf", None, "draw"),
        P(None, "leaf", "draw", None),
        P(None, "leaf", "draw", None, None),
        P(),
        P(None, "leaf", None),
        P(None, "leaf"),
    )
    return jax.shard_map(
        functools.partial(on_device, mesh.shape["leaf"], mesh.shape["draw"]),
        mesh=mesh,
        in_specs=placed,
        out_specs=P(None, "leaf", None, "draw"),
        check_vma=False,
    )
```

```python
import functools

import jax
import jax.numpy as jnp
from jax import lax
from jax.experimental import pallas as pl
from jax.experimental.pallas import tpu as pltpu
from jax.sharding import PartitionSpec as P

SHARES = (3, 1)
LANES = 128
VMEM = pl.BlockSpec(memory_space=pltpu.VMEM)
ANY = pl.BlockSpec(memory_space=pl.ANY)
BF16, F32 = jnp.bfloat16, jnp.float32


def hop(value, axis, size, step):
    return lax.ppermute(value, axis, [(at, at ^ step) for at in range(size)])


def far_rows(value, axis, size):
    values, held, step = [value], [[0]], size // 2
    while step > 1:
        if len(values) > 1:
            values, held = [jnp.concatenate(values)], [held[0] + held[1]]
        values.append(hop(values[0], axis, size, step))
        held.append([have ^ step for have in held[0]])
        step //= 2
    return values, held


def near_rows(values, held, axis, size):
    others = [hop(value, axis, size, 1) for value in values]
    return values + others, held + [[have ^ 1 for have in steps] for steps in held]


def column_chunks(columns):
    chunks, first, left = [], 0, sum(SHARES)
    for share in SHARES:
        wide = max((columns - first) * share // left // LANES, 1) * LANES
        chunks.append((first, wide))
        first, left = first + wide, left - share
    return chunks


def transposed_dot(left, right):
    return lax.dot_general(left, right, (((0,), (0,)), ((), ())), preferred_element_type=F32)


def take(refs, count):
    return list(refs[:count]), list(refs[count:])


def shape(*dims):
    return jax.ShapeDtypeStruct(dims, BF16)


def entry_of(tile, row, column):
    rows = lax.broadcasted_iota(jnp.int32, tile.shape, 0)
    columns = lax.broadcasted_iota(jnp.int32, tile.shape, 1)
    return jnp.sum(jnp.where((rows == row) & (columns == column), tile, 0))


def call(kernel, outs, scratch, arrays, out_spec=VMEM, flops=0, aliases={}):
    size = sum(value.size * value.dtype.itemsize for value in (*arrays, *outs))
    return list(pl.pallas_call(
        kernel,
        out_shape=outs,
        in_specs=[VMEM] * len(arrays),
        out_specs=[out_spec] * len(outs),
        scratch_shapes=scratch,
        input_output_aliases=aliases,
        cost_estimate=pl.CostEstimate(flops=flops, bytes_accessed=size, transcendentals=0),
        compiler_params=pltpu.CompilerParams(vmem_limit_bytes=16 * 1024 * 1024),
    )(*arrays))


def row_blocks(refs, held, block):
    return [
        (ref, at * block, step)
        for ref, steps in zip(refs, held, strict=True) for at, step in enumerate(steps)
    ]


def fill_inverse(target, found, offset, draw):
    rows = target.shape[1] // len(found)
    for ref, at, step in found:
        start = pl.multiple_of((draw ^ step) * rows, rows)
        for node in range(target.shape[0]):
            first = at + offset + node * rows
            target[node, pl.ds(start, rows), :] = ref[first:first + rows, :]


def first_kernel(held, picks, noise, *refs):
    parts, (_, solved, *sends, _, inv) = take(refs, len(held))
    myself, draw = lax.axis_index("leaf"), lax.axis_index("draw")
    nodes = noise.shape[0]
    draws = sum(map(len, held))
    rows = inv.shape[1] // draws
    fill_inverse(inv, row_blocks(parts, held, nodes * rows), 0, draw)
    for node in range(nodes):
        solved[node] = transposed_dot(inv[node], noise[node]).astype(BF16)
    for step, send in enumerate(sends, 1):
        send[0] = solved[entry_of(picks[0], myself ^ step, myself)]


def relay_kernel(half, source, starts, waits, through, picks, far, *refs):
    sends = refs[waits + through:len(refs) - through]
    myself = lax.axis_index("leaf")
    for at, send in enumerate(sends):
        chunk, step = divmod(at, half - 1)
        wide = send.shape[-1]
        node = entry_of(picks[source], myself ^ (step + 1), myself ^ half)
        send[0] = far[node, :, starts[chunk]:starts[chunk] + wide]


def inverse_kernel(held, levels, span, *refs):
    packs, refs = take(refs, len(held))
    draw = lax.axis_index("draw")
    draws = sum(map(len, held))
    found = row_blocks(packs, held, levels * span)
    for level, target in enumerate(refs[-levels:]):
        nodes, rows = target.shape[0], target.shape[1] // draws
        fill_inverse(target, found, (level + 1) * span - nodes * rows, draw)


def level_kernel(
    level, owners, held, width, start, places, stored, sides, mates,
    picks, lists, counts, noise, inv, *refs,
):
    half = owners // 2
    packs, refs = take(refs, len(held))
    known, refs = take(refs, level * owners)
    done, refs = take(refs, len(stored))
    chunks, refs = take(refs, mates)
    target, *refs = refs
    sends, (table, *refs) = take(refs, sides)
    myself, draw = lax.axis_index("leaf"), lax.axis_index("draw")
    levels, nodes = noise.shape[:2]
    wide = table.shape[-1]
    columns = slice(start, start + wide)
    depth = inv.shape[1]
    rows = depth // sum(map(len, held))
    span = nodes * (width * depth + rows)
    found = row_blocks(packs, held, (levels - 1) * span)
    offset = (level - 1) * span
    copies = []
    solved = target
    if done:
        solved, sems = refs
        for at, (ref, (into, first)) in enumerate(zip(done, stored, strict=True)):
            here = target.at[into, :, :, pl.ds(first, ref.shape[-1])]
            copies.append(pltpu.make_async_copy(ref, here, sems.at[at]))
            copies[-1].start()
    for at, (ref, place) in enumerate(zip(known, places, strict=True)):
        step = at % owners
        if step % half == 0:
            place = entry_of(picks[at // owners], myself, myself ^ step)
        table[at] = ref[place] if ref.shape[-1] == wide else ref[place, :, columns]
    empty = level * owners
    table[empty] = jnp.zeros_like(table[empty])
    entries = lists[level - 1]
    slots = lax.broadcasted_iota(jnp.int32, entries.shape, 1)
    live = jnp.zeros(entries.shape, jnp.int32)
    for node in range(nodes):
        here = lax.broadcasted_iota(jnp.int32, entries.shape, 0) == node
        live = jnp.where(here, entry_of(counts[...], level - 1, node), live)
    entries = jnp.where(slots < live, entries ^ myself, empty)
    for node in range(nodes):
        total = None
        for pack, base, step in found:
            for slot in range(width):
                entry = entry_of(entries, node, (draw ^ step) * width + slot)
                at = base + offset + (node * width + slot) * depth
                term = transposed_dot(pack[at:at + depth, :], table[entry])
                total = term if total is None else total + term
        right_side = (noise[level, node, :, columns].astype(F32) - total).astype(BF16)
        solved[node] = transposed_dot(inv[node], right_side).astype(BF16)
        if done:
            here = target.at[level, node, :, pl.ds(start, wide)]
            copies.append(pltpu.make_async_copy(solved.at[node], here, sems.at[len(copies)]))
            copies[-1].start()
    for step, send in enumerate(sends, 1):
        node = entry_of(picks[level], myself ^ step, myself)
        at = 0
        for ref in (*chunks, solved):
            send[0, :, at:at + ref.shape[-1]] = ref[node]
            at += ref.shape[-1]
    for copy in copies:
        copy.wait()


def on_device(owners, draws, noise, inverse, coupling, picks, lists, counts):
    levels, nodes, rows, columns = noise.shape
    half, chunks = owners // 2, column_chunks(columns)
    width = coupling.shape[2]
    flat = lambda value: value.reshape(-1, rows)
    leaf = lambda value, step: hop(value, "leaf", owners, step)
    near = lambda values: [leaf(value, step) for step, value in enumerate(values, 1)]
    inv_here = pltpu.VMEM((nodes, rows, rows), BF16)
    dot_flops = 2 * rows * rows * columns

    raw = jnp.concatenate([
        flat(value) for level in range(1, levels) for value in (coupling[level - 1], inverse[level])
    ])
    values, steps = far_rows(flat(inverse[0]), "draw", draws)
    values, steps = near_rows(values, steps, "draw", draws)
    solved, *sends, raw = call(
        functools.partial(first_kernel, steps),
        [shape(nodes, rows, columns)] + [shape(1, rows, columns)] * (half - 1) + [shape(*raw.shape)],
        [inv_here],
        (picks, noise[0], *values, raw),
        flops=nodes * dot_flops,
        aliases={2 + len(values): half},
    )
    far, got = leaf(solved, half), near(sends)
    values, steps = far_rows(raw, "draw", draws)
    sends = call(
        functools.partial(relay_kernel, half, 0, [at for at, _ in chunks], len(got), len(values)),
        [shape(1, rows, wide) for _, wide in chunks for _ in range(half - 1)]
        + [shape(*value.shape) for value in values],
        [],
        (picks, far, *got, *values),
        aliases={2 + len(got) + at: len(chunks) * (half - 1) + at for at in range(len(values))},
    )
    sends, values = take(sends, len(chunks) * (half - 1))
    packs, steps = near_rows(values, steps, "draw", draws)
    first, later = take(sends, half - 1)
    span = nodes * (width * rows + inverse.shape[2])
    outs = call(
        functools.partial(inverse_kernel, steps, levels - 1, span),
        [shape(*value.shape) for value in later] + [shape(nodes, rows, rows)] * (levels - 1),
        [],
        (*packs, *later),
        aliases={len(packs) + at: at for at in range(len(later))},
    )
    later, inverses = take(outs, len(later))
    sends = first + later
    pieces, done = [[]], [(solved, (0, 0))]
    for _ in chunks:
        distant, sends = take(sends, half - 1)
        pieces[0].append([
            (solved, 0), *((ref, 0) for ref in got),
            (far, 0), *((ref, 0) for ref in near(distant)),
        ])

    for level in range(1, levels):
        last_level = level == levels - 1
        solved, sends = [], []
        for at, (start, wide) in enumerate(chunks):
            ends = at == len(chunks) - 1 and not last_level
            sides, mates = (half - 1, list(solved)) if ends else (0, [])
            if level == 1 and at == 0:
                mates = [ref for ref, _ in pieces[0][-1][half + 1:]]
            final = last_level and at == len(chunks) - 1
            known = [entry for below in range(level) for entry in pieces[below][at]]
            stored = done if final else []
            scratch = [pltpu.VMEM((level * owners + 1, rows, wide), BF16)]
            if final:
                scratch += [
                    pltpu.VMEM((nodes, rows, wide), BF16),
                    pltpu.SemaphoreType.DMA((len(stored) + nodes,)),
                ]
            here, *sent = call(
                functools.partial(
                    level_kernel, level, owners, steps, width, start,
                    [place for _, place in known], [place for _, place in stored], sides, len(mates),
                ),
                [shape(*noise.shape) if final else shape(nodes, rows, wide)]
                + [shape(1, rows, columns)] * sides,
                scratch,
                (picks, lists, counts, noise, inverses[level - 1], *packs, *(ref for ref, _ in known), *(ref for ref, _ in stored), *mates),
                out_spec=ANY if final else VMEM,
                flops=nodes * (draws * width + 1) * dot_flops * wide // columns,
            )
            solved.append(here)
            done.append((here, (level, start)))
            sends += sent
        if last_level:
            return here
        far = [leaf(value, half) for value in solved]
        got = near(sends)
        pieces.append([])
        for at, (_, wide) in enumerate(chunks):
            waits = got if at == len(chunks) - 1 else []
            sends = call(
                functools.partial(relay_kernel, half, level, [0], len(waits), 0),
                [shape(1, rows, wide)] * (half - 1),
                [],
                (picks, far[at], *waits),
            )
            pieces[level].append([
                (solved[at], 0), *((ref, 0) for ref in got),
                (far[at], 0), *((ref, 0) for ref in near(sends)),
            ])


def solution(mesh):
    placed = (
        P(None, "leaf", None, "draw"),
        P(None, "leaf", "draw", None),
        P(None, "leaf", "draw", None, None),
        P(),
        P(None, "leaf", None),
        P(None, "leaf"),
    )
    return jax.shard_map(
        functools.partial(on_device, mesh.shape["leaf"], mesh.shape["draw"]),
        mesh=mesh,
        in_specs=placed,
        out_specs=P(None, "leaf", None, "draw"),
        check_vma=False,
    )
```

```python
import functools

import jax
import jax.numpy as jnp
from jax import lax
from jax.experimental import pallas as pl
from jax.experimental.pallas import tpu as pltpu
from jax.sharding import PartitionSpec as P

CHUNKS = 2
VMEM = pl.BlockSpec(memory_space=pltpu.VMEM)
ANY = pl.BlockSpec(memory_space=pl.ANY)
BF16, F32 = jnp.bfloat16, jnp.float32


def hop(value, axis, size, step):
    return lax.ppermute(value, axis, [(at, at ^ step) for at in range(size)])


def far_rows(value, axis, size):
    values, held, step = [value], [[0]], size // 2
    while step > 1:
        if len(values) > 1:
            values, held = [jnp.concatenate(values)], [held[0] + held[1]]
        values.append(hop(values[0], axis, size, step))
        held.append([have ^ step for have in held[0]])
        step //= 2
    return values, held


def near_rows(values, held, axis, size):
    others = [hop(value, axis, size, 1) for value in values]
    return values + others, held + [[have ^ 1 for have in steps] for steps in held]


def transposed_dot(left, right):
    return lax.dot_general(left, right, (((0,), (0,)), ((), ())), preferred_element_type=F32)


def take(refs, count):
    return list(refs[:count]), list(refs[count:])


def shape(*dims):
    return jax.ShapeDtypeStruct(dims, BF16)


def entry_of(tile, row, column):
    rows = lax.broadcasted_iota(jnp.int32, tile.shape, 0)
    columns = lax.broadcasted_iota(jnp.int32, tile.shape, 1)
    return jnp.sum(jnp.where((rows == row) & (columns == column), tile, 0))


def call(kernel, outs, scratch, arrays, out_spec=VMEM, flops=0, aliases={}):
    size = sum(value.size * value.dtype.itemsize for value in (*arrays, *outs))
    return list(pl.pallas_call(
        kernel,
        out_shape=outs,
        in_specs=[VMEM] * len(arrays),
        out_specs=[out_spec] * len(outs),
        scratch_shapes=scratch,
        input_output_aliases=aliases,
        cost_estimate=pl.CostEstimate(flops=flops, bytes_accessed=size, transcendentals=0),
        compiler_params=pltpu.CompilerParams(vmem_limit_bytes=16 * 1024 * 1024),
    )(*arrays))


def row_blocks(refs, held, block):
    return [
        (ref, at * block, step)
        for ref, steps in zip(refs, held, strict=True) for at, step in enumerate(steps)
    ]


def fill_inverse(target, found, offset, draw):
    rows = target.shape[1] // len(found)
    for ref, at, step in found:
        start = pl.multiple_of((draw ^ step) * rows, rows)
        for node in range(target.shape[0]):
            first = at + offset + node * rows
            target[node, pl.ds(start, rows), :] = ref[first:first + rows, :]


def first_kernel(held, picks, noise, *refs):
    parts, (_, solved, *sends, _, inv) = take(refs, len(held))
    myself, draw = lax.axis_index("leaf"), lax.axis_index("draw")
    nodes = noise.shape[0]
    draws = sum(map(len, held))
    rows = inv.shape[1] // draws
    fill_inverse(inv, row_blocks(parts, held, nodes * rows), 0, draw)
    for node in range(nodes):
        solved[node] = transposed_dot(inv[node], noise[node]).astype(BF16)
    for step, send in enumerate(sends, 1):
        send[0] = solved[entry_of(picks[0], myself ^ step, myself)]


def relay_kernel(half, source, waits, through, picks, far, *refs):
    sends = refs[waits + through:len(refs) - through]
    myself = lax.axis_index("leaf")
    for at, send in enumerate(sends):
        chunk, step = divmod(at, half - 1)
        wide = send.shape[-1]
        node = entry_of(picks[source], myself ^ (step + 1), myself ^ half)
        send[0] = far[node, :, chunk * wide:(chunk + 1) * wide]


def inverse_kernel(held, levels, span, *refs):
    packs, refs = take(refs, len(held))
    draw = lax.axis_index("draw")
    draws = sum(map(len, held))
    found = row_blocks(packs, held, levels * span)
    for level, target in enumerate(refs[-levels:]):
        nodes, rows = target.shape[0], target.shape[1] // draws
        fill_inverse(target, found, (level + 1) * span - nodes * rows, draw)


def level_kernel(
    level, owners, held, width, chunk, places, stored, sides, mates,
    picks, lists, counts, noise, inv, *refs,
):
    half = owners // 2
    packs, refs = take(refs, len(held))
    known, refs = take(refs, level * owners)
    done, refs = take(refs, len(stored))
    chunks, refs = take(refs, mates)
    target, *refs = refs
    sends, (table, *refs) = take(refs, sides)
    myself, draw = lax.axis_index("leaf"), lax.axis_index("draw")
    levels, nodes = noise.shape[:2]
    wide = table.shape[-1]
    columns = slice(chunk * wide, (chunk + 1) * wide)
    depth = inv.shape[1]
    rows = depth // sum(map(len, held))
    span = nodes * (width * depth + rows)
    found = row_blocks(packs, held, (levels - 1) * span)
    offset = (level - 1) * span
    copies = []
    solved = target
    if done:
        solved, sems = refs
        for at, (ref, (into, first)) in enumerate(zip(done, stored, strict=True)):
            here = target.at[into, :, :, pl.ds(first, ref.shape[-1])]
            copies.append(pltpu.make_async_copy(ref, here, sems.at[at]))
            copies[-1].start()
    for at, (ref, place) in enumerate(zip(known, places, strict=True)):
        step = at % owners
        if step % half == 0:
            place = entry_of(picks[at // owners], myself, myself ^ step)
        table[at] = ref[place] if ref.shape[-1] == wide else ref[place, :, columns]
    empty = level * owners
    table[empty] = jnp.zeros_like(table[empty])
    entries = lists[level - 1]
    slots = lax.broadcasted_iota(jnp.int32, entries.shape, 1)
    live = jnp.zeros(entries.shape, jnp.int32)
    for node in range(nodes):
        here = lax.broadcasted_iota(jnp.int32, entries.shape, 0) == node
        live = jnp.where(here, entry_of(counts[...], level - 1, node), live)
    entries = jnp.where(slots < live, entries ^ myself, empty)
    for node in range(nodes):
        total = None
        for pack, start, step in found:
            for slot in range(width):
                entry = entry_of(entries, node, (draw ^ step) * width + slot)
                at = start + offset + (node * width + slot) * depth
                term = transposed_dot(pack[at:at + depth, :], table[entry])
                total = term if total is None else total + term
        right_side = (noise[level, node, :, columns].astype(F32) - total).astype(BF16)
        solved[node] = transposed_dot(inv[node], right_side).astype(BF16)
        if done:
            here = target.at[level, node, :, pl.ds(chunk * wide, wide)]
            copies.append(pltpu.make_async_copy(solved.at[node], here, sems.at[len(copies)]))
            copies[-1].start()
    for step, send in enumerate(sends, 1):
        node = entry_of(picks[level], myself ^ step, myself)
        for at, ref in enumerate([*chunks, solved]):
            send[at] = ref[node]
    for copy in copies:
        copy.wait()


def on_device(owners, draws, noise, inverse, coupling, picks, lists, counts):
    levels, nodes, rows, columns = noise.shape
    wide, half, chunks = columns // CHUNKS, owners // 2, range(CHUNKS)
    width = coupling.shape[2]
    part = shape(nodes, rows, wide)
    flat = lambda value: value.reshape(-1, rows)
    leaf = lambda value, step: hop(value, "leaf", owners, step)
    near = lambda values: [leaf(value, step) for step, value in enumerate(values, 1)]
    inv_here = pltpu.VMEM((nodes, rows, rows), BF16)
    dot_flops = 2 * rows * rows * wide

    raw = jnp.concatenate([
        flat(value) for level in range(1, levels) for value in (coupling[level - 1], inverse[level])
    ])
    values, steps = far_rows(flat(inverse[0]), "draw", draws)
    values, steps = near_rows(values, steps, "draw", draws)
    solved, *sends, raw = call(
        functools.partial(first_kernel, steps),
        [shape(nodes, rows, columns)] + [shape(1, rows, columns)] * (half - 1) + [shape(*raw.shape)],
        [inv_here],
        (picks, noise[0], *values, raw),
        flops=nodes * CHUNKS * dot_flops,
        aliases={2 + len(values): half},
    )
    far, got = leaf(solved, half), near(sends)
    values, steps = far_rows(raw, "draw", draws)
    sends = call(
        functools.partial(relay_kernel, half, 0, len(got), len(values)),
        [shape(1, rows, wide)] * (CHUNKS * (half - 1)) + [shape(*value.shape) for value in values],
        [],
        (picks, far, *got, *values),
        aliases={2 + len(got) + at: CHUNKS * (half - 1) + at for at in range(len(values))},
    )
    sends, values = take(sends, CHUNKS * (half - 1))
    packs, steps = near_rows(values, steps, "draw", draws)
    first, later = take(sends, half - 1)
    span = nodes * (width * rows + inverse.shape[2])
    outs = call(
        functools.partial(inverse_kernel, steps, levels - 1, span),
        [shape(*value.shape) for value in later] + [shape(nodes, rows, rows)] * (levels - 1),
        [],
        (*packs, *later),
        aliases={len(packs) + at: at for at in range(len(later))},
    )
    later, inverses = take(outs, len(later))
    sends = first + later
    pieces, done = [[]], [(solved, (0, 0))]
    for at in chunks:
        distant, sends = take(sends, half - 1)
        pieces[0].append([
            (solved, 0), *((ref, 0) for ref in got),
            (far, 0), *((ref, 0) for ref in near(distant)),
        ])

    for level in range(1, levels):
        last_level = level == levels - 1
        solved, sends = [], []
        for at in chunks:
            ends = at == CHUNKS - 1 and not last_level
            sides, mates = (half - 1, list(solved)) if ends else (0, [])
            final = last_level and at == CHUNKS - 1
            known = [entry for below in range(level) for entry in pieces[below][at]]
            stored = done if final else []
            scratch = [pltpu.VMEM((level * owners + 1, rows, wide), BF16)]
            if final:
                scratch += [
                    pltpu.VMEM((nodes, rows, wide), BF16),
                    pltpu.SemaphoreType.DMA((len(stored) + nodes,)),
                ]
            here, *sent = call(
                functools.partial(
                    level_kernel, level, owners, steps, width, at,
                    [place for _, place in known], [place for _, place in stored], sides, len(mates),
                ),
                [shape(*noise.shape) if final else part] + [shape(CHUNKS, rows, wide)] * sides,
                scratch,
                (picks, lists, counts, noise, inverses[level - 1], *packs, *(ref for ref, _ in known), *(ref for ref, _ in stored), *mates),
                out_spec=ANY if final else VMEM,
                flops=nodes * (draws * width + 1) * dot_flops,
            )
            solved.append(here)
            done.append((here, (level, at * wide)))
            sends += sent
        if last_level:
            return here
        far = [leaf(value, half) for value in solved]
        got = near(sends)
        pieces.append([])
        for at in chunks:
            waits = got[:half // 2] if at == CHUNKS - 1 else []
            sends = call(
                functools.partial(relay_kernel, half, level, len(waits), 0),
                [shape(1, rows, wide)] * (half - 1),
                [],
                (picks, far[at], *waits),
            )
            pieces[level].append([
                (solved[at], 0), *((ref, at) for ref in got),
                (far[at], 0), *((ref, 0) for ref in near(sends)),
            ])


def solution(mesh):
    placed = (
        P(None, "leaf", None, "draw"),
        P(None, "leaf", "draw", None),
        P(None, "leaf", "draw", None, None),
        P(),
        P(None, "leaf", None),
        P(None, "leaf"),
    )
    return jax.shard_map(
        functools.partial(on_device, mesh.shape["leaf"], mesh.shape["draw"]),
        mesh=mesh,
        in_specs=placed,
        out_specs=P(None, "leaf", None, "draw"),
        check_vma=False,
    )
```

```python
import functools

import jax
import jax.numpy as jnp
from jax import lax
from jax.experimental import pallas as pl
from jax.experimental.pallas import tpu as pltpu
from jax.sharding import PartitionSpec as P

CHUNKS = 2
VMEM = pl.BlockSpec(memory_space=pltpu.VMEM)
ANY = pl.BlockSpec(memory_space=pl.ANY)
BF16, F32 = jnp.bfloat16, jnp.float32


def hop(value, axis, size, step):
    return lax.ppermute(value, axis, [(at, at ^ step) for at in range(size)])


def far_rows(value, axis, size):
    values, held, step = [value], [[0]], size // 2
    while step > 1:
        if len(values) > 1:
            values, held = [jnp.concatenate(values)], [held[0] + held[1]]
        values.append(hop(values[0], axis, size, step))
        held.append([have ^ step for have in held[0]])
        step //= 2
    return values, held


def near_rows(values, held, axis, size):
    others = [hop(value, axis, size, 1) for value in values]
    return values + others, held + [[have ^ 1 for have in steps] for steps in held]


def transposed_dot(left, right):
    return lax.dot_general(left, right, (((0,), (0,)), ((), ())), preferred_element_type=F32)


def take(refs, count):
    return list(refs[:count]), list(refs[count:])


def shape(*dims):
    return jax.ShapeDtypeStruct(dims, BF16)


def entry_of(tile, row, column):
    rows = lax.broadcasted_iota(jnp.int32, tile.shape, 0)
    columns = lax.broadcasted_iota(jnp.int32, tile.shape, 1)
    return jnp.sum(jnp.where((rows == row) & (columns == column), tile, 0))


def call(kernel, outs, scratch, arrays, out_spec=VMEM, flops=0, aliases={}):
    size = sum(value.size * value.dtype.itemsize for value in (*arrays, *outs))
    return list(pl.pallas_call(
        kernel,
        out_shape=outs,
        in_specs=[VMEM] * len(arrays),
        out_specs=[out_spec] * len(outs),
        scratch_shapes=scratch,
        input_output_aliases=aliases,
        cost_estimate=pl.CostEstimate(flops=flops, bytes_accessed=size, transcendentals=0),
        compiler_params=pltpu.CompilerParams(vmem_limit_bytes=16 * 1024 * 1024),
    )(*arrays))


def row_blocks(refs, held, block):
    return [
        (ref, at * block, step)
        for ref, steps in zip(refs, held, strict=True) for at, step in enumerate(steps)
    ]


def fill_inverse(target, found, offset, draw):
    rows = target.shape[1] // len(found)
    for ref, at, step in found:
        start = pl.multiple_of((draw ^ step) * rows, rows)
        for node in range(target.shape[0]):
            first = at + offset + node * rows
            target[node, pl.ds(start, rows), :] = ref[first:first + rows, :]


def first_kernel(held, picks, noise, *refs):
    parts, (_, solved, *sends, _, inv) = take(refs, len(held))
    myself, draw = lax.axis_index("leaf"), lax.axis_index("draw")
    nodes = noise.shape[0]
    draws = sum(map(len, held))
    rows = inv.shape[1] // draws
    fill_inverse(inv, row_blocks(parts, held, nodes * rows), 0, draw)
    for node in range(nodes):
        solved[node] = transposed_dot(inv[node], noise[node]).astype(BF16)
    for step, send in enumerate(sends, 1):
        send[0] = solved[entry_of(picks[0], myself ^ step, myself)]


def relay_kernel(half, source, waits, through, picks, far, *refs):
    sends = refs[waits + through:len(refs) - through]
    myself = lax.axis_index("leaf")
    for at, send in enumerate(sends):
        chunk, step = divmod(at, half - 1)
        wide = send.shape[-1]
        node = entry_of(picks[source], myself ^ (step + 1), myself ^ half)
        send[0] = far[node, :, chunk * wide:(chunk + 1) * wide]


def inverse_kernel(held, levels, span, *refs):
    packs, refs = take(refs, len(held))
    draw = lax.axis_index("draw")
    draws = sum(map(len, held))
    found = row_blocks(packs, held, levels * span)
    for level, target in enumerate(refs[-levels:]):
        nodes, rows = target.shape[0], target.shape[1] // draws
        fill_inverse(target, found, (level + 1) * span - nodes * rows, draw)


def level_kernel(
    level, owners, held, width, chunk, places, stored, sides, mates,
    picks, lists, counts, noise, inv, *refs,
):
    half = owners // 2
    packs, refs = take(refs, len(held))
    known, refs = take(refs, level * owners)
    done, refs = take(refs, len(stored))
    chunks, refs = take(refs, mates)
    target, *refs = refs
    sends, (table, *refs) = take(refs, sides)
    myself, draw = lax.axis_index("leaf"), lax.axis_index("draw")
    levels, nodes = noise.shape[:2]
    wide = table.shape[-1]
    columns = slice(chunk * wide, (chunk + 1) * wide)
    depth = inv.shape[1]
    rows = depth // sum(map(len, held))
    span = nodes * (width * depth + rows)
    found = row_blocks(packs, held, (levels - 1) * span)
    offset = (level - 1) * span
    copies = []
    solved = target
    if done:
        solved, sems = refs
        for at, (ref, (into, first)) in enumerate(zip(done, stored, strict=True)):
            here = target.at[into, :, :, pl.ds(first, ref.shape[-1])]
            copies.append(pltpu.make_async_copy(ref, here, sems.at[at]))
            copies[-1].start()
    for at, (ref, place) in enumerate(zip(known, places, strict=True)):
        step = at % owners
        if step % half == 0:
            place = entry_of(picks[at // owners], myself, myself ^ step)
        table[at] = ref[place] if ref.shape[-1] == wide else ref[place, :, columns]
    empty = level * owners
    table[empty] = jnp.zeros_like(table[empty])
    entries = lists[level - 1]
    slots = lax.broadcasted_iota(jnp.int32, entries.shape, 1)
    live = jnp.zeros(entries.shape, jnp.int32)
    for node in range(nodes):
        here = lax.broadcasted_iota(jnp.int32, entries.shape, 0) == node
        live = jnp.where(here, entry_of(counts[...], level - 1, node), live)
    entries = jnp.where(slots < live, entries ^ myself, empty)
    for node in range(nodes):
        total = None
        for pack, start, step in found:
            for slot in range(width):
                entry = entry_of(entries, node, (draw ^ step) * width + slot)
                at = start + offset + (node * width + slot) * depth
                term = transposed_dot(pack[at:at + depth, :], table[entry])
                total = term if total is None else total + term
        right_side = (noise[level, node, :, columns].astype(F32) - total).astype(BF16)
        solved[node] = transposed_dot(inv[node], right_side).astype(BF16)
        if done:
            here = target.at[level, node, :, pl.ds(chunk * wide, wide)]
            copies.append(pltpu.make_async_copy(solved.at[node], here, sems.at[len(copies)]))
            copies[-1].start()
    for step, send in enumerate(sends, 1):
        node = entry_of(picks[level], myself ^ step, myself)
        for at, ref in enumerate([*chunks, solved]):
            send[at] = ref[node]
    for copy in copies:
        copy.wait()


def on_device(owners, draws, noise, inverse, coupling, picks, lists, counts):
    levels, nodes, rows, columns = noise.shape
    wide, half, chunks = columns // CHUNKS, owners // 2, range(CHUNKS)
    width = coupling.shape[2]
    part = shape(nodes, rows, wide)
    flat = lambda value: value.reshape(-1, rows)
    leaf = lambda value, step: hop(value, "leaf", owners, step)
    near = lambda values: [leaf(value, step) for step, value in enumerate(values, 1)]
    inv_here = pltpu.VMEM((nodes, rows, rows), BF16)
    dot_flops = 2 * rows * rows * wide

    raw = jnp.concatenate([
        flat(value) for level in range(1, levels) for value in (coupling[level - 1], inverse[level])
    ])
    values, steps = far_rows(flat(inverse[0]), "draw", draws)
    values, steps = near_rows(values, steps, "draw", draws)
    solved, *sends, raw = call(
        functools.partial(first_kernel, steps),
        [shape(nodes, rows, columns)] + [shape(1, rows, columns)] * (half - 1) + [shape(*raw.shape)],
        [inv_here],
        (picks, noise[0], *values, raw),
        flops=nodes * CHUNKS * dot_flops,
        aliases={2 + len(values): half},
    )
    far, got = leaf(solved, half), near(sends)
    values, steps = far_rows(raw, "draw", draws)
    sends = call(
        functools.partial(relay_kernel, half, 0, len(got), len(values)),
        [shape(1, rows, wide)] * (CHUNKS * (half - 1)) + [shape(*value.shape) for value in values],
        [],
        (picks, far, *got, *values),
        aliases={2 + len(got) + at: CHUNKS * (half - 1) + at for at in range(len(values))},
    )
    sends, values = take(sends, CHUNKS * (half - 1))
    packs, steps = near_rows(values, steps, "draw", draws)
    first, later = take(sends, half - 1)
    span = nodes * (width * rows + inverse.shape[2])
    outs = call(
        functools.partial(inverse_kernel, steps, levels - 1, span),
        [shape(*value.shape) for value in later] + [shape(nodes, rows, rows)] * (levels - 1),
        [],
        (*packs, *later),
        aliases={len(packs) + at: at for at in range(len(later))},
    )
    later, inverses = take(outs, len(later))
    sends = first + later
    pieces, done = [[]], [(solved, (0, 0))]
    for at in chunks:
        distant, sends = take(sends, half - 1)
        pieces[0].append([
            (solved, 0), *((ref, 0) for ref in got),
            (far, 0), *((ref, 0) for ref in near(distant)),
        ])

    for level in range(1, levels):
        last_level = level == levels - 1
        solved, sends = [], []
        for at in chunks:
            sides, mates = 0 if last_level else half - 1, []
            final = last_level and at == CHUNKS - 1
            known = [entry for below in range(level) for entry in pieces[below][at]]
            stored = done if final else []
            scratch = [pltpu.VMEM((level * owners + 1, rows, wide), BF16)]
            if final:
                scratch += [
                    pltpu.VMEM((nodes, rows, wide), BF16),
                    pltpu.SemaphoreType.DMA((len(stored) + nodes,)),
                ]
            here, *sent = call(
                functools.partial(
                    level_kernel, level, owners, steps, width, at,
                    [place for _, place in known], [place for _, place in stored], sides, len(mates),
                ),
                [shape(*noise.shape) if final else part] + [shape(1, rows, wide)] * sides,
                scratch,
                (picks, lists, counts, noise, inverses[level - 1], *packs, *(ref for ref, _ in known), *(ref for ref, _ in stored), *mates),
                out_spec=ANY if final else VMEM,
                flops=nodes * (draws * width + 1) * dot_flops,
            )
            solved.append(here)
            done.append((here, (level, at * wide)))
            sends.append(sent)
        if last_level:
            return here
        far = [leaf(value, half) for value in solved]
        got = [near(sent) for sent in sends]
        pieces.append([])
        for at in chunks:
            waits = got[0] if at == 0 else got[1][:half // 2]
            sends = call(
                functools.partial(relay_kernel, half, level, len(waits), 0),
                [shape(1, rows, wide)] * (half - 1),
                [],
                (picks, far[at], *waits),
            )
            pieces[level].append([
                (solved[at], 0), *((ref, 0) for ref in got[at]),
                (far[at], 0), *((ref, 0) for ref in near(sends)),
            ])


def solution(mesh):
    placed = (
        P(None, "leaf", None, "draw"),
        P(None, "leaf", "draw", None),
        P(None, "leaf", "draw", None, None),
        P(),
        P(None, "leaf", None),
        P(None, "leaf"),
    )
    return jax.shard_map(
        functools.partial(on_device, mesh.shape["leaf"], mesh.shape["draw"]),
        mesh=mesh,
        in_specs=placed,
        out_specs=P(None, "leaf", None, "draw"),
        check_vma=False,
    )
```

```python
import functools

import jax
import jax.numpy as jnp
from jax import lax
from jax.experimental import pallas as pl
from jax.experimental.pallas import tpu as pltpu
from jax.sharding import PartitionSpec as P

CHUNKS = 2
VMEM = pl.BlockSpec(memory_space=pltpu.VMEM)
ANY = pl.BlockSpec(memory_space=pl.ANY)
BF16, F32 = jnp.bfloat16, jnp.float32


def hop(value, axis, size, step):
    return lax.ppermute(value, axis, [(at, at ^ step) for at in range(size)])


def far_rows(value, axis, size):
    values, held, step = [value], [[0]], size // 2
    while step > 1:
        if len(values) > 1:
            values, held = [jnp.concatenate(values)], [held[0] + held[1]]
        values.append(hop(values[0], axis, size, step))
        held.append([have ^ step for have in held[0]])
        step //= 2
    return values, held


def near_rows(values, held, axis, size):
    others = [hop(value, axis, size, 1) for value in values]
    return values + others, held + [[have ^ 1 for have in steps] for steps in held]


def transposed_dot(left, right):
    return lax.dot_general(left, right, (((0,), (0,)), ((), ())), preferred_element_type=F32)


def take(refs, count):
    return list(refs[:count]), list(refs[count:])


def shape(*dims):
    return jax.ShapeDtypeStruct(dims, BF16)


def entry_of(tile, row, column):
    rows = lax.broadcasted_iota(jnp.int32, tile.shape, 0)
    columns = lax.broadcasted_iota(jnp.int32, tile.shape, 1)
    return jnp.sum(jnp.where((rows == row) & (columns == column), tile, 0))


def call(kernel, outs, scratch, arrays, out_spec=VMEM, flops=0, aliases={}):
    size = sum(value.size * value.dtype.itemsize for value in (*arrays, *outs))
    return list(pl.pallas_call(
        kernel,
        out_shape=outs,
        in_specs=[VMEM] * len(arrays),
        out_specs=[out_spec] * len(outs),
        scratch_shapes=scratch,
        input_output_aliases=aliases,
        cost_estimate=pl.CostEstimate(flops=flops, bytes_accessed=size, transcendentals=0),
        compiler_params=pltpu.CompilerParams(vmem_limit_bytes=16 * 1024 * 1024),
    )(*arrays))


def row_blocks(refs, held, block):
    return [
        (ref, at * block, step)
        for ref, steps in zip(refs, held, strict=True) for at, step in enumerate(steps)
    ]


def fill_inverse(target, found, offset, draw):
    rows = target.shape[1] // len(found)
    for ref, at, step in found:
        start = pl.multiple_of((draw ^ step) * rows, rows)
        for node in range(target.shape[0]):
            first = at + offset + node * rows
            target[node, pl.ds(start, rows), :] = ref[first:first + rows, :]


def first_kernel(held, picks, noise, *refs):
    parts, (_, solved, *sends, _, inv) = take(refs, len(held))
    myself, draw = lax.axis_index("leaf"), lax.axis_index("draw")
    nodes = noise.shape[0]
    draws = sum(map(len, held))
    rows = inv.shape[1] // draws
    fill_inverse(inv, row_blocks(parts, held, nodes * rows), 0, draw)
    for node in range(nodes):
        solved[node] = transposed_dot(inv[node], noise[node]).astype(BF16)
    side = len(sends) // CHUNKS
    for at, send in enumerate(sends):
        chunk, step = divmod(at, side)
        wide = send.shape[-1]
        node = entry_of(picks[0], myself ^ (step + 1), myself)
        send[0] = solved[node, :, chunk * wide:(chunk + 1) * wide]


def relay_kernel(half, source, waits, through, picks, far, *refs):
    sends = refs[waits + through:len(refs) - through]
    myself = lax.axis_index("leaf")
    for at, send in enumerate(sends):
        chunk, step = divmod(at, half - 1)
        wide = send.shape[-1]
        node = entry_of(picks[source], myself ^ (step + 1), myself ^ half)
        send[0] = far[node, :, chunk * wide:(chunk + 1) * wide]


def inverse_kernel(held, levels, span, *refs):
    packs, refs = take(refs, len(held))
    draw = lax.axis_index("draw")
    draws = sum(map(len, held))
    found = row_blocks(packs, held, levels * span)
    for level, target in enumerate(refs[-levels:]):
        nodes, rows = target.shape[0], target.shape[1] // draws
        fill_inverse(target, found, (level + 1) * span - nodes * rows, draw)


def level_kernel(
    level, owners, held, width, chunk, places, stored, sides, mates,
    picks, lists, counts, noise, inv, *refs,
):
    half = owners // 2
    packs, refs = take(refs, len(held))
    known, refs = take(refs, level * owners)
    done, refs = take(refs, len(stored))
    chunks, refs = take(refs, mates)
    target, *refs = refs
    sends, (table, *refs) = take(refs, sides)
    myself, draw = lax.axis_index("leaf"), lax.axis_index("draw")
    levels, nodes = noise.shape[:2]
    wide = table.shape[-1]
    columns = slice(chunk * wide, (chunk + 1) * wide)
    depth = inv.shape[1]
    rows = depth // sum(map(len, held))
    span = nodes * (width * depth + rows)
    found = row_blocks(packs, held, (levels - 1) * span)
    offset = (level - 1) * span
    copies = []
    solved = target
    if done:
        solved, sems = refs
        for at, (ref, (into, first)) in enumerate(zip(done, stored, strict=True)):
            here = target.at[into, :, :, pl.ds(first, ref.shape[-1])]
            copies.append(pltpu.make_async_copy(ref, here, sems.at[at]))
            copies[-1].start()
    for at, (ref, place) in enumerate(zip(known, places, strict=True)):
        step = at % owners
        if step % half == 0:
            place = entry_of(picks[at // owners], myself, myself ^ step)
        table[at] = ref[place] if ref.shape[-1] == wide else ref[place, :, columns]
    empty = level * owners
    table[empty] = jnp.zeros_like(table[empty])
    entries = lists[level - 1]
    slots = lax.broadcasted_iota(jnp.int32, entries.shape, 1)
    live = jnp.zeros(entries.shape, jnp.int32)
    for node in range(nodes):
        here = lax.broadcasted_iota(jnp.int32, entries.shape, 0) == node
        live = jnp.where(here, entry_of(counts[...], level - 1, node), live)
    entries = jnp.where(slots < live, entries ^ myself, empty)
    for node in range(nodes):
        total = None
        for pack, start, step in found:
            for slot in range(width):
                entry = entry_of(entries, node, (draw ^ step) * width + slot)
                at = start + offset + (node * width + slot) * depth
                term = transposed_dot(pack[at:at + depth, :], table[entry])
                total = term if total is None else total + term
        right_side = (noise[level, node, :, columns].astype(F32) - total).astype(BF16)
        solved[node] = transposed_dot(inv[node], right_side).astype(BF16)
        if done:
            here = target.at[level, node, :, pl.ds(chunk * wide, wide)]
            copies.append(pltpu.make_async_copy(solved.at[node], here, sems.at[len(copies)]))
            copies[-1].start()
    for step, send in enumerate(sends, 1):
        node = entry_of(picks[level], myself ^ step, myself)
        for at, ref in enumerate([*chunks, solved]):
            send[at] = ref[node]
    for copy in copies:
        copy.wait()


def on_device(owners, draws, noise, inverse, coupling, picks, lists, counts):
    levels, nodes, rows, columns = noise.shape
    wide, half, chunks = columns // CHUNKS, owners // 2, range(CHUNKS)
    width = coupling.shape[2]
    part = shape(nodes, rows, wide)
    flat = lambda value: value.reshape(-1, rows)
    leaf = lambda value, step: hop(value, "leaf", owners, step)
    near = lambda values: [leaf(value, step) for step, value in enumerate(values, 1)]
    inv_here = pltpu.VMEM((nodes, rows, rows), BF16)
    dot_flops = 2 * rows * rows * wide

    raw = jnp.concatenate([
        flat(value) for level in range(1, levels) for value in (coupling[level - 1], inverse[level])
    ])
    values, steps = far_rows(flat(inverse[0]), "draw", draws)
    values, steps = near_rows(values, steps, "draw", draws)
    solved, *sends, raw = call(
        functools.partial(first_kernel, steps),
        [shape(nodes, rows, columns)] + [shape(1, rows, wide)] * (CHUNKS * (half - 1))
        + [shape(*raw.shape)],
        [inv_here],
        (picks, noise[0], *values, raw),
        flops=nodes * CHUNKS * dot_flops,
        aliases={2 + len(values): 1 + CHUNKS * (half - 1)},
    )
    far, got = leaf(solved, half), []
    for _ in chunks:
        sent, sends = take(sends, half - 1)
        got.append(near(sent))
    waits = got[0] + got[1][:2]
    values, steps = far_rows(raw, "draw", draws)
    sends = call(
        functools.partial(relay_kernel, half, 0, len(waits), len(values)),
        [shape(1, rows, wide)] * (CHUNKS * (half - 1)) + [shape(*value.shape) for value in values],
        [],
        (picks, far, *waits, *values),
        aliases={2 + len(waits) + at: CHUNKS * (half - 1) + at for at in range(len(values))},
    )
    sends, values = take(sends, CHUNKS * (half - 1))
    packs, steps = near_rows(values, steps, "draw", draws)
    first, later = take(sends, half - 1)
    span = nodes * (width * rows + inverse.shape[2])
    outs = call(
        functools.partial(inverse_kernel, steps, levels - 1, span),
        [shape(*value.shape) for value in later] + [shape(nodes, rows, rows)] * (levels - 1),
        [],
        (*packs, *later),
        aliases={len(packs) + at: at for at in range(len(later))},
    )
    later, inverses = take(outs, len(later))
    sends = first + later
    pieces, done = [[]], [(solved, (0, 0))]
    for at in chunks:
        distant, sends = take(sends, half - 1)
        pieces[0].append([
            (solved, 0), *((ref, 0) for ref in got[at]),
            (far, 0), *((ref, 0) for ref in near(distant)),
        ])

    for level in range(1, levels):
        last_level = level == levels - 1
        solved, sends = [], []
        for at in chunks:
            sides, mates = 0 if last_level else half - 1, []
            final = last_level and at == CHUNKS - 1
            known = [entry for below in range(level) for entry in pieces[below][at]]
            stored = done if final else []
            scratch = [pltpu.VMEM((level * owners + 1, rows, wide), BF16)]
            if final:
                scratch += [
                    pltpu.VMEM((nodes, rows, wide), BF16),
                    pltpu.SemaphoreType.DMA((len(stored) + nodes,)),
                ]
            here, *sent = call(
                functools.partial(
                    level_kernel, level, owners, steps, width, at,
                    [place for _, place in known], [place for _, place in stored], sides, len(mates),
                ),
                [shape(*noise.shape) if final else part] + [shape(1, rows, wide)] * sides,
                scratch,
                (picks, lists, counts, noise, inverses[level - 1], *packs, *(ref for ref, _ in known), *(ref for ref, _ in stored), *mates),
                out_spec=ANY if final else VMEM,
                flops=nodes * (draws * width + 1) * dot_flops,
            )
            solved.append(here)
            done.append((here, (level, at * wide)))
            sends.append(sent)
        if last_level:
            return here
        far = [leaf(value, half) for value in solved]
        got = [near(sent) for sent in sends]
        pieces.append([])
        for at in chunks:
            waits = got[0] if at == 0 else got[1][:half // 2]
            sends = call(
                functools.partial(relay_kernel, half, level, len(waits), 0),
                [shape(1, rows, wide)] * (half - 1),
                [],
                (picks, far[at], *waits),
            )
            pieces[level].append([
                (solved[at], 0), *((ref, 0) for ref in got[at]),
                (far[at], 0), *((ref, 0) for ref in near(sends)),
            ])


def solution(mesh):
    placed = (
        P(None, "leaf", None, "draw"),
        P(None, "leaf", "draw", None),
        P(None, "leaf", "draw", None, None),
        P(),
        P(None, "leaf", None),
        P(None, "leaf"),
    )
    return jax.shard_map(
        functools.partial(on_device, mesh.shape["leaf"], mesh.shape["draw"]),
        mesh=mesh,
        in_specs=placed,
        out_specs=P(None, "leaf", None, "draw"),
        check_vma=False,
    )
```

```python
import functools

import jax
import jax.numpy as jnp
from jax import lax
from jax.experimental import pallas as pl
from jax.experimental.pallas import tpu as pltpu
from jax.sharding import PartitionSpec as P

CHUNKS = 2
VMEM = pl.BlockSpec(memory_space=pltpu.VMEM)
ANY = pl.BlockSpec(memory_space=pl.ANY)
BF16, F32 = jnp.bfloat16, jnp.float32


def hop(value, axis, size, step):
    return lax.ppermute(value, axis, [(at, at ^ step) for at in range(size)])


def far_rows(value, axis, size):
    values, held, step = [value], [[0]], size // 2
    while step > 1:
        if len(values) > 1:
            values, held = [jnp.concatenate(values)], [held[0] + held[1]]
        values.append(hop(values[0], axis, size, step))
        held.append([have ^ step for have in held[0]])
        step //= 2
    return values, held


def near_rows(values, held, axis, size):
    others = [hop(value, axis, size, 1) for value in values]
    return values + others, held + [[have ^ 1 for have in steps] for steps in held]


def transposed_dot(left, right):
    return lax.dot_general(left, right, (((0,), (0,)), ((), ())), preferred_element_type=F32)


def take(refs, count):
    return list(refs[:count]), list(refs[count:])


def shape(*dims):
    return jax.ShapeDtypeStruct(dims, BF16)


def entry_of(tile, row, column):
    rows = lax.broadcasted_iota(jnp.int32, tile.shape, 0)
    columns = lax.broadcasted_iota(jnp.int32, tile.shape, 1)
    return jnp.sum(jnp.where((rows == row) & (columns == column), tile, 0))


def call(kernel, outs, scratch, arrays, out_spec=VMEM, flops=0, aliases={}):
    size = sum(value.size * value.dtype.itemsize for value in (*arrays, *outs))
    return list(pl.pallas_call(
        kernel,
        out_shape=outs,
        in_specs=[VMEM] * len(arrays),
        out_specs=[out_spec] * len(outs),
        scratch_shapes=scratch,
        input_output_aliases=aliases,
        cost_estimate=pl.CostEstimate(flops=flops, bytes_accessed=size, transcendentals=0),
        compiler_params=pltpu.CompilerParams(vmem_limit_bytes=16 * 1024 * 1024),
    )(*arrays))


def row_blocks(refs, held, block):
    return [
        (ref, at * block, step)
        for ref, steps in zip(refs, held, strict=True) for at, step in enumerate(steps)
    ]


def fill_inverse(target, found, offset, draw):
    rows = target.shape[1] // len(found)
    for ref, at, step in found:
        start = pl.multiple_of((draw ^ step) * rows, rows)
        for node in range(target.shape[0]):
            first = at + offset + node * rows
            target[node, pl.ds(start, rows), :] = ref[first:first + rows, :]


def first_kernel(held, picks, noise, *refs):
    parts, (_, solved, *sends, _, inv) = take(refs, len(held))
    myself, draw = lax.axis_index("leaf"), lax.axis_index("draw")
    nodes = noise.shape[0]
    draws = sum(map(len, held))
    rows = inv.shape[1] // draws
    fill_inverse(inv, row_blocks(parts, held, nodes * rows), 0, draw)
    for node in range(nodes):
        solved[node] = transposed_dot(inv[node], noise[node]).astype(BF16)
    for at, send in enumerate(sends):
        send[0] = solved[entry_of(picks[0], myself ^ (len(sends) - at), myself)]


def relay_kernel(half, source, waits, through, picks, far, *refs):
    sends = refs[waits + through:len(refs) - through]
    myself = lax.axis_index("leaf")
    for at, send in enumerate(sends):
        chunk, step = divmod(at, half - 1)
        wide = send.shape[-1]
        node = entry_of(picks[source], myself ^ (half - 1 - step), myself ^ half)
        send[0] = far[node, :, chunk * wide:(chunk + 1) * wide]


def inverse_kernel(held, levels, span, *refs):
    packs, refs = take(refs, len(held))
    draw = lax.axis_index("draw")
    draws = sum(map(len, held))
    found = row_blocks(packs, held, levels * span)
    for level, target in enumerate(refs[-levels:]):
        nodes, rows = target.shape[0], target.shape[1] // draws
        fill_inverse(target, found, (level + 1) * span - nodes * rows, draw)


def level_kernel(
    level, owners, held, width, chunk, places, stored, sides, mates,
    picks, lists, counts, noise, inv, *refs,
):
    half = owners // 2
    packs, refs = take(refs, len(held))
    known, refs = take(refs, level * owners)
    done, refs = take(refs, len(stored))
    chunks, refs = take(refs, mates)
    target, *refs = refs
    sends, (table, *refs) = take(refs, sides)
    myself, draw = lax.axis_index("leaf"), lax.axis_index("draw")
    levels, nodes = noise.shape[:2]
    wide = table.shape[-1]
    columns = slice(chunk * wide, (chunk + 1) * wide)
    depth = inv.shape[1]
    rows = depth // sum(map(len, held))
    span = nodes * (width * depth + rows)
    found = row_blocks(packs, held, (levels - 1) * span)
    offset = (level - 1) * span
    copies = []
    solved = target
    if done:
        solved, sems = refs
        for at, (ref, (into, first)) in enumerate(zip(done, stored, strict=True)):
            here = target.at[into, :, :, pl.ds(first, ref.shape[-1])]
            copies.append(pltpu.make_async_copy(ref, here, sems.at[at]))
            copies[-1].start()
    order = [0, *range(half - 1, 0, -1), half, *range(owners - 1, half, -1)]
    for at, (ref, place) in enumerate(zip(known, places, strict=True)):
        source, step = at // owners, order[at % owners]
        if step % half == 0:
            place = entry_of(picks[source], myself, myself ^ step)
        table[source * owners + step] = ref[place] if ref.shape[-1] == wide else ref[place, :, columns]
    empty = level * owners
    table[empty] = jnp.zeros_like(table[empty])
    entries = lists[level - 1]
    slots = lax.broadcasted_iota(jnp.int32, entries.shape, 1)
    live = jnp.zeros(entries.shape, jnp.int32)
    for node in range(nodes):
        here = lax.broadcasted_iota(jnp.int32, entries.shape, 0) == node
        live = jnp.where(here, entry_of(counts[...], level - 1, node), live)
    entries = jnp.where(slots < live, entries ^ myself, empty)
    for node in range(nodes):
        total = None
        for pack, start, step in found:
            for slot in range(width):
                entry = entry_of(entries, node, (draw ^ step) * width + slot)
                at = start + offset + (node * width + slot) * depth
                term = transposed_dot(pack[at:at + depth, :], table[entry])
                total = term if total is None else total + term
        right_side = (noise[level, node, :, columns].astype(F32) - total).astype(BF16)
        solved[node] = transposed_dot(inv[node], right_side).astype(BF16)
        if done:
            here = target.at[level, node, :, pl.ds(chunk * wide, wide)]
            copies.append(pltpu.make_async_copy(solved.at[node], here, sems.at[len(copies)]))
            copies[-1].start()
    for step, send in enumerate(sends):
        node = entry_of(picks[level], myself ^ (len(sends) - step), myself)
        for at, ref in enumerate([*chunks, solved]):
            send[at] = ref[node]
    for copy in copies:
        copy.wait()


def on_device(owners, draws, noise, inverse, coupling, picks, lists, counts):
    levels, nodes, rows, columns = noise.shape
    wide, half, chunks = columns // CHUNKS, owners // 2, range(CHUNKS)
    width = coupling.shape[2]
    part = shape(nodes, rows, wide)
    flat = lambda value: value.reshape(-1, rows)
    leaf = lambda value, step: hop(value, "leaf", owners, step)
    near = lambda values: [leaf(value, len(values) - at) for at, value in enumerate(values)]
    inv_here = pltpu.VMEM((nodes, rows, rows), BF16)
    dot_flops = 2 * rows * rows * wide

    raw = jnp.concatenate([
        flat(value) for level in range(1, levels) for value in (coupling[level - 1], inverse[level])
    ])
    values, steps = far_rows(flat(inverse[0]), "draw", draws)
    values, steps = near_rows(values, steps, "draw", draws)
    solved, *sends, raw = call(
        functools.partial(first_kernel, steps),
        [shape(nodes, rows, columns)] + [shape(1, rows, columns)] * (half - 1) + [shape(*raw.shape)],
        [inv_here],
        (picks, noise[0], *values, raw),
        flops=nodes * CHUNKS * dot_flops,
        aliases={2 + len(values): half},
    )
    far, got = leaf(solved, half), near(sends)
    values, steps = far_rows(raw, "draw", draws)
    sends = call(
        functools.partial(relay_kernel, half, 0, len(got), len(values)),
        [shape(1, rows, wide)] * (CHUNKS * (half - 1)) + [shape(*value.shape) for value in values],
        [],
        (picks, far, *got, *values),
        aliases={2 + len(got) + at: CHUNKS * (half - 1) + at for at in range(len(values))},
    )
    sends, values = take(sends, CHUNKS * (half - 1))
    packs, steps = near_rows(values, steps, "draw", draws)
    first, later = take(sends, half - 1)
    span = nodes * (width * rows + inverse.shape[2])
    outs = call(
        functools.partial(inverse_kernel, steps, levels - 1, span),
        [shape(*value.shape) for value in later] + [shape(nodes, rows, rows)] * (levels - 1),
        [],
        (*packs, *later),
        aliases={len(packs) + at: at for at in range(len(later))},
    )
    later, inverses = take(outs, len(later))
    sends = first + later
    pieces, done = [[]], [(solved, (0, 0))]
    for at in chunks:
        distant, sends = take(sends, half - 1)
        pieces[0].append([
            (solved, 0), *((ref, 0) for ref in got),
            (far, 0), *((ref, 0) for ref in near(distant)),
        ])

    for level in range(1, levels):
        last_level = level == levels - 1
        solved, sends = [], []
        for at in chunks:
            sides, mates = 0 if last_level else half - 1, []
            final = last_level and at == CHUNKS - 1
            known = [entry for below in range(level) for entry in pieces[below][at]]
            stored = done if final else []
            scratch = [pltpu.VMEM((level * owners + 1, rows, wide), BF16)]
            if final:
                scratch += [
                    pltpu.VMEM((nodes, rows, wide), BF16),
                    pltpu.SemaphoreType.DMA((len(stored) + nodes,)),
                ]
            here, *sent = call(
                functools.partial(
                    level_kernel, level, owners, steps, width, at,
                    [place for _, place in known], [place for _, place in stored], sides, len(mates),
                ),
                [shape(*noise.shape) if final else part] + [shape(1, rows, wide)] * sides,
                scratch,
                (picks, lists, counts, noise, inverses[level - 1], *packs, *(ref for ref, _ in known), *(ref for ref, _ in stored), *mates),
                out_spec=ANY if final else VMEM,
                flops=nodes * (draws * width + 1) * dot_flops,
            )
            solved.append(here)
            done.append((here, (level, at * wide)))
            sends.append(sent)
        if last_level:
            return here
        far = [leaf(value, half) for value in solved]
        got = [near(sent) for sent in sends]
        pieces.append([])
        for at in chunks:
            waits = got[0] if at == 0 else got[1][1:]
            sends = call(
                functools.partial(relay_kernel, half, level, len(waits), 0),
                [shape(1, rows, wide)] * (half - 1),
                [],
                (picks, far[at], *waits),
            )
            pieces[level].append([
                (solved[at], 0), *((ref, 0) for ref in got[at]),
                (far[at], 0), *((ref, 0) for ref in near(sends)),
            ])


def solution(mesh):
    placed = (
        P(None, "leaf", None, "draw"),
        P(None, "leaf", "draw", None),
        P(None, "leaf", "draw", None, None),
        P(),
        P(None, "leaf", None),
        P(None, "leaf"),
    )
    return jax.shard_map(
        functools.partial(on_device, mesh.shape["leaf"], mesh.shape["draw"]),
        mesh=mesh,
        in_specs=placed,
        out_specs=P(None, "leaf", None, "draw"),
        check_vma=False,
    )
```
